32 devices in a mesh: sec: 4 (over y, x), tile: 8 (over z, core).
Axes of the slice: x: 2, y: 2, z: 4, core: 2. Of those that a mesh axis runs over, the one named last changes fastest.
Arguments:
- patches: bfloat16 [4, 32, 512, 512], P('sec', 'tile'), may hold values from -6 to 6
- zoom: float32 [4, 2, 32], P('sec'), may hold values from 0.75 to 0.9
- frac: float32 [4, 2, 32], P('sec'), may hold values from 0 to 1
- offset: int32 [4, 2, 32], P('sec'), may hold values from 0 to 15
- owner: int32 [4, 32, 16, 1], P('sec'), may hold values from 0 to 7; in each aligned block of 64 rows (0 to 63, 64 to 127, ..., all dimensions but the last counted through in order) at most 16 rows name the same one
- top_grid: bfloat16 [8, 256, 256], P('tile'), may hold values from -3 to 3
Outputs:
- grid_image: bfloat16 [4, 8, 256, 256], P('sec', 'tile')
- corrections: float32 [6, 4, 32], P(None, 'sec', 'tile')
The draws below stay inside these ranges and needn't reach their ends.
Inputs may be any that keep to these rules, and one draw needn't show every extreme that they name: `owner`: in each section, the bands of one device's 4 tiles (aligned blocks of 64 rows) name no grid tile more than 16 times; in some blocks one grid tile is named exactly 16 times.
All inputs are finite; a program needn't handle non-finite values.
Results may differ from the reference program's by a relative error of at most 0.0018.
The reference program's roundings to bfloat16 on the way count: a program that leaves them out, or rounds other values in their place, can miss the bound.
Values may be sent and summed in bfloat16 or wider, within the bound.
No kernel may reach another device: no remote copies, remote signals or barrier semaphores. Data moves between devices by JAX's collectives and lax.ppermute only.
A program may use at most 64 MiB of HBM per device.

```python
import math
import jax
import jax.numpy as jnp
import numpy as np
from jax import lax

P_SIZE = 512
Q = 256
BAND = 16
NB = 16
TILE_DEV = 4
ITERS = 2
CAP = 16
SECTIONS = 4
TILES = 32
GRID = 8
N_TILE = 8


def plant(values, own_key, smallest, top_value):
    spot = [jax.random.randint(jax.random.fold_in(own_key, axis), (), 0, length) for axis, length in enumerate(values.shape)]
    main_axis = values.shape.index(max(values.shape))
    beside = spot[:main_axis] + [(spot[main_axis] + 1) % values.shape[main_axis]] + spot[main_axis + 1:]
    return values.at[tuple(spot)].set(smallest).at[tuple(beside)].set(top_value)


def level_of(own_key, shape, shards, low, top_value):
    def one(position, blocks):
        steps = jax.random.uniform(jax.random.fold_in(jax.random.fold_in(own_key, 6), position), (blocks,), jnp.float32, low / len(shards), top_value / len(shards))
        return jnp.repeat(jnp.exp(steps), shape[position] // blocks).reshape((-1,) + (1,) * (len(shape) - position - 1))

    loudness = one(*shards[0])
    for cut in shards[1:]:
        loudness = loudness * one(*cut)
    return loudness


def assign_block(key, own, number, rows, count, top, limit, slope):
    sequence = jax.random.permutation(key, count)
    crowded, usual = shares(count, rows * top, limit, slope, True), shares(count, rows * top, limit, slope, False)
    places = jnp.arange(count)

    def named(tallies, offset_by):
        used = int((tallies > 0).sum())
        fixed = max(1, used // 4)
        moved = fixed + (places - fixed + offset_by * (used - fixed)) % max(1, count - fixed)
        return jnp.zeros((count,), jnp.int32).at[sequence[jnp.where(places < fixed, places, moved)]].set(jnp.asarray(tallies, jnp.int32))

    tallies = jnp.where(number % 4 == 0, named(crowded, number // 4), named(usual, number - number // 4 - 1))
    mixed = jax.random.permutation(jax.random.fold_in(own, 3), count)
    source_of, taker = mixed[0:count // 2 * 2:2], mixed[1:count // 2 * 2:2]
    slack = jnp.minimum(tallies[source_of] - 1, limit - tallies[taker]) // 2
    slack = jnp.where((source_of == sequence[0]) | (taker == sequence[0]) | (tallies[taker] == 0), 0, jnp.maximum(slack, 0))
    moved = jax.random.randint(jax.random.fold_in(own, 4), (count // 2,), 0, 1 << 20) % (slack + 1)
    tallies = tallies.at[source_of].add(-moved).at[taker].add(moved)
    labels = jnp.searchsorted(jnp.cumsum(tallies), jnp.arange(rows * top), side="right").astype(jnp.int32)
    grid = labels.reshape(top, rows).T
    grid = grid[jax.random.permutation(jax.random.fold_in(own, 1), rows)]
    offset_by = jax.random.randint(jax.random.fold_in(own, 2), (rows, 1), 0, top)
    return jnp.take_along_axis(grid, (jnp.arange(top)[None, :] + offset_by) % top, axis=1)


def shares(amount, total, reach, slope, full):
    portions = [(1 << 20) // math.isqrt(standing ** slope) + 1 for standing in range(1, amount + 1)]
    largest = reach if full else min(reach, max(-(-total // amount), total * portions[0] // sum(portions)))
    least = 1 if total - largest >= amount - 1 else 0
    given, rest = [largest] + [least] * (amount - 1), total - largest - least * (amount - 1)
    while rest > 0:
        free = [i for i in range(1, amount) if given[i] < largest] or [i for i in range(1, amount) if given[i] < reach]
        whole, remaining = sum([portions[i] for i in free]), rest
        for i in free:
            extra = min(reach - given[i], max(1, remaining * portions[i] // whole), rest)
            given[i] = given[i] + extra
            rest = rest - extra
    return np.array(given)


def normal_values(key, extent, deviation, most, split=(), kind=jnp.bfloat16):
    values = jax.random.normal(key, extent, jnp.float32) * deviation
    if len(split) > 0:
        values = level_of(key, extent, split, -0.22, 0.18) * values
    return jnp.clip(values, min=-most, max=most).astype(kind)


def setup_inputs(seed: int = 0) -> dict:
    streams_of = jax.random.split(jax.random.key(seed), 7)
    patches = normal_values(streams_of[0], (SECTIONS, TILES, P_SIZE, P_SIZE), 1.0, 6.0, ((0, 4), (1, 8)))
    zoom = jnp.clip(0.75 + 0.14999998 * jax.random.uniform(streams_of[1], (SECTIONS, 2, TILES), jnp.float32) ** level_of(streams_of[1], (SECTIONS, 2, TILES), ((0, 4),), -0.2, 0.2), 0.75, 0.9)
    frac = jnp.clip(1.0 * jax.random.uniform(streams_of[2], (SECTIONS, 2, TILES), jnp.float32) ** level_of(streams_of[2], (SECTIONS, 2, TILES), ((0, 4),), -0.2, 0.2), 0.0, 1.0)
    offset = plant(jax.random.randint(streams_of[3], (SECTIONS, 2, TILES), 0, Q // 16), jax.random.fold_in(streams_of[3], 1), 0, (Q // 16) - 1).astype(jnp.int32)
    owner_keys = jax.random.split(jax.random.fold_in(streams_of[4], 1), SECTIONS * TILES * NB // (TILE_DEV * NB))
    owner_turns = jax.random.permutation(jax.random.fold_in(streams_of[4], 3), SECTIONS * TILES * NB // (TILE_DEV * NB))
    owner = jax.vmap(lambda own, number: assign_block(jax.random.fold_in(streams_of[4], 2), own, number, TILE_DEV * NB, N_TILE, 1, CAP, 2))(owner_keys, owner_turns).reshape((SECTIONS, TILES, NB, 1))
    top_grid = normal_values(streams_of[5], (GRID, Q, Q), 0.4, 3.0, ((0, 8),))
    return {"patches": patches, "zoom": zoom, "frac": frac, "offset": offset, "owner": owner, "top_grid": top_grid}


COUPLING = 0.25


def hat_weight(distance):
    return jnp.maximum(0.0, 1.0 - jnp.abs(distance))


def sample_points(zoom, frac, offset, frame, source):
    scale = zoom * (frame / source)
    spots = jnp.arange(frame, dtype=jnp.float32)
    return (spots - offset.astype(jnp.float32)[..., None] - frac[..., None]) / scale[..., None]


def coverage(points, source):
    return jnp.clip(jnp.minimum(points + 1.0, source - points), 0.0, 1.0)


def moments(intensity, target, row_cover, col_cover, row_pos, frame):
    middle = (frame - 1) / 2.0
    level = intensity.astype(jnp.float32)
    error = target.astype(jnp.float32) - level
    weight = row_cover[:, :, None] * col_cover[:, None, :] / (frame * frame)
    columns = (jnp.arange(frame, dtype=jnp.float32) - middle) / (frame / 2.0)
    row_coord = (row_pos - middle) / (frame / 2.0)
    x_grid = jnp.broadcast_to(columns[None, None, :], level.shape)
    y_grid = jnp.broadcast_to(row_coord[:, :, None], level.shape)
    features = jnp.stack([jnp.ones_like(level), x_grid, y_grid, level, level * x_grid, level * y_grid], axis=1)
    weighted = features * weight[:, None]
    normal = jnp.einsum("bfrq,bgrq->bfg", weighted, features, precision=lax.Precision.HIGHEST)
    gradient = jnp.einsum("bfrq,brq->bf", weighted, error, precision=lax.Precision.HIGHEST)
    return normal, gradient


def blocked_moments(intensity, target, row_cover, col_cover, row_pos, frame):
    count = intensity.shape[0]
    block_size = math.gcd(count, 64)

    def block_moments(block_args):
        return moments(block_args[0], block_args[1], block_args[2], block_args[3], block_args[4], frame)

    shaped = tuple(member.reshape((count // block_size, block_size) + member.shape[1:]) for member in (intensity, target, row_cover, col_cover, row_pos))
    normal, gradient = lax.map(block_moments, shaped)
    return normal.reshape(count, 6, 6), gradient.reshape(count, 6)


def tap_pair(points, source):
    base = jnp.floor(points)
    lower = base.astype(jnp.int32)
    upper = lower + 1
    weight_lower = jnp.where((lower >= 0) & (lower < source), hat_weight(points - base), 0.0).astype(jnp.bfloat16)
    weight_upper = jnp.where((upper >= 0) & (upper < source), hat_weight(points - (base + 1.0)), 0.0).astype(jnp.bfloat16)
    return jnp.clip(lower, 0, source - 1), jnp.clip(upper, 0, source - 1), weight_lower, weight_upper


def render_tile(patch, row_points, col_points):
    row_lower, row_upper, row_wlow, row_wup = tap_pair(row_points, P_SIZE)
    halfway = (row_wlow.astype(jnp.float32)[:, None] * patch[row_lower].astype(jnp.float32)
               + row_wup.astype(jnp.float32)[:, None] * patch[row_upper].astype(jnp.float32)).astype(jnp.bfloat16)
    col_lower, col_upper, col_wlow, col_wup = tap_pair(col_points, P_SIZE)
    return (halfway[:, col_lower].astype(jnp.float32) * col_wlow.astype(jnp.float32)[None, :]
            + halfway[:, col_upper].astype(jnp.float32) * col_wup.astype(jnp.float32)[None, :]).astype(jnp.bfloat16)


def reference(patches, zoom, frac, offset, owner, top_grid):
    bands = Q // BAND
    points = sample_points(zoom, frac, offset, Q, P_SIZE)
    covered = coverage(points, P_SIZE)
    routes = owner[..., 0]

    def render_section(section_args):
        patch_set, point_set = section_args
        return jax.vmap(render_tile)(patch_set, point_set[0], point_set[1])

    rendered = lax.map(render_section, (patches, points))
    band_ids = jnp.arange(bands, dtype=jnp.int32)

    def grid_section(section_args):
        frames, route_set, cover_set = section_args
        segment = (route_set * bands + band_ids[None, :]).reshape(TILES * bands)
        band_stack = frames.reshape(TILES * bands, BAND * Q).astype(jnp.float32)
        image_sum = jax.ops.segment_sum(band_stack, segment, num_segments=GRID * bands)
        row_bands = cover_set[0].reshape(TILES * bands, BAND)
        col_rows = jnp.repeat(cover_set[1], bands, axis=0)
        products = (row_bands[:, :, None] * col_rows[:, None, :]).reshape(TILES * bands, BAND * Q)
        cover_sum = jax.ops.segment_sum(products, segment, num_segments=GRID * bands)
        return (image_sum / (1.0 + cover_sum)).astype(jnp.bfloat16).reshape(GRID, Q, Q)

    grid_image = lax.map(grid_section, (rendered, routes, covered))
    above_all = jnp.concatenate([grid_image[1:], top_grid[None]], axis=0)
    row_spots = jnp.arange(BAND, dtype=jnp.float32)
    row_pos = ((jnp.arange(TILES * bands, dtype=jnp.int32) % bands).astype(jnp.float32) * BAND)[:, None] + row_spots

    def normal_section(section_args):
        frames, route_set, cover_set, target_grid = section_args
        segment = (route_set * bands + band_ids[None, :]).reshape(TILES * bands)
        target = target_grid.reshape(GRID * bands, BAND, Q)[segment]
        row_bands = cover_set[0].reshape(TILES * bands, BAND)
        col_rows = jnp.repeat(cover_set[1], bands, axis=0)
        normal, gradient = blocked_moments(frames.reshape(TILES * bands, BAND, Q), target, row_bands, col_rows, row_pos, Q)
        return normal.reshape(TILES, bands, 6, 6).sum(axis=1), gradient.reshape(TILES, bands, 6).sum(axis=1)

    normals, gradients = lax.map(normal_section, (rendered, routes, covered, above_all))
    right_side = jnp.transpose(gradients, (2, 0, 1))
    diagonal_part = jnp.transpose(jnp.diagonal(normals, axis1=2, axis2=3), (2, 0, 1))
    precond = 1.0 / (diagonal_part + 4.0 * COUPLING)

    def apply_system(vector):
        padded = jnp.pad(vector, ((0, 0), (1, 1), (1, 1)))
        beside = padded[:, 2:, 1:-1] + padded[:, :-2, 1:-1] + padded[:, 1:-1, 2:] + padded[:, 1:-1, :-2]
        return jnp.einsum("stfg,gst->fst", normals, vector, precision=lax.Precision.HIGHEST) + COUPLING * (4.0 * vector - beside)

    solution = jnp.zeros_like(right_side)
    residual = right_side
    scaled = precond * residual
    direction = scaled
    current = jnp.sum(residual * scaled)
    for step in range(ITERS):
        image = apply_system(direction)
        alpha = current / jnp.sum(direction * image)
        solution = solution + alpha * direction
        if step + 1 < ITERS:
            residual = residual - alpha * image
            scaled = precond * residual
            following = jnp.sum(residual * scaled)
            direction = scaled + (following / current) * direction
            current = following
    return grid_image, solution
```

```python
import functools

import jax
import jax.numpy as jnp
from jax import lax
from jax.experimental import pallas as pl
from jax.experimental.pallas import tpu as pltpu
from jax.sharding import PartitionSpec as P

BAND = 16
ITERS = 2
COUPLING = 0.25
LANES = 128
ROWS = 8
SMEM = pl.BlockSpec(memory_space=pltpu.SMEM)
VMEM = pl.BlockSpec(memory_space=pltpu.VMEM)


def params(mebibytes):
    return pltpu.CompilerParams(vmem_limit_bytes=mebibytes * 1024 * 1024)


def cost(flops, size):
    return pl.CostEstimate(flops=flops, bytes_accessed=size, transcendentals=0)


def exact_dot(left, right):
    return lax.dot_general(
        left,
        right,
        (((1,), (1,)), ((), ())),
        precision=lax.Precision.HIGHEST,
        preferred_element_type=jnp.float32,
    )


def points_of(spots, zoom, frac, offset, axis, tile, ratio):
    scale = zoom[axis, tile] * ratio
    return (spots - offset[axis, tile].astype(jnp.float32) - frac[axis, tile]) / scale


def cover_of(points, source):
    return jnp.clip(jnp.minimum(points + 1.0, source - points), 0.0, 1.0)


def hat_weight(distance):
    return jnp.maximum(0.0, 1.0 - jnp.abs(distance))


def spots_along(shape, dim, start=0):
    return (lax.broadcasted_iota(jnp.int32, shape, dim) + start).astype(jnp.float32)


def coords(spots, frame):
    return (spots - (frame - 1) / 2.0) / (frame / 2.0)


def render_kernel(sizes, zoom, frac, offset, owner, patch, outgoing, frames, named):
    tiles, bands, frame, source, capacity, devices = sizes
    step = pl.program_id(0)
    tile = lax.axis_index("tile") * tiles + step

    @pl.when(step == 0)
    def _():
        for g in range(devices):
            named[g] = 0
        outgoing[...] = jnp.zeros_like(outgoing)

    ratio = frame / source
    row_points = points_of(spots_along((frame, LANES), 0), zoom, frac, offset, 0, tile, ratio)
    row_weights = jnp.concatenate(
        [
            hat_weight(row_points - spots_along((frame, LANES), 1, first)).astype(jnp.bfloat16)
            for first in range(0, source, LANES)
        ],
        axis=1,
    )
    col_points = points_of(spots_along((ROWS, frame), 1), zoom, frac, offset, 1, tile, ratio)
    col_points = jnp.broadcast_to(col_points[:1], (source, frame))
    col_weights = hat_weight(col_points - spots_along((source, frame), 0)).astype(jnp.bfloat16)
    halfway = jnp.dot(row_weights, patch[0], preferred_element_type=jnp.float32)
    rendered = jnp.dot(
        halfway.astype(jnp.bfloat16), col_weights, preferred_element_type=jnp.float32
    ).astype(jnp.bfloat16)
    frames[0] = rendered
    for band in range(bands):
        target = owner[band, 0, tile]
        slot = named[target]
        named[target] = slot + 1
        outgoing[target * capacity + slot] = rendered[band * BAND : (band + 1) * BAND]


def feature_rows(frame, wanted):
    shape = (ROWS, frame)
    x = coords(spots_along(shape, 1), frame)
    row = lax.broadcasted_iota(jnp.int32, shape, 0)
    rows = jnp.zeros(shape, jnp.float32)
    for r, power in wanted.items():
        rows = jnp.where(row == r, (jnp.ones_like(x), x, x * x)[power], rows)
    return rows


MOMENT_ROWS = ({0: 0, 1: 1, 3: 2}, {2: 0, 4: 1}, {5: 0})


def moment_kernel(
    sizes,
    zoom,
    frac,
    offset,
    owner,
    frames,
    base,
    cover_sum,
    col_cover,
    codes,
    parts,
):
    tiles, bands, frame, source, capacity, devices = sizes
    me = lax.axis_index("tile")
    sec = lax.axis_index("sec")
    sections = lax.axis_size("sec")
    all_tiles = tiles * devices
    ratio = frame / source

    for device in range(devices):

        def note(position, count):
            tile = device * tiles + position // bands
            band = position % bands
            codes[device * capacity + count] = tile * bands + band
            return count + (owner[band, 0, tile] == me).astype(jnp.int32)

        count = lax.fori_loop(0, tiles * bands, note, 0, unroll=8)

        def blank(position, carry):
            codes[device * capacity + position] = -1
            return carry

        lax.fori_loop(count, capacity, blank, 0)

    def cover_row(tile, carry):
        points = points_of(spots_along((1, frame), 1), zoom, frac, offset, 1, tile, ratio)
        col_cover[pl.ds(tile, 1), :] = cover_of(points, source)
        return carry

    lax.fori_loop(0, all_tiles, cover_row, 0, unroll=8)

    cover_sum[...] = jnp.zeros_like(cover_sum)

    def add_cover(slot, carry):
        code = codes[slot]

        @pl.when(code >= 0)
        def _():
            tile, band = code // bands, code % bands
            points = points_of(
                spots_along((BAND, frame), 0, band * BAND), zoom, frac, offset, 0, tile, ratio
            )
            cover_sum[band] += cover_of(points, source) * col_cover[pl.ds(tile, 1), :]

        return carry

    lax.fori_loop(0, devices * capacity, add_cover, 0)

    parts[...] = jnp.zeros_like(parts)
    for j in range(tiles):
        tile = me * tiles + j
        spots = spots_along((frame, frame), 0)
        y = coords(spots, frame)
        cover = cover_of(points_of(spots, zoom, frac, offset, 0, tile, ratio), source)
        level = frames[j].astype(jnp.float32)
        columns = col_cover[pl.ds(tile, 1), :]
        weighted = (cover, cover * y, cover * y * y)
        for power, image in enumerate((None, level, level * level)):
            block = (sec + 1 + power) % sections
            place = block * all_tiles + tile
            for a, rows in enumerate(weighted):
                total = rows if image is None else rows * image
                parts[a, pl.ds(place, 1), :] = columns * jnp.sum(total, axis=0, keepdims=True)
    total = exact_dot(feature_rows(frame, MOMENT_ROWS[0]), parts[0])
    for a in (1, 2):
        total += exact_dot(feature_rows(frame, MOMENT_ROWS[a]), parts[a])
    base[...] = total


def blend_kernel(sizes, codes, incoming, cover_sum, grid, total):
    tiles, bands, frame, source, capacity, devices = sizes
    total[...] = jnp.zeros_like(total)

    def add(slot, carry):
        code = codes[slot]

        @pl.when(code >= 0)
        def _():
            total[code % bands] += incoming[slot].astype(jnp.float32)

        return carry

    lax.fori_loop(0, devices * capacity, add, 0)
    grid[...] = (total[...] / (1.0 + cover_sum[...])).astype(jnp.bfloat16)


GRADIENT_ROWS = ({0: 0, 1: 1}, {2: 0}, {3: 0, 4: 1}, {5: 0})


def gradient_kernel(
    sizes,
    zoom,
    frac,
    offset,
    codes,
    incoming,
    from_next,
    top_grid,
    col_cover,
    base,
    payload,
    above,
    parts,
):
    tiles, bands, frame, source, capacity, devices = sizes
    sec = lax.axis_index("sec")
    sections = lax.axis_size("sec")
    all_tiles = tiles * devices
    ratio = frame / source

    @pl.when(sec == sections - 1)
    def _():
        above[...] = top_grid[...].astype(jnp.float32)

    @pl.when(sec != sections - 1)
    def _():
        above[...] = from_next[...].astype(jnp.float32)

    parts[...] = jnp.zeros_like(parts)

    def add(slot, carry):
        code = codes[slot]

        @pl.when(code >= 0)
        def _():
            tile, band = code // bands, code % bands
            spots = spots_along((BAND, frame), 0, band * BAND)
            cover = cover_of(points_of(spots, zoom, frac, offset, 0, tile, ratio), source)
            lifted = cover * coords(spots, frame)
            level = incoming[slot].astype(jnp.float32)
            error = above[band] - level
            product = error * level
            place = sec * all_tiles + tile
            for part, term in enumerate(
                (cover * error, lifted * error, cover * product, lifted * product)
            ):
                parts[part, pl.ds(place, 1), :] += jnp.sum(term, axis=0, keepdims=True)

        return carry

    lax.fori_loop(0, devices * capacity, add, 0)
    first = pl.multiple_of(sec * all_tiles, all_tiles)
    total = base[...]
    for part, wanted in enumerate(GRADIENT_ROWS):
        parts[part, pl.ds(first, all_tiles), :] *= col_cover[...]
        total += exact_dot(feature_rows(frame, wanted), parts[part])
    payload[...] = jnp.broadcast_to(total[None], payload.shape)


def solve_kernel(sizes, received, corrections):
    tiles, bands, frame, source, capacity, devices = sizes
    sec, me = lax.axis_index("sec"), lax.axis_index("tile")
    sections = lax.axis_size("sec")
    all_tiles = tiles * devices
    lanes = sections * all_tiles
    lane = lax.broadcasted_iota(jnp.int32, (ROWS, lanes), 1)
    within = lane % all_tiles
    area = frame * frame

    gradients = jnp.zeros((ROWS, lanes), jnp.float32)
    moments = [jnp.zeros((ROWS, lanes), jnp.float32) for _ in range(3)]
    for s in range(sections):
        own = received[s * devices]
        for t in range(1, devices):
            own += received[s * devices + t]
        here = lane // all_tiles == s
        gradients = jnp.where(here, own, gradients)
        for power in range(3):
            shift = ((sections - 1 - power) * all_tiles) % lanes
            moved = pltpu.roll(own, shift, 1) if shift else own
            moments[power] = jnp.where(here, moved, moments[power])
    gradients = gradients * (1.0 / area)
    moments = [m * (1.0 / area) for m in moments]

    where = ((0, 1, 2), (1, 3, 4), (2, 4, 5))
    row = lax.broadcasted_iota(jnp.int32, (ROWS, lanes), 0)

    def entry(f, g):
        kind = moments[(f >= 3) + (g >= 3)]
        index = where[f % 3][g % 3]
        return kind[index : index + 1]

    def stacked(rows):
        result = jnp.zeros((ROWS, lanes), jnp.float32)
        for f, value in enumerate(rows):
            result = jnp.where(row == f, value, result)
        return result

    normal = [stacked([entry(f, g) for f in range(6)]) for g in range(6)]
    diagonal = stacked([entry(f, f) for f in range(6)])
    precond = 1.0 / (diagonal + 4.0 * COUPLING)

    def total(values):
        return jnp.sum(jnp.sum(values, axis=1, keepdims=True), axis=0, keepdims=True)

    def operator(vector):
        beside = jnp.where(within < all_tiles - 1, pltpu.roll(vector, lanes - 1, 1), 0.0)
        beside += jnp.where(within > 0, pltpu.roll(vector, 1, 1), 0.0)
        upward = pltpu.roll(vector, lanes - all_tiles, 1)
        beside += jnp.where(lane < lanes - all_tiles, upward, 0.0)
        beside += jnp.where(lane >= all_tiles, pltpu.roll(vector, all_tiles, 1), 0.0)
        image = COUPLING * (4.0 * vector - beside)
        for g in range(6):
            image += normal[g] * vector[g : g + 1]
        return image

    answer = jnp.zeros((ROWS, lanes), jnp.float32)
    residual = gradients
    scaled = precond * residual
    direction = scaled
    current = total(residual * scaled)
    for step in range(ITERS):
        image = operator(direction)
        alpha = current / total(direction * image)
        answer = answer + alpha * direction
        if step + 1 < ITERS:
            residual = residual - alpha * image
            scaled = precond * residual
            following = total(residual * scaled)
            direction = scaled + following / current * direction
            current = following

    first = sec * all_tiles + me * tiles
    chosen = lax.broadcasted_iota(jnp.int32, (ROWS, lanes), 0) + first == lane
    own = exact_dot(chosen.astype(jnp.float32), answer)
    corrections[...] = own[:tiles, :6]


def shards(patches, zoom, frac, offset, owner, top_grid):
    _, tiles, source, _ = patches.shape
    frame = top_grid.shape[1]
    devices, sections = lax.axis_size("tile"), lax.axis_size("sec")
    bands = frame // BAND
    capacity = max(2, 2 * tiles * bands // devices)
    slots = devices * capacity
    all_tiles = tiles * devices
    lanes = sections * all_tiles
    sizes = (tiles, bands, frame, source, capacity, devices)
    place = (zoom[0], frac[0], offset[0])
    routes = jnp.transpose(owner, (0, 2, 3, 1))[0]

    whole = lambda *shape: pl.BlockSpec(shape, lambda i: (0,) * len(shape))
    outgoing, frames = pl.pallas_call(
        functools.partial(render_kernel, sizes),
        name="render",
        grid=(tiles,),
        in_specs=[SMEM] * 4 + [pl.BlockSpec((1, source, source), lambda i: (i, 0, 0))],
        out_specs=[
            whole(slots, BAND, frame),
            pl.BlockSpec((1, frame, frame), lambda i: (i, 0, 0)),
        ],
        out_shape=[
            jax.ShapeDtypeStruct((slots, BAND, frame), jnp.bfloat16),
            jax.ShapeDtypeStruct((tiles, frame, frame), jnp.bfloat16),
        ],
        scratch_shapes=[pltpu.SMEM((devices,), jnp.int32)],
        compiler_params=params(24),
        cost_estimate=cost(800_000_000, 4 << 20),
    )(*place, routes, patches[0])

    incoming = lax.all_to_all(
        outgoing.reshape(devices, capacity, BAND, frame),
        "tile",
        split_axis=0,
        concat_axis=0,
        tiled=True,
    ).reshape(slots, BAND, frame)

    base, cover_sum, col_cover, codes = pl.pallas_call(
        functools.partial(moment_kernel, sizes),
        name="moments",
        in_specs=[SMEM] * 4 + [VMEM],
        out_specs=[VMEM, VMEM, VMEM, SMEM],
        out_shape=[
            jax.ShapeDtypeStruct((ROWS, lanes), jnp.float32),
            jax.ShapeDtypeStruct((bands, BAND, frame), jnp.float32),
            jax.ShapeDtypeStruct((all_tiles, frame), jnp.float32),
            jax.ShapeDtypeStruct((slots + 1,), jnp.int32),
        ],
        scratch_shapes=[pltpu.VMEM((3, lanes, frame), jnp.float32)],
        compiler_params=params(24),
        cost_estimate=cost(20_000_000, 1 << 20),
    )(*place, routes, frames)

    grid = pl.pallas_call(
        functools.partial(blend_kernel, sizes),
        name="blend",
        in_specs=[SMEM, VMEM, VMEM],
        out_specs=VMEM,
        out_shape=jax.ShapeDtypeStruct((bands, BAND, frame), jnp.bfloat16),
        scratch_shapes=[pltpu.VMEM((bands, BAND, frame), jnp.float32)],
        compiler_params=params(24),
        cost_estimate=cost(1_000_000, 2 << 20),
    )(codes, incoming, cover_sum)

    from_next = lax.ppermute(grid, "sec", [(i, (i - 1) % sections) for i in range(sections)])

    payload = pl.pallas_call(
        functools.partial(gradient_kernel, sizes),
        name="gradient",
        in_specs=[SMEM] * 4 + [VMEM] * 5,
        out_specs=VMEM,
        out_shape=jax.ShapeDtypeStruct((sections * devices, ROWS, lanes), jnp.float32),
        scratch_shapes=[
            pltpu.VMEM((bands, BAND, frame), jnp.float32),
            pltpu.VMEM((4, lanes, frame), jnp.float32),
        ],
        compiler_params=params(24),
        cost_estimate=cost(8_000_000, 2 << 20),
    )(
        *place,
        codes,
        incoming,
        from_next,
        top_grid.reshape(bands, BAND, frame),
        col_cover,
        base,
    )

    received = lax.all_to_all(
        payload, ("sec", "tile"), split_axis=0, concat_axis=0, tiled=True
    )

    corrections = pl.pallas_call(
        functools.partial(solve_kernel, sizes),
        name="solve",
        in_specs=[VMEM],
        out_specs=VMEM,
        out_shape=jax.ShapeDtypeStruct((tiles, 6), jnp.float32),
        compiler_params=params(24),
        cost_estimate=cost(100_000, 1 << 18),
    )(received)
    return (
        grid.reshape(1, 1, frame, frame),
        jnp.transpose(corrections[None], (2, 0, 1)),
    )


def solution(mesh):
    placed = (
        P("sec", "tile", None, None),
        P("sec", None, None),
        P("sec", None, None),
        P("sec", None, None),
        P("sec", None, None, None),
        P("tile", None, None),
    )
    return jax.shard_map(
        shards,
        mesh=mesh,
        in_specs=placed,
        out_specs=(P("sec", "tile", None, None), P(None, "sec", "tile")),
        check_vma=False,
    )
```

```python
import functools
import math

import jax
import jax.numpy as jnp
from jax import lax
from jax.experimental import pallas as pl
from jax.experimental.pallas import tpu as pltpu
from jax.sharding import PartitionSpec as P

BAND = 16
ITERS = 2
COUPLING = 0.25
LANES = 128
ROWS = 8
ANY = pl.BlockSpec(memory_space=pl.ANY)
SMEM = pl.BlockSpec(memory_space=pltpu.SMEM)
VMEM = pl.BlockSpec(memory_space=pltpu.VMEM)


def params(mebibytes):
    return pltpu.CompilerParams(vmem_limit_bytes=mebibytes * 1024 * 1024)


def cost(flops, size):
    return pl.CostEstimate(flops=flops, bytes_accessed=size, transcendentals=0)


def exact_dot(left, right):
    return lax.dot_general(
        left,
        right,
        (((1,), (1,)), ((), ())),
        precision=lax.Precision.HIGHEST,
        preferred_element_type=jnp.float32,
    )


def points_of(spots, zoom, frac, offset, axis, tile, ratio):
    scale = zoom[axis, tile] * ratio
    return (spots - offset[axis, tile].astype(jnp.float32) - frac[axis, tile]) / scale


def cover_of(points, source):
    return jnp.clip(jnp.minimum(points + 1.0, source - points), 0.0, 1.0)


def hat_weight(distance):
    return jnp.maximum(0.0, 1.0 - jnp.abs(distance))


def spots_along(shape, dim, start=0):
    return (lax.broadcasted_iota(jnp.int32, shape, dim) + start).astype(jnp.float32)


def coords(spots, frame):
    return (spots - (frame - 1) / 2.0) / (frame / 2.0)


def render_kernel(
    sizes,
    zoom_in,
    frac_in,
    offset_in,
    owner_in,
    patches_in,
    outgoing,
    frames_out,
    zoom,
    frac,
    offset,
    owner,
    patches,
    frames,
    named,
    small_sems,
    patch_sems,
    frame_sem,
    band_sem,
):
    tiles, bands, frame, source, capacity, devices = sizes
    first = lax.axis_index("tile") * tiles
    ratio = frame / source
    fetched = [
        pltpu.make_async_copy(patches_in.at[j], patches.at[j], patch_sems.at[j])
        for j in range(tiles)
    ]
    small = [
        pltpu.make_async_copy(there, here, small_sems.at[k])
        for k, (there, here) in enumerate(
            ((zoom_in, zoom), (frac_in, frac), (offset_in, offset), (owner_in, owner))
        )
    ]
    for copy in small + fetched:
        copy.start()
    for g in range(devices):
        named[g] = 0
    for copy in small:
        copy.wait()
    for j in range(tiles):
        tile = first + j
        row_points = points_of(spots_along((frame, LANES), 0), zoom, frac, offset, 0, tile, ratio)
        row_weights = jnp.concatenate(
            [
                hat_weight(row_points - spots_along((frame, LANES), 1, p)).astype(jnp.bfloat16)
                for p in range(0, source, LANES)
            ],
            axis=1,
        )
        col_points = points_of(spots_along((ROWS, frame), 1), zoom, frac, offset, 1, tile, ratio)
        col_points = jnp.broadcast_to(col_points[:1], (source, frame))
        col_weights = hat_weight(col_points - spots_along((source, frame), 0)).astype(jnp.bfloat16)
        fetched[j].wait()
        halfway = jnp.dot(row_weights, patches[j], preferred_element_type=jnp.float32)
        rendered = jnp.dot(
            halfway.astype(jnp.bfloat16), col_weights, preferred_element_type=jnp.float32
        ).astype(jnp.bfloat16)
        for band in range(bands):
            row = j * bands + band
            frames[row] = rendered[band * BAND : (band + 1) * BAND]
            target = owner[band, 0, tile]
            slot = named[target]
            named[target] = slot + 1
            pltpu.make_async_copy(
                frames.at[row], outgoing.at[target * capacity + slot], band_sem
            ).start()
    kept = pltpu.make_async_copy(frames, frames_out, frame_sem)
    kept.start()
    pltpu.make_async_copy(frames, outgoing.at[pl.ds(0, tiles * bands)], band_sem).wait()
    kept.wait()


def feature_rows(frame, wanted):
    shape = (ROWS, frame)
    x = coords(spots_along(shape, 1), frame)
    row = lax.broadcasted_iota(jnp.int32, shape, 0)
    rows = jnp.zeros(shape, jnp.float32)
    for r, power in wanted.items():
        rows = jnp.where(row == r, (jnp.ones_like(x), x, x * x)[power], rows)
    return rows


MOMENT_ROWS = ({0: 0, 1: 1, 3: 2}, {2: 0, 4: 1}, {5: 0})


def moment_kernel(
    sizes,
    zoom,
    frac,
    offset,
    owner,
    frames,
    base,
    cover_sum,
    slot_cover,
    slot_lines,
    slot_bands,
    codes,
    col_cover,
    parts,
):
    tiles, bands, frame, source, capacity, devices = sizes
    me = lax.axis_index("tile")
    sec = lax.axis_index("sec")
    sections = lax.axis_size("sec")
    all_tiles = tiles * devices
    ratio = frame / source

    for device in range(devices):

        def note(position, count):
            tile = device * tiles + position // bands
            band = position % bands
            codes[device * capacity + count] = tile * bands + band
            return count + (owner[band, 0, tile] == me).astype(jnp.int32)

        count = lax.fori_loop(0, tiles * bands, note, 0, unroll=8)

        def blank(position, carry):
            codes[device * capacity + position] = -1
            return carry

        lax.fori_loop(count, capacity, blank, 0)

    def cover_row(tile, carry):
        points = points_of(spots_along((1, frame), 1), zoom, frac, offset, 1, tile, ratio)
        col_cover[pl.ds(tile, 1), :] = cover_of(points, source)
        return carry

    lax.fori_loop(0, all_tiles, cover_row, 0, unroll=8)

    cover_sum[...] = jnp.zeros_like(cover_sum)

    def describe(slot, carry):
        code = codes[slot]
        used = code >= 0
        code = jnp.maximum(code, 0)
        tile, band = code // bands, code % bands
        slot_bands[slot] = jnp.where(used, band, bands)
        here = pl.ds(slot, 1)
        row = jnp.zeros((1, LANES), jnp.float32)
        start = (band * BAND).astype(jnp.float32)
        scale = row + zoom[0, tile] * ratio
        slot_lines[0, here, :] = 1.0 / scale
        slot_lines[1, here, :] = (
            row + start - offset[0, tile].astype(jnp.float32) - frac[0, tile]
        ) / scale
        slot_lines[2, here, :] = coords(row + start, frame)
        place = jnp.where(used, sec * all_tiles + tile, -1)
        slot_lines[3, here, :] = row + place.astype(jnp.float32)
        slot_cover[here, :] = col_cover[pl.ds(tile, 1), :]

        @pl.when(used)
        def _():
            points = points_of(
                spots_along((BAND, frame), 0, band * BAND), zoom, frac, offset, 0, tile, ratio
            )
            cover_sum[band] += cover_of(points, source) * col_cover[pl.ds(tile, 1), :]

        return carry

    lax.fori_loop(0, devices * capacity, describe, 0)

    parts[...] = jnp.zeros_like(parts)
    for j in range(tiles):
        tile = me * tiles + j
        spots = spots_along((frame, frame), 0)
        y = coords(spots, frame)
        cover = cover_of(points_of(spots, zoom, frac, offset, 0, tile, ratio), source)
        level = frames[j * bands : (j + 1) * bands].reshape(frame, frame).astype(jnp.float32)
        columns = col_cover[pl.ds(tile, 1), :]
        weighted = (cover, cover * y, cover * y * y)
        for power, image in enumerate((None, level, level * level)):
            block = (sec + 1 + power) % sections
            place = block * all_tiles + tile
            for a, rows in enumerate(weighted):
                total = rows if image is None else rows * image
                parts[a, pl.ds(place, 1), :] = columns * jnp.sum(total, axis=0, keepdims=True)
    total = exact_dot(feature_rows(frame, MOMENT_ROWS[0]), parts[0])
    for a in (1, 2):
        total += exact_dot(feature_rows(frame, MOMENT_ROWS[a]), parts[a])
    base[...] = total


def blend_kernel(sizes, unroll, slot_bands, incoming, cover_sum, grid, total):
    tiles, bands, frame, source, capacity, devices = sizes
    total[...] = jnp.zeros_like(total)

    def add(group, carry):
        for k in range(unroll):
            slot = group * unroll + k
            total[slot_bands[slot]] += incoming[slot].astype(jnp.float32)
        return carry

    lax.fori_loop(0, devices * capacity // unroll, add, 0)
    grid[...] = (total[:bands] / (1.0 + cover_sum[...])).astype(jnp.bfloat16)


GRADIENT_ROWS = ({0: 0, 1: 1}, {2: 0}, {3: 0, 4: 1}, {5: 0})


def gradient_kernel(
    sizes,
    unroll,
    slot_bands,
    incoming,
    from_next,
    top_grid,
    slot_cover,
    slot_lines,
    base,
    payload,
    above,
    sums,
):
    tiles, bands, frame, source, capacity, devices = sizes
    sec = lax.axis_index("sec")
    slots = devices * capacity
    lanes = base.shape[1]

    @pl.when(sec == lax.axis_size("sec") - 1)
    def _():
        above[:bands] = top_grid[...].astype(jnp.float32)

    @pl.when(sec != lax.axis_size("sec") - 1)
    def _():
        above[:bands] = from_next[...].astype(jnp.float32)

    above[bands] = jnp.zeros((BAND, frame), jnp.float32)
    spots = spots_along((BAND, LANES), 0)
    raised = spots * (2.0 / frame)

    def add(group, carry):
        for k in range(unroll):
            slot = group * unroll + k
            here = pl.ds(slot, 1)
            points = spots * slot_lines[0, here, :] + slot_lines[1, here, :]
            cover = cover_of(points, source)
            lifted = cover * (raised + slot_lines[2, here, :])
            level = incoming[slot].astype(jnp.float32)
            error = above[slot_bands[slot]] - level
            product = error * level
            rows = pl.ds(pl.multiple_of(slot * ROWS, ROWS), ROWS)
            for half in range(frame // LANES):
                part = slice(half * LANES, (half + 1) * LANES)
                for kind, (weight, value) in enumerate(
                    ((cover, error), (lifted, error), (cover, product), (lifted, product))
                ):
                    term = weight * value[:, part]
                    sums[kind, half, rows, :] = term[:ROWS] + term[ROWS:]
        return carry

    lax.fori_loop(0, slots // unroll, add, 0)
    used = slot_lines[3] >= 0.0
    by_slot = jnp.zeros((ROWS, slots), jnp.float32)
    for kind, wanted in enumerate(GRADIENT_ROWS):
        halves = []
        for half in range(frame // LANES):
            value = sums[kind, half, pl.ds(0, slots, stride=ROWS), :]
            for r in range(1, ROWS):
                value += sums[kind, half, pl.ds(r, slots, stride=ROWS), :]
            columns = slot_cover[:, half * LANES : (half + 1) * LANES]
            halves.append(jnp.where(used, value * columns, 0.0))
        by_slot += exact_dot(feature_rows(frame, wanted), jnp.concatenate(halves, axis=1))
    places = jnp.concatenate(
        [
            (slot_lines[3] == spots_along((slots, LANES), 1, p)).astype(jnp.float32)
            for p in range(0, lanes, LANES)
        ],
        axis=1,
    )
    total = base[...] + lax.dot_general(
        by_slot,
        places,
        (((1,), (0,)), ((), ())),
        precision=lax.Precision.HIGHEST,
        preferred_element_type=jnp.float32,
    )
    payload[...] = jnp.broadcast_to(total[None], payload.shape)


def solve_kernel(sizes, received, corrections):
    tiles, bands, frame, source, capacity, devices = sizes
    sec, me = lax.axis_index("sec"), lax.axis_index("tile")
    sections = lax.axis_size("sec")
    all_tiles = tiles * devices
    lanes = sections * all_tiles
    lane = lax.broadcasted_iota(jnp.int32, (ROWS, lanes), 1)
    within = lane % all_tiles
    area = frame * frame

    gradients = jnp.zeros((ROWS, lanes), jnp.float32)
    moments = [jnp.zeros((ROWS, lanes), jnp.float32) for _ in range(3)]
    for s in range(sections):
        own = received[s * devices]
        for t in range(1, devices):
            own += received[s * devices + t]
        here = lane // all_tiles == s
        gradients = jnp.where(here, own, gradients)
        for power in range(3):
            shift = ((sections - 1 - power) * all_tiles) % lanes
            moved = pltpu.roll(own, shift, 1) if shift else own
            moments[power] = jnp.where(here, moved, moments[power])
    gradients = gradients * (1.0 / area)
    moments = [m * (1.0 / area) for m in moments]

    where = ((0, 1, 2), (1, 3, 4), (2, 4, 5))
    row = lax.broadcasted_iota(jnp.int32, (ROWS, lanes), 0)

    def entry(f, g):
        kind = moments[(f >= 3) + (g >= 3)]
        index = where[f % 3][g % 3]
        return kind[index : index + 1]

    def stacked(rows):
        result = jnp.zeros((ROWS, lanes), jnp.float32)
        for f, value in enumerate(rows):
            result = jnp.where(row == f, value, result)
        return result

    normal = [stacked([entry(f, g) for f in range(6)]) for g in range(6)]
    diagonal = stacked([entry(f, f) for f in range(6)])
    precond = 1.0 / (diagonal + 4.0 * COUPLING)

    def total(values):
        return jnp.sum(jnp.sum(values, axis=1, keepdims=True), axis=0, keepdims=True)

    def operator(vector):
        beside = jnp.where(within < all_tiles - 1, pltpu.roll(vector, lanes - 1, 1), 0.0)
        beside += jnp.where(within > 0, pltpu.roll(vector, 1, 1), 0.0)
        upward = pltpu.roll(vector, lanes - all_tiles, 1)
        beside += jnp.where(lane < lanes - all_tiles, upward, 0.0)
        beside += jnp.where(lane >= all_tiles, pltpu.roll(vector, all_tiles, 1), 0.0)
        image = COUPLING * (4.0 * vector - beside)
        for g in range(6):
            image += normal[g] * vector[g : g + 1]
        return image

    answer = jnp.zeros((ROWS, lanes), jnp.float32)
    residual = gradients
    scaled = precond * residual
    direction = scaled
    current = total(residual * scaled)
    for step in range(ITERS):
        image = operator(direction)
        alpha = current / total(direction * image)
        answer = answer + alpha * direction
        if step + 1 < ITERS:
            residual = residual - alpha * image
            scaled = precond * residual
            following = total(residual * scaled)
            direction = scaled + following / current * direction
            current = following

    first = sec * all_tiles + me * tiles
    chosen = lax.broadcasted_iota(jnp.int32, (ROWS, lanes), 0) + first == lane
    own = exact_dot(chosen.astype(jnp.float32), answer)
    corrections[...] = own[:tiles, :6]


def shards(patches, zoom, frac, offset, owner, top_grid):
    _, tiles, source, _ = patches.shape
    frame = top_grid.shape[1]
    devices, sections = lax.axis_size("tile"), lax.axis_size("sec")
    bands = frame // BAND
    capacity = max(2, 2 * tiles * bands // devices)
    slots = devices * capacity
    all_tiles = tiles * devices
    lanes = sections * all_tiles
    sizes = (tiles, bands, frame, source, capacity, devices)
    place = (zoom[0], frac[0], offset[0])
    routes = jnp.transpose(owner, (0, 2, 3, 1))[0]

    unroll = math.gcd(slots, 16)
    rows = tiles * bands
    outgoing, frames = pl.pallas_call(
        functools.partial(render_kernel, sizes),
        name="render",
        in_specs=[ANY] * 5,
        out_specs=[ANY] * 2,
        out_shape=[
            jax.ShapeDtypeStruct((slots, BAND, frame), jnp.bfloat16),
            jax.ShapeDtypeStruct((rows, BAND, frame), jnp.bfloat16),
        ],
        scratch_shapes=[
            pltpu.SMEM(place[0].shape, jnp.float32),
            pltpu.SMEM(place[1].shape, jnp.float32),
            pltpu.SMEM(place[2].shape, jnp.int32),
            pltpu.SMEM(routes.shape, jnp.int32),
            pltpu.VMEM((tiles, source, source), jnp.bfloat16),
            pltpu.VMEM((rows, BAND, frame), jnp.bfloat16),
            pltpu.SMEM((devices,), jnp.int32),
            pltpu.SemaphoreType.DMA((4,)),
            pltpu.SemaphoreType.DMA((tiles,)),
            pltpu.SemaphoreType.DMA,
            pltpu.SemaphoreType.DMA,
        ],
        compiler_params=params(58),
        cost_estimate=cost(800_000_000, 4 << 20),
    )(*place, routes, patches[0])

    incoming = lax.all_to_all(
        outgoing.reshape(devices, capacity, BAND, frame),
        "tile",
        split_axis=0,
        concat_axis=0,
        tiled=True,
    ).reshape(slots, BAND, frame)

    base, cover_sum, slot_cover, slot_lines, slot_bands = pl.pallas_call(
        functools.partial(moment_kernel, sizes),
        name="moments",
        in_specs=[SMEM] * 4 + [VMEM],
        out_specs=[VMEM, VMEM, VMEM, VMEM, SMEM],
        out_shape=[
            jax.ShapeDtypeStruct((ROWS, lanes), jnp.float32),
            jax.ShapeDtypeStruct((bands, BAND, frame), jnp.float32),
            jax.ShapeDtypeStruct((slots, frame), jnp.float32),
            jax.ShapeDtypeStruct((4, slots, LANES), jnp.float32),
            jax.ShapeDtypeStruct((slots,), jnp.int32),
        ],
        scratch_shapes=[
            pltpu.SMEM((slots + 1,), jnp.int32),
            pltpu.VMEM((all_tiles, frame), jnp.float32),
            pltpu.VMEM((3, lanes, frame), jnp.float32),
        ],
        compiler_params=params(24),
        cost_estimate=cost(20_000_000, 1 << 20),
    )(*place, routes, frames)

    grid = pl.pallas_call(
        functools.partial(blend_kernel, sizes, unroll),
        name="blend",
        in_specs=[SMEM, VMEM, VMEM],
        out_specs=VMEM,
        out_shape=jax.ShapeDtypeStruct((bands, BAND, frame), jnp.bfloat16),
        scratch_shapes=[pltpu.VMEM((bands + 1, BAND, frame), jnp.float32)],
        compiler_params=params(24),
        cost_estimate=cost(1_000_000, 2 << 20),
    )(slot_bands, incoming, cover_sum)

    from_next = lax.ppermute(grid, "sec", [(i, (i - 1) % sections) for i in range(sections)])

    payload = pl.pallas_call(
        functools.partial(gradient_kernel, sizes, unroll),
        name="gradient",
        in_specs=[SMEM] + [VMEM] * 6,
        out_specs=VMEM,
        out_shape=jax.ShapeDtypeStruct((sections * devices, ROWS, lanes), jnp.float32),
        scratch_shapes=[
            pltpu.VMEM((bands + 1, BAND, frame), jnp.float32),
            pltpu.VMEM((4, frame // LANES, slots * ROWS, LANES), jnp.float32),
        ],
        compiler_params=params(24),
        cost_estimate=cost(8_000_000, 2 << 20),
    )(
        slot_bands,
        incoming,
        from_next,
        top_grid.reshape(bands, BAND, frame),
        slot_cover,
        slot_lines,
        base,
    )

    received = lax.all_to_all(
        payload, ("sec", "tile"), split_axis=0, concat_axis=0, tiled=True
    )

    corrections = pl.pallas_call(
        functools.partial(solve_kernel, sizes),
        name="solve",
        in_specs=[VMEM],
        out_specs=VMEM,
        out_shape=jax.ShapeDtypeStruct((tiles, 6), jnp.float32),
        compiler_params=params(24),
        cost_estimate=cost(100_000, 1 << 18),
    )(received)
    return (
        grid.reshape(1, 1, frame, frame),
        jnp.transpose(corrections[None], (2, 0, 1)),
    )


def solution(mesh):
    placed = (
        P("sec", "tile", None, None),
        P("sec", None, None),
        P("sec", None, None),
        P("sec", None, None),
        P("sec", None, None, None),
        P("tile", None, None),
    )
    return jax.shard_map(
        shards,
        mesh=mesh,
        in_specs=placed,
        out_specs=(P("sec", "tile", None, None), P(None, "sec", "tile")),
        check_vma=False,
    )
```

```python
import functools

import jax
import jax.numpy as jnp
from jax import lax
from jax.experimental import pallas as pl
from jax.experimental.pallas import tpu as pltpu
from jax.sharding import PartitionSpec as P

BAND = 16
ITERS = 2
COUPLING = 0.25
LANES = 128
ROWS = 8
HBM = pl.BlockSpec(memory_space=pltpu.HBM)
SMEM = pl.BlockSpec(memory_space=pltpu.SMEM)
VMEM = pl.BlockSpec(memory_space=pltpu.VMEM)


def params(mebibytes):
    return pltpu.CompilerParams(vmem_limit_bytes=mebibytes * 1024 * 1024)


def cost(flops, size):
    return pl.CostEstimate(flops=flops, bytes_accessed=size, transcendentals=0)


def exact_dot(left, right):
    return lax.dot_general(
        left,
        right,
        (((1,), (1,)), ((), ())),
        precision=lax.Precision.HIGHEST,
        preferred_element_type=jnp.float32,
    )


def points_of(spots, zoom, frac, offset, axis, tile, ratio):
    scale = zoom[axis, tile] * ratio
    return (spots - offset[axis, tile].astype(jnp.float32) - frac[axis, tile]) / scale


def cover_of(points, source):
    return jnp.clip(jnp.minimum(points + 1.0, source - points), 0.0, 1.0)


def hat_weight(distance):
    return jnp.maximum(0.0, 1.0 - jnp.abs(distance))


def spots_along(shape, dim, start=0):
    return (lax.broadcasted_iota(jnp.int32, shape, dim) + start).astype(jnp.float32)


def coords(spots, frame):
    return (spots - (frame - 1) / 2.0) / (frame / 2.0)


def render_kernel(
    sizes, zoom_in, frac_in, offset_in, owner_in, patches_in, frames, *outgoing_and_scratch
):
    tiles, bands, frame, source, capacity, devices = sizes
    outgoing = outgoing_and_scratch[:devices]
    zoom, frac, offset, owner, patches, named, rows, small_sems, patch_sems = (
        outgoing_and_scratch[devices:]
    )
    me = lax.axis_index("tile")
    first = me * tiles
    ratio = frame / source
    fetched = [
        pltpu.make_async_copy(patches_in.at[j], patches.at[j], patch_sems.at[j])
        for j in range(tiles)
    ]
    small = [
        pltpu.make_async_copy(there, here, small_sems.at[k])
        for k, (there, here) in enumerate(
            ((zoom_in, zoom), (frac_in, frac), (offset_in, offset), (owner_in, owner))
        )
    ]
    for copy in small + fetched:
        copy.start()
    for g in range(devices):
        named[g] = 0
    for slot in range(devices * capacity):
        rows[slot] = 0
    for copy in small:
        copy.wait()
    for j in range(tiles):
        for band in range(bands):
            target = owner[band, 0, first + j]
            slot = named[target]
            named[target] = slot + 1
            rows[target * capacity + slot] = j * bands + band
    for j in range(tiles):
        tile = first + j
        row_points = points_of(spots_along((frame, LANES), 0), zoom, frac, offset, 0, tile, ratio)
        row_weights = jnp.concatenate(
            [
                hat_weight(row_points - spots_along((frame, LANES), 1, p)).astype(jnp.bfloat16)
                for p in range(0, source, LANES)
            ],
            axis=1,
        )
        col_points = points_of(spots_along((ROWS, frame), 1), zoom, frac, offset, 1, tile, ratio)
        col_points = jnp.broadcast_to(col_points[:1], (source, frame))
        col_weights = hat_weight(col_points - spots_along((source, frame), 0)).astype(jnp.bfloat16)
        fetched[j].wait()
        halfway = jnp.dot(row_weights, patches[j], preferred_element_type=jnp.float32)
        rendered = jnp.dot(
            halfway.astype(jnp.bfloat16), col_weights, preferred_element_type=jnp.float32
        ).astype(jnp.bfloat16)
        frames[j * bands : (j + 1) * bands] = rendered.reshape(bands, BAND, frame)
    for distance in range(devices):
        target = me ^ distance
        for slot in range(capacity):
            outgoing[distance][slot] = frames[rows[target * capacity + slot]]


def feature_rows(frame, wanted):
    shape = (ROWS, frame)
    x = coords(spots_along(shape, 1), frame)
    row = lax.broadcasted_iota(jnp.int32, shape, 0)
    rows = jnp.zeros(shape, jnp.float32)
    for r, power in wanted.items():
        rows = jnp.where(row == r, (jnp.ones_like(x), x, x * x)[power], rows)
    return rows


MOMENT_ROWS = ({0: 0, 1: 1, 3: 2}, {2: 0, 4: 1}, {5: 0})


def moment_kernel(
    sizes,
    zoom,
    frac,
    offset,
    owner,
    frames,
    base,
    cover_sum,
    slot_cover,
    slot_lines,
    slot_bands,
    codes,
    col_cover,
    parts,
):
    tiles, bands, frame, source, capacity, devices = sizes
    me = lax.axis_index("tile")
    sec = lax.axis_index("sec")
    sections = lax.axis_size("sec")
    all_tiles = tiles * devices
    ratio = frame / source

    for distance in range(devices):
        device = me ^ distance

        def note(position, count):
            tile = device * tiles + position // bands
            band = position % bands
            codes[distance * capacity + count] = tile * bands + band
            return count + (owner[band, 0, tile] == me).astype(jnp.int32)

        count = lax.fori_loop(0, tiles * bands, note, 0, unroll=8)

        def blank(position, carry):
            codes[distance * capacity + position] = -1
            return carry

        lax.fori_loop(count, capacity, blank, 0)

    def cover_row(tile, carry):
        points = points_of(spots_along((1, frame), 1), zoom, frac, offset, 1, tile, ratio)
        col_cover[pl.ds(tile, 1), :] = cover_of(points, source)
        return carry

    lax.fori_loop(0, all_tiles, cover_row, 0, unroll=8)

    cover_sum[...] = jnp.zeros_like(cover_sum)

    def describe(slot, carry):
        code = codes[slot]
        used = code >= 0
        code = jnp.maximum(code, 0)
        tile, band = code // bands, code % bands
        slot_bands[slot] = jnp.where(used, band, bands)
        here = pl.ds(slot, 1)
        row = jnp.zeros((1, LANES), jnp.float32)
        start = (band * BAND).astype(jnp.float32)
        scale = row + zoom[0, tile] * ratio
        slot_lines[0, here, :] = 1.0 / scale
        slot_lines[1, here, :] = (
            row + start - offset[0, tile].astype(jnp.float32) - frac[0, tile]
        ) / scale
        slot_lines[2, here, :] = coords(row + start, frame)
        place = jnp.where(used, sec * all_tiles + tile, -1)
        slot_lines[3, here, :] = row + place.astype(jnp.float32)
        slot_cover[here, :] = col_cover[pl.ds(tile, 1), :]

        @pl.when(used)
        def _():
            points = points_of(
                spots_along((BAND, frame), 0, band * BAND), zoom, frac, offset, 0, tile, ratio
            )
            cover_sum[band] += cover_of(points, source) * col_cover[pl.ds(tile, 1), :]

        return carry

    lax.fori_loop(0, devices * capacity, describe, 0)

    parts[...] = jnp.zeros_like(parts)
    for j in range(tiles):
        tile = me * tiles + j
        spots = spots_along((frame, frame), 0)
        y = coords(spots, frame)
        cover = cover_of(points_of(spots, zoom, frac, offset, 0, tile, ratio), source)
        level = frames[j * bands : (j + 1) * bands].reshape(frame, frame).astype(jnp.float32)
        columns = col_cover[pl.ds(tile, 1), :]
        weighted = (cover, cover * y, cover * y * y)
        for power, image in enumerate((None, level, level * level)):
            block = (sec + 1 + power) % sections
            place = block * all_tiles + tile
            for a, rows in enumerate(weighted):
                total = rows if image is None else rows * image
                parts[a, pl.ds(place, 1), :] = columns * jnp.sum(total, axis=0, keepdims=True)
    total = exact_dot(feature_rows(frame, MOMENT_ROWS[0]), parts[0])
    for a in (1, 2):
        total += exact_dot(feature_rows(frame, MOMENT_ROWS[a]), parts[a])
    base[...] = total


def blend_kernel(sizes, slot_bands, cover_sum, *blocks_and_rest):
    tiles, bands, frame, source, capacity, devices = sizes
    blocks = blocks_and_rest[:devices]
    grid, total = blocks_and_rest[devices:]
    total[...] = jnp.zeros_like(total)
    for distance, block in enumerate(blocks):
        for k in range(capacity):
            total[slot_bands[distance * capacity + k]] += block[k].astype(jnp.float32)
    grid[...] = (total[:bands] / (1.0 + cover_sum[...])).astype(jnp.bfloat16)


GRADIENT_ROWS = ({0: 0, 1: 1}, {2: 0}, {3: 0, 4: 1}, {5: 0})


def gradient_kernel(
    sizes, slot_bands, from_next, top_grid, slot_cover, slot_lines, base, grid, *blocks_and_rest
):
    devices = sizes[-1]
    blocks = blocks_and_rest[:devices]
    payload, grid_out, above, sums, grid_sem = blocks_and_rest[devices:]
    written = pltpu.make_async_copy(grid, grid_out, grid_sem)
    written.start()
    tiles, bands, frame, source, capacity, devices = sizes
    sec = lax.axis_index("sec")
    slots = devices * capacity
    lanes = base.shape[1]

    @pl.when(sec == lax.axis_size("sec") - 1)
    def _():
        above[:bands] = top_grid[...].astype(jnp.float32)

    @pl.when(sec != lax.axis_size("sec") - 1)
    def _():
        above[:bands] = from_next[...].astype(jnp.float32)

    above[bands] = jnp.zeros((BAND, frame), jnp.float32)
    spots = spots_along((BAND, LANES), 0)
    raised = spots * (2.0 / frame)

    for distance, block in enumerate(blocks):
        for k in range(capacity):
            slot = distance * capacity + k
            here = slice(slot, slot + 1)
            points = spots * slot_lines[0, here] + slot_lines[1, here]
            cover = cover_of(points, source)
            lifted = cover * (raised + slot_lines[2, here])
            level = block[k].astype(jnp.float32)
            error = above[slot_bands[slot]] - level
            product = error * level
            rows = slice(slot * ROWS, (slot + 1) * ROWS)
            for half in range(frame // LANES):
                part = slice(half * LANES, (half + 1) * LANES)
                for kind, (weight, value) in enumerate(
                    ((cover, error), (lifted, error), (cover, product), (lifted, product))
                ):
                    term = weight * value[:, part]
                    sums[kind, half, rows, :] = term[:ROWS] + term[ROWS:]
    used = slot_lines[3] >= 0.0
    by_slot = jnp.zeros((ROWS, slots), jnp.float32)
    for kind, wanted in enumerate(GRADIENT_ROWS):
        halves = []
        for half in range(frame // LANES):
            value = sums[kind, half, pl.ds(0, slots, stride=ROWS), :]
            for r in range(1, ROWS):
                value += sums[kind, half, pl.ds(r, slots, stride=ROWS), :]
            columns = slot_cover[:, half * LANES : (half + 1) * LANES]
            halves.append(jnp.where(used, value * columns, 0.0))
        by_slot += exact_dot(feature_rows(frame, wanted), jnp.concatenate(halves, axis=1))
    places = jnp.concatenate(
        [
            (slot_lines[3] == spots_along((slots, LANES), 1, p)).astype(jnp.float32)
            for p in range(0, lanes, LANES)
        ],
        axis=1,
    )
    total = base[...] + lax.dot_general(
        by_slot,
        places,
        (((1,), (0,)), ((), ())),
        precision=lax.Precision.HIGHEST,
        preferred_element_type=jnp.float32,
    )
    payload[...] = jnp.broadcast_to(total[None], payload.shape)
    written.wait()


def solve_kernel(sizes, received, corrections):
    tiles, bands, frame, source, capacity, devices = sizes
    sec, me = lax.axis_index("sec"), lax.axis_index("tile")
    sections = lax.axis_size("sec")
    all_tiles = tiles * devices
    lanes = sections * all_tiles
    lane = lax.broadcasted_iota(jnp.int32, (ROWS, lanes), 1)
    within = lane % all_tiles
    area = frame * frame

    gradients = jnp.zeros((ROWS, lanes), jnp.float32)
    moments = [jnp.zeros((ROWS, lanes), jnp.float32) for _ in range(3)]
    for s in range(sections):
        own = received[s * devices]
        for t in range(1, devices):
            own += received[s * devices + t]
        here = lane // all_tiles == s
        gradients = jnp.where(here, own, gradients)
        for power in range(3):
            shift = ((sections - 1 - power) * all_tiles) % lanes
            moved = pltpu.roll(own, shift, 1) if shift else own
            moments[power] = jnp.where(here, moved, moments[power])
    gradients = gradients * (1.0 / area)
    moments = [m * (1.0 / area) for m in moments]

    where = ((0, 1, 2), (1, 3, 4), (2, 4, 5))
    row = lax.broadcasted_iota(jnp.int32, (ROWS, lanes), 0)

    def entry(f, g):
        kind = moments[(f >= 3) + (g >= 3)]
        index = where[f % 3][g % 3]
        return kind[index : index + 1]

    def stacked(rows):
        result = jnp.zeros((ROWS, lanes), jnp.float32)
        for f, value in enumerate(rows):
            result = jnp.where(row == f, value, result)
        return result

    normal = [stacked([entry(f, g) for f in range(6)]) for g in range(6)]
    diagonal = stacked([entry(f, f) for f in range(6)])
    precond = 1.0 / (diagonal + 4.0 * COUPLING)

    def total(values):
        return jnp.sum(jnp.sum(values, axis=1, keepdims=True), axis=0, keepdims=True)

    def operator(vector):
        beside = jnp.where(within < all_tiles - 1, pltpu.roll(vector, lanes - 1, 1), 0.0)
        beside += jnp.where(within > 0, pltpu.roll(vector, 1, 1), 0.0)
        upward = pltpu.roll(vector, lanes - all_tiles, 1)
        beside += jnp.where(lane < lanes - all_tiles, upward, 0.0)
        beside += jnp.where(lane >= all_tiles, pltpu.roll(vector, all_tiles, 1), 0.0)
        image = COUPLING * (4.0 * vector - beside)
        for g in range(6):
            image += normal[g] * vector[g : g + 1]
        return image

    answer = jnp.zeros((ROWS, lanes), jnp.float32)
    residual = gradients
    scaled = precond * residual
    direction = scaled
    current = total(residual * scaled)
    for step in range(ITERS):
        image = operator(direction)
        alpha = current / total(direction * image)
        answer = answer + alpha * direction
        if step + 1 < ITERS:
            residual = residual - alpha * image
            scaled = precond * residual
            following = total(residual * scaled)
            direction = scaled + following / current * direction
            current = following

    first = sec * all_tiles + me * tiles
    chosen = lax.broadcasted_iota(jnp.int32, (ROWS, lanes), 0) + first == lane
    own = exact_dot(chosen.astype(jnp.float32), answer)
    corrections[...] = own[:tiles, :6]


def shards(patches, zoom, frac, offset, owner, top_grid):
    _, tiles, source, _ = patches.shape
    frame = top_grid.shape[1]
    devices, sections = lax.axis_size("tile"), lax.axis_size("sec")
    bands = frame // BAND
    capacity = max(2, 2 * tiles * bands // devices)
    slots = devices * capacity
    all_tiles = tiles * devices
    lanes = sections * all_tiles
    sizes = (tiles, bands, frame, source, capacity, devices)
    place = (zoom[0], frac[0], offset[0])
    routes = jnp.transpose(owner, (0, 2, 3, 1))[0]

    rows = tiles * bands
    block = jax.ShapeDtypeStruct((capacity, BAND, frame), jnp.bfloat16)
    frames, *outgoing = pl.pallas_call(
        functools.partial(render_kernel, sizes),
        name="render",
        in_specs=[HBM] * 5,
        out_specs=[VMEM] * (1 + devices),
        out_shape=[jax.ShapeDtypeStruct((rows, BAND, frame), jnp.bfloat16)] + [block] * devices,
        scratch_shapes=[
            pltpu.SMEM(place[0].shape, jnp.float32),
            pltpu.SMEM(place[1].shape, jnp.float32),
            pltpu.SMEM(place[2].shape, jnp.int32),
            pltpu.SMEM(routes.shape, jnp.int32),
            pltpu.VMEM((tiles, source, source), jnp.bfloat16),
            pltpu.SMEM((devices,), jnp.int32),
            pltpu.SMEM((slots,), jnp.int32),
            pltpu.SemaphoreType.DMA((4,)),
            pltpu.SemaphoreType.DMA((tiles,)),
        ],
        compiler_params=params(24),
        cost_estimate=cost(800_000_000, 4 << 20),
    )(*(pltpu.with_memory_space_constraint(x, pltpu.HBM) for x in (*place, routes, patches[0])))

    incoming = [outgoing[0]] + [None] * (devices - 1)
    for distance in sorted(range(1, devices), key=lambda d: (-(d.bit_length()), d)):
        incoming[distance] = lax.ppermute(
            outgoing[distance], "tile", [(i, i ^ distance) for i in range(devices)]
        )

    base, cover_sum, slot_cover, slot_lines, slot_bands = pl.pallas_call(
        functools.partial(moment_kernel, sizes),
        name="moments",
        in_specs=[SMEM] * 4 + [VMEM],
        out_specs=[VMEM, VMEM, VMEM, VMEM, SMEM],
        out_shape=[
            jax.ShapeDtypeStruct((ROWS, lanes), jnp.float32),
            jax.ShapeDtypeStruct((bands, BAND, frame), jnp.float32),
            jax.ShapeDtypeStruct((slots, frame), jnp.float32),
            jax.ShapeDtypeStruct((4, slots, LANES), jnp.float32),
            jax.ShapeDtypeStruct((slots,), jnp.int32),
        ],
        scratch_shapes=[
            pltpu.SMEM((slots + 1,), jnp.int32),
            pltpu.VMEM((all_tiles, frame), jnp.float32),
            pltpu.VMEM((3, lanes, frame), jnp.float32),
        ],
        compiler_params=params(24),
        cost_estimate=cost(20_000_000, 1 << 20),
    )(*place, routes, frames)

    grid = pl.pallas_call(
        functools.partial(blend_kernel, sizes),
        name="blend",
        in_specs=[SMEM] + [VMEM] * (1 + devices),
        out_specs=VMEM,
        out_shape=jax.ShapeDtypeStruct((bands, BAND, frame), jnp.bfloat16),
        scratch_shapes=[pltpu.VMEM((bands + 1, BAND, frame), jnp.float32)],
        compiler_params=params(24),
        cost_estimate=cost(1_000_000, 2 << 20),
    )(slot_bands, cover_sum, *incoming)

    from_next = lax.ppermute(grid, "sec", [(i, (i - 1) % sections) for i in range(sections)])

    payload, grid_out = pl.pallas_call(
        functools.partial(gradient_kernel, sizes),
        name="gradient",
        in_specs=[SMEM] + [VMEM] * (6 + devices),
        out_specs=[VMEM, HBM],
        out_shape=[
            jax.ShapeDtypeStruct((sections * devices, ROWS, lanes), jnp.float32),
            jax.ShapeDtypeStruct((bands, BAND, frame), jnp.bfloat16),
        ],
        scratch_shapes=[
            pltpu.VMEM((bands + 1, BAND, frame), jnp.float32),
            pltpu.VMEM((4, frame // LANES, slots * ROWS, LANES), jnp.float32),
            pltpu.SemaphoreType.DMA,
        ],
        compiler_params=params(24),
        cost_estimate=cost(8_000_000, 2 << 20),
    )(
        slot_bands,
        from_next,
        top_grid.reshape(bands, BAND, frame),
        slot_cover,
        slot_lines,
        base,
        grid,
        *incoming,
    )

    received = lax.all_to_all(
        payload, ("sec", "tile"), split_axis=0, concat_axis=0, tiled=True
    )

    corrections = pl.pallas_call(
        functools.partial(solve_kernel, sizes),
        name="solve",
        in_specs=[VMEM],
        out_specs=VMEM,
        out_shape=jax.ShapeDtypeStruct((tiles, 6), jnp.float32),
        compiler_params=params(24),
        cost_estimate=cost(100_000, 1 << 18),
    )(received)
    return (
        grid_out.reshape(1, 1, frame, frame),
        jnp.transpose(corrections[None], (2, 0, 1)),
    )


def solution(mesh):
    placed = (
        P("sec", "tile", None, None),
        P("sec", None, None),
        P("sec", None, None),
        P("sec", None, None),
        P("sec", None, None, None),
        P("tile", None, None),
    )
    return jax.shard_map(
        shards,
        mesh=mesh,
        in_specs=placed,
        out_specs=(P("sec", "tile", None, None), P(None, "sec", "tile")),
        check_vma=False,
    )
```

```python
import functools
import math

import jax
import jax.numpy as jnp
from jax import lax
from jax.experimental import pallas as pl
from jax.experimental.pallas import tpu as pltpu
from jax.sharding import PartitionSpec as P

BAND = 16
ITERS = 2
COUPLING = 0.25
LANES = 128
ROWS = 8
HBM = pl.BlockSpec(memory_space=pltpu.HBM)
SMEM = pl.BlockSpec(memory_space=pltpu.SMEM)
VMEM = pl.BlockSpec(memory_space=pltpu.VMEM)


def params(mebibytes):
    return pltpu.CompilerParams(vmem_limit_bytes=mebibytes * 1024 * 1024)


def cost(flops, size):
    return pl.CostEstimate(flops=flops, bytes_accessed=size, transcendentals=0)


def exact_dot(left, right):
    return lax.dot_general(
        left,
        right,
        (((1,), (1,)), ((), ())),
        precision=lax.Precision.HIGHEST,
        preferred_element_type=jnp.float32,
    )


def points_of(spots, zoom, frac, offset, axis, tile, ratio):
    scale = zoom[axis, tile] * ratio
    return (spots - offset[axis, tile].astype(jnp.float32) - frac[axis, tile]) / scale


def cover_of(points, source):
    return jnp.clip(jnp.minimum(points + 1.0, source - points), 0.0, 1.0)


def hat_weight(distance):
    return jnp.maximum(0.0, 1.0 - jnp.abs(distance))


def spots_along(shape, dim, start=0):
    return (lax.broadcasted_iota(jnp.int32, shape, dim) + start).astype(jnp.float32)


def coords(spots, frame):
    return (spots - (frame - 1) / 2.0) / (frame / 2.0)


def exchange_plan(devices):
    if devices == 8:
        outgoing = [[0], [2, 3], [4], [5], [6], [7], [1]]
        return outgoing, [(0, 0), (1, 2), (2, 4), (3, 5), (4, 6), (5, 7), (6, 1), (7, 3)]
    return [[d] for d in range(devices)], [(d, d) for d in range(devices)]


def render_kernel(
    sizes, zoom_in, frac_in, offset_in, owner_in, patches_in, frames, *outgoing_and_scratch
):
    tiles, bands, frame, source, capacity, devices = sizes
    plan, _ = exchange_plan(devices)
    outgoing = outgoing_and_scratch[: len(plan)]
    zoom, frac, offset, owner, patches, named, rows, small_sems, patch_sems = (
        outgoing_and_scratch[len(plan) :]
    )
    me = lax.axis_index("tile")
    first = me * tiles
    ratio = frame / source
    fetched = [
        pltpu.make_async_copy(patches_in.at[j], patches.at[j], patch_sems.at[j])
        for j in range(tiles)
    ]
    small = [
        pltpu.make_async_copy(there, here, small_sems.at[k])
        for k, (there, here) in enumerate(
            ((zoom_in, zoom), (frac_in, frac), (offset_in, offset), (owner_in, owner))
        )
    ]
    for copy in small + fetched:
        copy.start()
    for g in range(devices):
        named[g] = 0
    for slot in range(devices * capacity):
        rows[slot] = 0
    for copy in small:
        copy.wait()
    for j in range(tiles):
        tile = first + j
        row_points = points_of(spots_along((frame, LANES), 0), zoom, frac, offset, 0, tile, ratio)
        row_weights = jnp.concatenate(
            [
                hat_weight(row_points - spots_along((frame, LANES), 1, p)).astype(jnp.bfloat16)
                for p in range(0, source, LANES)
            ],
            axis=1,
        )
        col_points = points_of(spots_along((ROWS, frame), 1), zoom, frac, offset, 1, tile, ratio)
        col_points = jnp.broadcast_to(col_points[:1], (source, frame))
        col_weights = hat_weight(col_points - spots_along((source, frame), 0)).astype(jnp.bfloat16)
        fetched[j].wait()
        half, quarter = source // 2, frame // 4
        upper = jnp.dot(
            row_weights[: 3 * quarter, :half],
            patches[j, :half],
            preferred_element_type=jnp.float32,
        )
        lower = jnp.dot(
            row_weights[quarter:, half:],
            patches[j, half:],
            preferred_element_type=jnp.float32,
        )
        halfway = jnp.concatenate(
            [upper[:quarter], upper[quarter:] + lower[: 2 * quarter], lower[2 * quarter :]]
        )
        rendered = jnp.dot(
            halfway.astype(jnp.bfloat16), col_weights, preferred_element_type=jnp.float32
        ).astype(jnp.bfloat16)
        frames[j * bands : (j + 1) * bands] = rendered.reshape(bands, BAND, frame)
        for band in range(bands):
            target = owner[band, 0, tile]
            slot = named[target]
            named[target] = slot + 1
            rows[target * capacity + slot] = j * bands + band
    for there, group in zip(outgoing, plan):
        for position, distance in enumerate(group):
            target = me ^ distance
            for slot in range(capacity):
                there[position * capacity + slot] = frames[rows[target * capacity + slot]]


def feature_rows(frame, wanted):
    shape = (ROWS, frame)
    x = coords(spots_along(shape, 1), frame)
    row = lax.broadcasted_iota(jnp.int32, shape, 0)
    rows = jnp.zeros(shape, jnp.float32)
    for r, power in wanted.items():
        rows = jnp.where(row == r, (jnp.ones_like(x), x, x * x)[power], rows)
    return rows


MOMENT_ROWS = ({0: 0, 1: 1, 3: 2}, {2: 0, 4: 1}, {5: 0})


def scan_kernel(sizes, owner, codes):
    tiles, bands, frame, source, capacity, devices = sizes
    me = lax.axis_index("tile")

    def scan(block, distance):
        count = 0
        for j in range(tiles):
            tile = (me ^ distance) * tiles + j
            named = [owner[band, 0, tile] for band in range(bands)]
            for band in range(bands):
                codes[block * capacity + count] = tile * bands + band
                count += (named[band] == me).astype(jnp.int32)

        def blank(position, carry):
            codes[block * capacity + position] = -1
            return carry

        lax.fori_loop(count, capacity, blank, 0)

    arriving = exchange_plan(devices)[1]
    if devices == 8:
        for block, (_, distance) in enumerate(arriving):
            scan(block, distance)
    else:
        pl.loop(0, devices)(lambda block: scan(block, block))


def slot_kernel(
    sizes, zoom, frac, offset, codes, cover_sum, col_cover, slot_lines, slot_bands
):
    tiles, bands, frame, source, capacity, devices = sizes
    slots = devices * capacity
    all_tiles = tiles * devices
    ratio = frame / source

    @pl.loop(0, all_tiles // ROWS)
    def _(group):
        for k in range(ROWS):
            tile = group * ROWS + k
            points = points_of(spots_along((1, frame), 1), zoom, frac, offset, 1, tile, ratio)
            col_cover[pl.ds(tile, 1), :] = cover_of(points, source)

    cover_sum[...] = jnp.zeros_like(cover_sum)
    unroll = math.gcd(slots, ROWS)

    @pl.loop(0, slots // unroll)
    def _(group):
        for k in range(unroll):
            slot = group * unroll + k
            used = codes[slot] >= 0
            code = jnp.maximum(codes[slot], 0)
            tile, band = code // bands, code % bands
            before = jnp.maximum(codes[jnp.maximum(slot - 1, 0)], 0) // bands
            place = jnp.where(used, band, bands)
            slot_bands[0, slot] = place
            slot_bands[1, slot] = jnp.where(used, tile, all_tiles)
            slot_bands[2, slot] = (used & (before == tile)).astype(jnp.int32)
            here = pl.ds(slot, 1)
            row = jnp.zeros((1, LANES), jnp.float32)
            start = row + (band * BAND).astype(jnp.float32)
            shift = row + (offset[0, tile].astype(jnp.float32) + frac[0, tile])
            inverse = 1.0 / (row + zoom[0, tile] * ratio)
            slope = jnp.broadcast_to(inverse, (BAND, LANES))
            first = (start - shift) * inverse
            slot_lines[0, here, :] = inverse
            slot_lines[1, here, :] = first
            slot_lines[2, here, :] = coords(start, frame)
            cover = cover_of(spots_along((BAND, LANES), 0) * slope + first, source)
            columns = col_cover[pl.ds(tile, 1), :]
            for half in range(frame // LANES):
                part = slice(half * LANES, (half + 1) * LANES)
                cover_sum[place, :, part] += cover * columns[:, part]


def moment_kernel(sizes, zoom, frac, offset, frames, base, parts):
    tiles, bands, frame, source, capacity, devices = sizes
    me = lax.axis_index("tile")
    sec = lax.axis_index("sec")
    sections = lax.axis_size("sec")
    all_tiles = tiles * devices
    ratio = frame / source
    parts[...] = jnp.zeros_like(parts)
    for j in range(tiles):
        tile = me * tiles + j
        spots = spots_along((frame, frame), 0)
        y = coords(spots, frame)
        cover = cover_of(points_of(spots, zoom, frac, offset, 0, tile, ratio), source)
        level = frames[j * bands : (j + 1) * bands].reshape(frame, frame).astype(jnp.float32)
        columns = points_of(spots_along((1, frame), 1), zoom, frac, offset, 1, tile, ratio)
        columns = cover_of(columns, source)
        weighted = (cover, cover * y, cover * y * y)
        for power, image in enumerate((None, level, level * level)):
            block = (sec + 1 + power) % sections
            place = block * all_tiles + tile
            for a, rows in enumerate(weighted):
                total = rows if image is None else rows * image
                parts[a, pl.ds(place, 1), :] = columns * jnp.sum(total, axis=0, keepdims=True)
    total = exact_dot(feature_rows(frame, MOMENT_ROWS[0]), parts[0])
    for a in (1, 2):
        total += exact_dot(feature_rows(frame, MOMENT_ROWS[a]), parts[a])
    base[...] = total


def blend_kernel(sizes, slot_bands, cover_sum, *blocks_and_rest):
    tiles, bands, frame, source, capacity, devices = sizes
    *blocks, grid, total = blocks_and_rest
    total[...] = jnp.zeros_like(total)
    for block, (array, _) in enumerate(exchange_plan(devices)[1]):
        for k in range(capacity):
            level = blocks[array][k].astype(jnp.float32)
            total[slot_bands[0, block * capacity + k]] += level
    grid[...] = (total[:bands] / (1.0 + cover_sum[:bands])).astype(jnp.bfloat16)


GRADIENT_ROWS = ({0: 0, 1: 1}, {2: 0}, {3: 0, 4: 1}, {5: 0})


def gradient_kernel(
    sizes, slot_bands, from_next, top_grid, col_cover, slot_lines, base, grid, *blocks_and_rest
):
    tiles, bands, frame, source, capacity, devices = sizes
    *blocks, payload, grid_out, above, sums, grid_sem = blocks_and_rest
    written = pltpu.make_async_copy(grid, grid_out, grid_sem)
    written.start()
    sec = lax.axis_index("sec")
    all_tiles = tiles * devices
    lanes = base.shape[1]

    @pl.when(sec == lax.axis_size("sec") - 1)
    def _():
        above[:bands] = top_grid[...].astype(jnp.float32)

    @pl.when(sec != lax.axis_size("sec") - 1)
    def _():
        above[:bands] = from_next[...].astype(jnp.float32)

    above[bands] = jnp.zeros((BAND, frame), jnp.float32)
    sums[...] = jnp.zeros_like(sums)
    spots = spots_along((BAND, LANES), 0)
    raised = spots * (2.0 / frame)
    halves = range(frame // LANES)

    for block, (array, _) in enumerate(exchange_plan(devices)[1]):
        running = None
        for k in range(capacity):
            slot = block * capacity + k
            here = slice(slot, slot + 1)
            points = spots * slot_lines[0, here] + slot_lines[1, here]
            cover = cover_of(points, source)
            lifted = cover * (raised + slot_lines[2, here])
            level = blocks[array][k].astype(jnp.float32)
            error = above[slot_bands[0, slot]] - level
            product = error * level
            terms = []
            for half in halves:
                part = slice(half * LANES, (half + 1) * LANES)
                for weight, value in (
                    (cover, error),
                    (lifted, error),
                    (cover, product),
                    (lifted, product),
                ):
                    term = weight * value[:, part]
                    terms.append(term[:ROWS] + term[ROWS:])
            if running is not None:
                same = slot_bands[2, slot] == 1
                terms = [
                    term + jnp.where(same, before, 0.0) for term, before in zip(terms, running)
                ]
            running = terms
            rows = pl.ds(pl.multiple_of(slot_bands[1, slot] * ROWS, ROWS), ROWS)
            for index, term in enumerate(terms):
                sums[index, rows, :] = term

    values = [jnp.zeros((all_tiles, 1), jnp.float32)] * 6
    for half in halves:
        columns = col_cover[:, half * LANES : (half + 1) * LANES]
        x = coords(spots_along((all_tiles, LANES), 1, half * LANES), frame)
        for kind, wanted in enumerate(GRADIENT_ROWS):
            index = half * len(GRADIENT_ROWS) + kind
            value = sums[index, pl.ds(0, all_tiles, stride=ROWS), :]
            for r in range(1, ROWS):
                value += sums[index, pl.ds(r, all_tiles, stride=ROWS), :]
            value = value * columns
            for row, power in wanted.items():
                term = value * x if power else value
                values[row] += jnp.sum(term, axis=1, keepdims=True)
    total = []
    tile = lax.broadcasted_iota(jnp.int32, (all_tiles, LANES), 0) + sec * all_tiles
    for first in range(0, lanes, LANES):
        lane = lax.broadcasted_iota(jnp.int32, (all_tiles, LANES), 1) + first
        places = (tile == lane).astype(jnp.float32)
        rows = [jnp.sum(places * value, axis=0, keepdims=True) for value in values]
        total.append(jnp.concatenate(rows + [jnp.zeros_like(rows[0])] * (ROWS - 6), axis=0))
    total = base[...] + jnp.concatenate(total, axis=1)
    payload[...] = jnp.broadcast_to(total[None], payload.shape)
    written.wait()


def solve_kernel(sizes, received, corrections):
    tiles, bands, frame, source, capacity, devices = sizes
    sec, me = lax.axis_index("sec"), lax.axis_index("tile")
    sections = lax.axis_size("sec")
    all_tiles = tiles * devices
    lanes = sections * all_tiles
    lane = lax.broadcasted_iota(jnp.int32, (ROWS, lanes), 1)
    within = lane % all_tiles
    area = frame * frame

    gradients = jnp.zeros((ROWS, lanes), jnp.float32)
    moments = [jnp.zeros((ROWS, lanes), jnp.float32) for _ in range(3)]
    for s in range(sections):
        own = received[s * devices]
        for t in range(1, devices):
            own += received[s * devices + t]
        here = lane // all_tiles == s
        gradients = jnp.where(here, own, gradients)
        for power in range(3):
            shift = ((sections - 1 - power) * all_tiles) % lanes
            moved = pltpu.roll(own, shift, 1) if shift else own
            moments[power] = jnp.where(here, moved, moments[power])
    gradients = gradients * (1.0 / area)
    moments = [m * (1.0 / area) for m in moments]

    where = ((0, 1, 2), (1, 3, 4), (2, 4, 5))
    row = lax.broadcasted_iota(jnp.int32, (ROWS, lanes), 0)

    def entry(f, g):
        kind = moments[(f >= 3) + (g >= 3)]
        index = where[f % 3][g % 3]
        return kind[index : index + 1]

    def stacked(rows):
        result = jnp.zeros((ROWS, lanes), jnp.float32)
        for f, value in enumerate(rows):
            result = jnp.where(row == f, value, result)
        return result

    normal = [stacked([entry(f, g) for f in range(6)]) for g in range(6)]
    diagonal = stacked([entry(f, f) for f in range(6)])
    precond = 1.0 / (diagonal + 4.0 * COUPLING)

    def total(values):
        return jnp.sum(jnp.sum(values, axis=1, keepdims=True), axis=0, keepdims=True)

    def operator(vector):
        beside = jnp.where(within < all_tiles - 1, pltpu.roll(vector, lanes - 1, 1), 0.0)
        beside += jnp.where(within > 0, pltpu.roll(vector, 1, 1), 0.0)
        upward = pltpu.roll(vector, lanes - all_tiles, 1)
        beside += jnp.where(lane < lanes - all_tiles, upward, 0.0)
        beside += jnp.where(lane >= all_tiles, pltpu.roll(vector, all_tiles, 1), 0.0)
        image = COUPLING * (4.0 * vector - beside)
        for g in range(6):
            image += normal[g] * vector[g : g + 1]
        return image

    answer = jnp.zeros((ROWS, lanes), jnp.float32)
    residual = gradients
    scaled = precond * residual
    direction = scaled
    current = total(residual * scaled)
    for step in range(ITERS):
        image = operator(direction)
        alpha = current / total(direction * image)
        answer = answer + alpha * direction
        if step + 1 < ITERS:
            residual = residual - alpha * image
            scaled = precond * residual
            following = total(residual * scaled)
            direction = scaled + following / current * direction
            current = following

    first = sec * all_tiles + me * tiles
    chosen = (row + first == lane).astype(jnp.float32)
    place = lax.broadcasted_iota(jnp.int32, (ROWS, LANES), 1)
    own = jnp.zeros((ROWS, LANES), jnp.float32)
    for f in range(6):
        value = jnp.sum(chosen * answer[f : f + 1], axis=1, keepdims=True)
        own = jnp.where(place == f, value, own)
    corrections[...] = own[:tiles, :6]


def shards(patches, zoom, frac, offset, owner, top_grid):
    _, tiles, source, _ = patches.shape
    frame = top_grid.shape[1]
    devices, sections = lax.axis_size("tile"), lax.axis_size("sec")
    bands = frame // BAND
    capacity = max(2, 2 * tiles * bands // devices)
    slots = devices * capacity
    all_tiles = tiles * devices
    lanes = sections * all_tiles
    sizes = (tiles, bands, frame, source, capacity, devices)
    place = (zoom[0], frac[0], offset[0])
    routes = jnp.transpose(owner, (0, 2, 3, 1))[0]

    rows = tiles * bands
    plan, arriving = exchange_plan(devices)
    blocks = [
        jax.ShapeDtypeStruct((len(group) * capacity, BAND, frame), jnp.bfloat16)
        for group in plan
    ]
    frames, *outgoing = pl.pallas_call(
        functools.partial(render_kernel, sizes),
        name="render",
        in_specs=[HBM] * 5,
        out_specs=[VMEM] * (1 + len(plan)),
        out_shape=[jax.ShapeDtypeStruct((rows, BAND, frame), jnp.bfloat16)] + blocks,
        scratch_shapes=[
            pltpu.SMEM(place[0].shape, jnp.float32),
            pltpu.SMEM(place[1].shape, jnp.float32),
            pltpu.SMEM(place[2].shape, jnp.int32),
            pltpu.SMEM(routes.shape, jnp.int32),
            pltpu.VMEM((tiles, source, source), jnp.bfloat16),
            pltpu.SMEM((devices,), jnp.int32),
            pltpu.SMEM((slots,), jnp.int32),
            pltpu.SemaphoreType.DMA((4,)),
            pltpu.SemaphoreType.DMA((tiles,)),
        ],
        compiler_params=params(24),
        cost_estimate=cost(800_000_000, 4 << 20),
    )(*(pltpu.with_memory_space_constraint(x, pltpu.HBM) for x in (*place, routes, patches[0])))

    base = pl.pallas_call(
        functools.partial(moment_kernel, sizes),
        name="moments",
        in_specs=[SMEM] * 3 + [VMEM],
        out_specs=VMEM,
        out_shape=jax.ShapeDtypeStruct((ROWS, lanes), jnp.float32),
        scratch_shapes=[pltpu.VMEM((3, lanes, frame), jnp.float32)],
        compiler_params=params(24),
        cost_estimate=cost(20_000_000, 1 << 20),
    )(*place, frames)

    codes = pl.pallas_call(
        functools.partial(scan_kernel, sizes),
        name="scan",
        in_specs=[SMEM],
        out_specs=SMEM,
        out_shape=jax.ShapeDtypeStruct((slots + 1,), jnp.int32),
        compiler_params=params(24),
        cost_estimate=cost(20_000_000, 1 << 20),
    )(routes)

    cover_sum, col_cover, slot_lines, slot_bands = pl.pallas_call(
        functools.partial(slot_kernel, sizes),
        name="slots",
        in_specs=[SMEM] * 4,
        out_specs=[VMEM] * 3 + [SMEM],
        out_shape=[
            jax.ShapeDtypeStruct((bands + 1, BAND, frame), jnp.float32),
            jax.ShapeDtypeStruct((all_tiles, frame), jnp.float32),
            jax.ShapeDtypeStruct((3, slots, LANES), jnp.float32),
            jax.ShapeDtypeStruct((3, slots), jnp.int32),
        ],
        compiler_params=params(24),
        cost_estimate=cost(20_000_000, 1 << 20),
    )(*place, codes)

    def swapped(block, distance):
        return lax.ppermute(block, "tile", [(i, i ^ distance) for i in range(devices)])

    incoming = [outgoing[0]]
    for block, group in zip(outgoing[1:], plan[1:]):
        incoming.append(swapped(block, group[0]))
        if len(group) == 2:
            passed_on = incoming[-1][capacity:]
    if devices == 8:
        incoming.append(swapped(passed_on, 1))

    grid = pl.pallas_call(
        functools.partial(blend_kernel, sizes),
        name="blend",
        in_specs=[SMEM] + [VMEM] * (1 + len(incoming)),
        out_specs=VMEM,
        out_shape=jax.ShapeDtypeStruct((bands, BAND, frame), jnp.bfloat16),
        scratch_shapes=[pltpu.VMEM((bands + 1, BAND, frame), jnp.float32)],
        compiler_params=params(24),
        cost_estimate=cost(1_000_000, 2 << 20),
    )(slot_bands, cover_sum, *incoming)

    from_next = lax.ppermute(grid, "sec", [(i, (i - 1) % sections) for i in range(sections)])

    payload, grid_out = pl.pallas_call(
        functools.partial(gradient_kernel, sizes),
        name="gradient",
        in_specs=[SMEM] + [VMEM] * (6 + len(incoming)),
        out_specs=[VMEM, HBM],
        out_shape=[
            jax.ShapeDtypeStruct((sections * devices, ROWS, lanes), jnp.float32),
            jax.ShapeDtypeStruct((bands, BAND, frame), jnp.bfloat16),
        ],
        scratch_shapes=[
            pltpu.VMEM((bands + 1, BAND, frame), jnp.float32),
            pltpu.VMEM((4 * frame // LANES, (all_tiles + 1) * ROWS, LANES), jnp.float32),
            pltpu.SemaphoreType.DMA,
        ],
        compiler_params=params(24),
        cost_estimate=cost(8_000_000, 2 << 20),
    )(
        slot_bands,
        from_next,
        top_grid.reshape(bands, BAND, frame),
        col_cover,
        slot_lines,
        base,
        grid,
        *incoming,
    )

    received = lax.all_to_all(
        payload, ("sec", "tile"), split_axis=0, concat_axis=0, tiled=True
    )

    corrections = pl.pallas_call(
        functools.partial(solve_kernel, sizes),
        name="solve",
        in_specs=[VMEM],
        out_specs=VMEM,
        out_shape=jax.ShapeDtypeStruct((tiles, 6), jnp.float32),
        compiler_params=params(24),
        cost_estimate=cost(100_000, 1 << 18),
    )(received)
    return (
        grid_out.reshape(1, 1, frame, frame),
        jnp.transpose(corrections[None], (2, 0, 1)),
    )


def solution(mesh):
    placed = (
        P("sec", "tile", None, None),
        P("sec", None, None),
        P("sec", None, None),
        P("sec", None, None),
        P("sec", None, None, None),
        P("tile", None, None),
    )
    return jax.shard_map(
        shards,
        mesh=mesh,
        in_specs=placed,
        out_specs=(P("sec", "tile", None, None), P(None, "sec", "tile")),
        check_vma=False,
    )
```

```python
import functools
import math

import jax
import jax.numpy as jnp
from jax import lax
from jax.experimental import pallas as pl
from jax.experimental.pallas import tpu as pltpu
from jax.sharding import PartitionSpec as P

BAND = 16
ITERS = 2
COUPLING = 0.25
LANES = 128
ROWS = 8
HBM = pl.BlockSpec(memory_space=pltpu.HBM)
SMEM = pl.BlockSpec(memory_space=pltpu.SMEM)
VMEM = pl.BlockSpec(memory_space=pltpu.VMEM)


def params(mebibytes):
    return pltpu.CompilerParams(vmem_limit_bytes=mebibytes * 1024 * 1024)


def cost(flops, size):
    return pl.CostEstimate(flops=flops, bytes_accessed=size, transcendentals=0)


def exact_dot(left, right):
    return lax.dot_general(
        left,
        right,
        (((1,), (1,)), ((), ())),
        precision=lax.Precision.HIGHEST,
        preferred_element_type=jnp.float32,
    )


def points_of(spots, zoom, frac, offset, axis, tile, ratio):
    scale = zoom[axis, tile] * ratio
    return (spots - offset[axis, tile].astype(jnp.float32) - frac[axis, tile]) / scale


def cover_of(points, source):
    return jnp.clip(jnp.minimum(points + 1.0, source - points), 0.0, 1.0)


def hat_weight(distance):
    return jnp.maximum(0.0, 1.0 - jnp.abs(distance))


def spots_along(shape, dim, start=0):
    return (lax.broadcasted_iota(jnp.int32, shape, dim) + start).astype(jnp.float32)


def coords(spots, frame):
    return (spots - (frame - 1) / 2.0) / (frame / 2.0)


def exchange_plan(devices):
    if devices == 8:
        outgoing = [[0], [2, 3], [4], [5], [6], [7], [1]]
        return outgoing, [(0, 0), (1, 2), (2, 4), (3, 5), (4, 6), (5, 7), (6, 1), (7, 3)]
    return [[d] for d in range(devices)], [(d, d) for d in range(devices)]


def render_kernel(
    sizes, zoom_in, frac_in, offset_in, owner_in, patches_in, frames, *outgoing_and_scratch
):
    tiles, bands, frame, source, capacity, devices = sizes
    plan, _ = exchange_plan(devices)
    outgoing = outgoing_and_scratch[: len(plan)]
    zoom, frac, offset, owner, patches, named, rows, small_sems, patch_sems = (
        outgoing_and_scratch[len(plan) :]
    )
    me = lax.axis_index("tile")
    first = me * tiles
    ratio = frame / source
    fetched = [
        pltpu.make_async_copy(patches_in.at[j], patches.at[j], patch_sems.at[j])
        for j in range(tiles)
    ]
    small = [
        pltpu.make_async_copy(there, here, small_sems.at[k])
        for k, (there, here) in enumerate(
            ((zoom_in, zoom), (frac_in, frac), (offset_in, offset), (owner_in, owner))
        )
    ]
    for copy in small + fetched:
        copy.start()
    for g in range(devices):
        named[g] = 0
    for slot in range(devices * capacity):
        rows[slot] = 0
    for copy in small:
        copy.wait()
    for j in range(tiles):
        tile = first + j
        row_points = points_of(spots_along((frame, LANES), 0), zoom, frac, offset, 0, tile, ratio)
        row_weights = jnp.concatenate(
            [
                hat_weight(row_points - spots_along((frame, LANES), 1, p)).astype(jnp.bfloat16)
                for p in range(0, source, LANES)
            ],
            axis=1,
        )
        col_points = points_of(spots_along((ROWS, frame), 1), zoom, frac, offset, 1, tile, ratio)
        col_points = jnp.broadcast_to(col_points[:1], (source, frame))
        col_weights = hat_weight(col_points - spots_along((source, frame), 0)).astype(jnp.bfloat16)
        fetched[j].wait()
        half, quarter = source // 2, frame // 4
        upper = jnp.dot(
            row_weights[: 3 * quarter, :half],
            patches[j, :half],
            preferred_element_type=jnp.float32,
        )
        lower = jnp.dot(
            row_weights[quarter:, half:],
            patches[j, half:],
            preferred_element_type=jnp.float32,
        )
        halfway = jnp.concatenate(
            [upper[:quarter], upper[quarter:] + lower[: 2 * quarter], lower[2 * quarter :]]
        )
        rendered = jnp.dot(
            halfway.astype(jnp.bfloat16), col_weights, preferred_element_type=jnp.float32
        ).astype(jnp.bfloat16)
        frames[j * bands : (j + 1) * bands] = rendered.reshape(bands, BAND, frame)
        for band in range(bands):
            target = owner[band, 0, tile]
            slot = named[target]
            named[target] = slot + 1
            rows[target * capacity + slot] = j * bands + band
    for there, group in zip(outgoing, plan):
        for position, distance in enumerate(group):
            target = me ^ distance
            for slot in range(capacity):
                there[position * capacity + slot] = frames[rows[target * capacity + slot]]


def feature_rows(frame, wanted):
    shape = (ROWS, frame)
    x = coords(spots_along(shape, 1), frame)
    row = lax.broadcasted_iota(jnp.int32, shape, 0)
    rows = jnp.zeros(shape, jnp.float32)
    for r, power in wanted.items():
        rows = jnp.where(row == r, (jnp.ones_like(x), x, x * x)[power], rows)
    return rows


MOMENT_ROWS = ({0: 0, 1: 1, 3: 2}, {2: 0, 4: 1}, {5: 0})


def scan_kernel(sizes, owner, codes):
    tiles, bands, frame, source, capacity, devices = sizes
    me = lax.axis_index("tile")

    def scan(block, distance):
        count = 0
        for j in range(tiles):
            tile = (me ^ distance) * tiles + j
            named = [owner[band, 0, tile] for band in range(bands)]
            for band in range(bands):
                codes[block * capacity + count] = tile * bands + band
                count += (named[band] == me).astype(jnp.int32)

        def blank(position, carry):
            codes[block * capacity + position] = -1
            return carry

        lax.fori_loop(count, capacity, blank, 0)

    arriving = exchange_plan(devices)[1]
    if devices == 8:
        for block, (_, distance) in enumerate(arriving):
            scan(block, distance)
    else:
        pl.loop(0, devices)(lambda block: scan(block, block))


def slot_kernel(
    sizes, zoom, frac, offset, codes, cover_sum, col_cover, slot_lines, slot_bands
):
    tiles, bands, frame, source, capacity, devices = sizes
    slots = devices * capacity
    all_tiles = tiles * devices
    ratio = frame / source

    @pl.loop(0, all_tiles // ROWS)
    def _(group):
        for k in range(ROWS):
            tile = group * ROWS + k
            points = points_of(spots_along((1, frame), 1), zoom, frac, offset, 1, tile, ratio)
            col_cover[pl.ds(tile, 1), :] = cover_of(points, source)

    cover_sum[...] = jnp.zeros_like(cover_sum)
    unroll = math.gcd(slots, ROWS)

    @pl.loop(0, slots // unroll)
    def _(group):
        for k in range(unroll):
            slot = group * unroll + k
            used = codes[slot] >= 0
            code = jnp.maximum(codes[slot], 0)
            tile, band = code // bands, code % bands
            before = jnp.maximum(codes[jnp.maximum(slot - 1, 0)], 0) // bands
            place = jnp.where(used, band, bands)
            slot_bands[0, slot] = place
            slot_bands[1, slot] = jnp.where(used, tile, all_tiles)
            slot_bands[2, slot] = (used & (before == tile)).astype(jnp.int32)
            here = pl.ds(slot, 1)
            row = jnp.zeros((1, LANES), jnp.float32)
            start = row + (band * BAND).astype(jnp.float32)
            shift = row + (offset[0, tile].astype(jnp.float32) + frac[0, tile])
            inverse = 1.0 / (row + zoom[0, tile] * ratio)
            slope = jnp.broadcast_to(inverse, (BAND, LANES))
            first = (start - shift) * inverse
            slot_lines[0, here, :] = inverse
            slot_lines[1, here, :] = first
            slot_lines[2, here, :] = coords(start, frame)
            cover = cover_of(spots_along((BAND, LANES), 0) * slope + first, source)
            columns = col_cover[pl.ds(tile, 1), :]
            for half in range(frame // LANES):
                part = slice(half * LANES, (half + 1) * LANES)
                cover_sum[place, :, part] += cover * columns[:, part]


def moment_kernel(sizes, zoom, frac, offset, frames, base, parts):
    tiles, bands, frame, source, capacity, devices = sizes
    me = lax.axis_index("tile")
    sec = lax.axis_index("sec")
    sections = lax.axis_size("sec")
    all_tiles = tiles * devices
    ratio = frame / source
    parts[...] = jnp.zeros_like(parts)
    for j in range(tiles):
        tile = me * tiles + j
        spots = spots_along((frame, frame), 0)
        y = coords(spots, frame)
        cover = cover_of(points_of(spots, zoom, frac, offset, 0, tile, ratio), source)
        level = frames[j * bands : (j + 1) * bands].reshape(frame, frame).astype(jnp.float32)
        columns = points_of(spots_along((1, frame), 1), zoom, frac, offset, 1, tile, ratio)
        columns = cover_of(columns, source)
        weighted = (cover, cover * y, cover * y * y)
        for power, image in enumerate((None, level, level * level)):
            block = (sec + 1 + power) % sections
            place = block * all_tiles + tile
            for a, rows in enumerate(weighted):
                total = rows if image is None else rows * image
                parts[a, pl.ds(place, 1), :] = columns * jnp.sum(total, axis=0, keepdims=True)
    total = exact_dot(feature_rows(frame, MOMENT_ROWS[0]), parts[0])
    for a in (1, 2):
        total += exact_dot(feature_rows(frame, MOMENT_ROWS[a]), parts[a])
    base[...] = total


def blend_kernel(sizes, slot_bands, cover_sum, *blocks_and_rest):
    tiles, bands, frame, source, capacity, devices = sizes
    *blocks, grid, total = blocks_and_rest
    total[...] = jnp.zeros_like(total)
    for block, (array, _) in enumerate(exchange_plan(devices)[1]):
        for k in range(capacity):
            level = blocks[array][k].astype(jnp.float32)
            total[slot_bands[0, block * capacity + k]] += level
    grid[...] = (total[:bands] / (1.0 + cover_sum[:bands])).astype(jnp.bfloat16)


GRADIENT_ROWS = ({0: 0, 1: 1}, {2: 0}, {3: 0, 4: 1}, {5: 0})


def gradient_kernel(
    sizes, slot_bands, from_next, top_grid, col_cover, slot_lines, base, grid, *blocks_and_rest
):
    tiles, bands, frame, source, capacity, devices = sizes
    *blocks, payload, grid_out, above, sums, grid_sem = blocks_and_rest
    written = pltpu.make_async_copy(grid, grid_out, grid_sem)
    written.start()
    sec = lax.axis_index("sec")
    all_tiles = tiles * devices
    lanes = base.shape[1]

    @pl.when(sec == lax.axis_size("sec") - 1)
    def _():
        above[:bands] = top_grid[...].astype(jnp.float32)

    @pl.when(sec != lax.axis_size("sec") - 1)
    def _():
        above[:bands] = from_next[...].astype(jnp.float32)

    above[bands] = jnp.zeros((BAND, frame), jnp.float32)
    sums[...] = jnp.zeros_like(sums)
    spots = spots_along((BAND, LANES), 0)
    raised = spots * (2.0 / frame)
    halves = range(frame // LANES)

    for block, (array, _) in enumerate(exchange_plan(devices)[1]):
        running = None
        for k in range(capacity):
            slot = block * capacity + k
            here = slice(slot, slot + 1)
            points = spots * slot_lines[0, here] + slot_lines[1, here]
            cover = cover_of(points, source)
            lifted = cover * (raised + slot_lines[2, here])
            level = blocks[array][k].astype(jnp.float32)
            error = above[slot_bands[0, slot]] - level
            product = error * level
            terms = []
            for half in halves:
                part = slice(half * LANES, (half + 1) * LANES)
                for weight, value in (
                    (cover, error),
                    (lifted, error),
                    (cover, product),
                    (lifted, product),
                ):
                    term = weight * value[:, part]
                    terms.append(term[:ROWS] + term[ROWS:])
            if running is not None:
                same = slot_bands[2, slot] == 1
                terms = [
                    term + jnp.where(same, before, 0.0) for term, before in zip(terms, running)
                ]
            running = terms
            rows = pl.ds(pl.multiple_of(slot_bands[1, slot] * ROWS, ROWS), ROWS)
            for index, term in enumerate(terms):
                sums[index, rows, :] = term

    values = [jnp.zeros((all_tiles, 1), jnp.float32)] * 6
    for half in halves:
        columns = col_cover[:, half * LANES : (half + 1) * LANES]
        x = coords(spots_along((all_tiles, LANES), 1, half * LANES), frame)
        for kind, wanted in enumerate(GRADIENT_ROWS):
            index = half * len(GRADIENT_ROWS) + kind
            value = sums[index, pl.ds(0, all_tiles, stride=ROWS), :]
            for r in range(1, ROWS):
                value += sums[index, pl.ds(r, all_tiles, stride=ROWS), :]
            value = value * columns
            for row, power in wanted.items():
                term = value * x if power else value
                values[row] += jnp.sum(term, axis=1, keepdims=True)
    total = []
    tile = lax.broadcasted_iota(jnp.int32, (all_tiles, LANES), 0) + sec * all_tiles
    for first in range(0, lanes, LANES):
        lane = lax.broadcasted_iota(jnp.int32, (all_tiles, LANES), 1) + first
        places = (tile == lane).astype(jnp.float32)
        rows = [jnp.sum(places * value, axis=0, keepdims=True) for value in values]
        total.append(jnp.concatenate(rows + [jnp.zeros_like(rows[0])] * (ROWS - 6), axis=0))
    total = base[...] + jnp.concatenate(total, axis=1)
    payload[...] = jnp.broadcast_to(total[None], payload.shape)
    written.wait()


def solve_kernel(sizes, received, corrections):
    tiles, bands, frame, source, capacity, devices = sizes
    sec, me = lax.axis_index("sec"), lax.axis_index("tile")
    sections = lax.axis_size("sec")
    all_tiles = tiles * devices
    lanes = sections * all_tiles
    lane = lax.broadcasted_iota(jnp.int32, (ROWS, lanes), 1)
    within = lane % all_tiles
    area = frame * frame

    gradients = jnp.zeros((ROWS, lanes), jnp.float32)
    moments = [jnp.zeros((ROWS, lanes), jnp.float32) for _ in range(3)]
    for s in range(sections):
        own = received[s * devices]
        for t in range(1, devices):
            own += received[s * devices + t]
        here = lane // all_tiles == s
        gradients = jnp.where(here, own, gradients)
        for power in range(3):
            shift = ((sections - 1 - power) * all_tiles) % lanes
            moved = pltpu.roll(own, shift, 1) if shift else own
            moments[power] = jnp.where(here, moved, moments[power])
    gradients = gradients * (1.0 / area)
    moments = [m * (1.0 / area) for m in moments]

    where = ((0, 1, 2), (1, 3, 4), (2, 4, 5))
    row = lax.broadcasted_iota(jnp.int32, (ROWS, lanes), 0)

    def entry(f, g):
        kind = moments[(f >= 3) + (g >= 3)]
        index = where[f % 3][g % 3]
        return kind[index : index + 1]

    def stacked(rows):
        result = jnp.zeros((ROWS, lanes), jnp.float32)
        for f, value in enumerate(rows):
            result = jnp.where(row == f, value, result)
        return result

    normal = [stacked([entry(f, g) for f in range(6)]) for g in range(6)]
    diagonal = stacked([entry(f, f) for f in range(6)])
    precond = 1.0 / (diagonal + 4.0 * COUPLING)

    def total(values):
        return jnp.sum(jnp.sum(values, axis=1, keepdims=True), axis=0, keepdims=True)

    def operator(vector):
        beside = jnp.where(within < all_tiles - 1, pltpu.roll(vector, lanes - 1, 1), 0.0)
        beside += jnp.where(within > 0, pltpu.roll(vector, 1, 1), 0.0)
        upward = pltpu.roll(vector, lanes - all_tiles, 1)
        beside += jnp.where(lane < lanes - all_tiles, upward, 0.0)
        beside += jnp.where(lane >= all_tiles, pltpu.roll(vector, all_tiles, 1), 0.0)
        image = COUPLING * (4.0 * vector - beside)
        for g in range(6):
            image += normal[g] * vector[g : g + 1]
        return image

    answer = jnp.zeros((ROWS, lanes), jnp.float32)
    residual = gradients
    scaled = precond * residual
    direction = scaled
    current = total(residual * scaled)
    for step in range(ITERS):
        image = operator(direction)
        alpha = current / total(direction * image)
        answer = answer + alpha * direction
        if step + 1 < ITERS:
            residual = residual - alpha * image
            scaled = precond * residual
            following = total(residual * scaled)
            direction = scaled + following / current * direction
            current = following

    first = sec * all_tiles + me * tiles
    chosen = (row + first == lane).astype(jnp.float32)
    place = lax.broadcasted_iota(jnp.int32, (ROWS, LANES), 1)
    own = jnp.zeros((ROWS, LANES), jnp.float32)
    for f in range(6):
        value = jnp.sum(chosen * answer[f : f + 1], axis=1, keepdims=True)
        own = jnp.where(place == f, value, own)
    corrections[...] = own[:tiles, :6]


def shards(patches, zoom, frac, offset, owner, top_grid):
    _, tiles, source, _ = patches.shape
    frame = top_grid.shape[1]
    devices, sections = lax.axis_size("tile"), lax.axis_size("sec")
    bands = frame // BAND
    capacity = max(2, 2 * tiles * bands // devices)
    slots = devices * capacity
    all_tiles = tiles * devices
    lanes = sections * all_tiles
    sizes = (tiles, bands, frame, source, capacity, devices)
    place = (zoom[0], frac[0], offset[0])
    routes = jnp.transpose(owner, (0, 2, 3, 1))[0]

    rows = tiles * bands
    plan, arriving = exchange_plan(devices)
    blocks = [
        jax.ShapeDtypeStruct((len(group) * capacity, BAND, frame), jnp.bfloat16)
        for group in plan
    ]
    frames, *outgoing = pl.pallas_call(
        functools.partial(render_kernel, sizes),
        name="render",
        in_specs=[HBM] * 5,
        out_specs=[VMEM] * (1 + len(plan)),
        out_shape=[jax.ShapeDtypeStruct((rows, BAND, frame), jnp.bfloat16)] + blocks,
        scratch_shapes=[
            pltpu.SMEM(place[0].shape, jnp.float32),
            pltpu.SMEM(place[1].shape, jnp.float32),
            pltpu.SMEM(place[2].shape, jnp.int32),
            pltpu.SMEM(routes.shape, jnp.int32),
            pltpu.VMEM((tiles, source, source), jnp.bfloat16),
            pltpu.SMEM((devices,), jnp.int32),
            pltpu.SMEM((slots,), jnp.int32),
            pltpu.SemaphoreType.DMA((4,)),
            pltpu.SemaphoreType.DMA((tiles,)),
        ],
        compiler_params=params(24),
        cost_estimate=cost(800_000_000, 4 << 20),
    )(*(pltpu.with_memory_space_constraint(x, pltpu.HBM) for x in (*place, routes, patches[0])))

    base = pl.pallas_call(
        functools.partial(moment_kernel, sizes),
        name="moments",
        in_specs=[SMEM] * 3 + [VMEM],
        out_specs=VMEM,
        out_shape=jax.ShapeDtypeStruct((ROWS, lanes), jnp.float32),
        scratch_shapes=[pltpu.VMEM((3, lanes, frame), jnp.float32)],
        compiler_params=params(24),
        cost_estimate=cost(20_000_000, 1 << 20),
    )(*place, frames)

    codes = pl.pallas_call(
        functools.partial(scan_kernel, sizes),
        name="scan",
        in_specs=[SMEM],
        out_specs=SMEM,
        out_shape=jax.ShapeDtypeStruct((slots + 1,), jnp.int32),
        compiler_params=params(24),
        cost_estimate=cost(20_000_000, 1 << 20),
    )(routes)

    cover_sum, col_cover, slot_lines, slot_bands = pl.pallas_call(
        functools.partial(slot_kernel, sizes),
        name="slots",
        in_specs=[SMEM] * 4,
        out_specs=[VMEM] * 3 + [SMEM],
        out_shape=[
            jax.ShapeDtypeStruct((bands + 1, BAND, frame), jnp.float32),
            jax.ShapeDtypeStruct((all_tiles, frame), jnp.float32),
            jax.ShapeDtypeStruct((3, slots, LANES), jnp.float32),
            pltpu.SMEM((3, slots), jnp.int32),
        ],
        compiler_params=params(24),
        cost_estimate=cost(20_000_000, 1 << 20),
    )(*place, codes)

    def swapped(block, distance):
        return lax.ppermute(block, "tile", [(i, i ^ distance) for i in range(devices)])

    incoming = [outgoing[0]]
    for block, group in zip(outgoing[1:], plan[1:]):
        incoming.append(swapped(block, group[0]))
        if len(group) == 2:
            passed_on = incoming[-1][capacity:]
    if devices == 8:
        incoming.append(swapped(passed_on, 1))

    grid = pl.pallas_call(
        functools.partial(blend_kernel, sizes),
        name="blend",
        in_specs=[SMEM] + [VMEM] * (1 + len(incoming)),
        out_specs=VMEM,
        out_shape=jax.ShapeDtypeStruct((bands, BAND, frame), jnp.bfloat16),
        scratch_shapes=[pltpu.VMEM((bands + 1, BAND, frame), jnp.float32)],
        compiler_params=params(24),
        cost_estimate=cost(1_000_000, 2 << 20),
    )(pltpu.with_memory_space_constraint(slot_bands, pltpu.SMEM), cover_sum, *incoming)

    from_next = lax.ppermute(grid, "sec", [(i, (i - 1) % sections) for i in range(sections)])

    payload, grid_out = pl.pallas_call(
        functools.partial(gradient_kernel, sizes),
        name="gradient",
        in_specs=[SMEM] + [VMEM] * (6 + len(incoming)),
        out_specs=[VMEM, HBM],
        out_shape=[
            jax.ShapeDtypeStruct((sections * devices, ROWS, lanes), jnp.float32),
            jax.ShapeDtypeStruct((bands, BAND, frame), jnp.bfloat16),
        ],
        scratch_shapes=[
            pltpu.VMEM((bands + 1, BAND, frame), jnp.float32),
            pltpu.VMEM((4 * frame // LANES, (all_tiles + 1) * ROWS, LANES), jnp.float32),
            pltpu.SemaphoreType.DMA,
        ],
        compiler_params=params(24),
        cost_estimate=cost(8_000_000, 2 << 20),
    )(
        pltpu.with_memory_space_constraint(slot_bands, pltpu.SMEM),
        from_next,
        top_grid.reshape(bands, BAND, frame),
        col_cover,
        slot_lines,
        base,
        grid,
        *incoming,
    )

    received = lax.all_to_all(
        payload, ("sec", "tile"), split_axis=0, concat_axis=0, tiled=True
    )

    corrections = pl.pallas_call(
        functools.partial(solve_kernel, sizes),
        name="solve",
        in_specs=[VMEM],
        out_specs=VMEM,
        out_shape=jax.ShapeDtypeStruct((tiles, 6), jnp.float32),
        compiler_params=params(24),
        cost_estimate=cost(100_000, 1 << 18),
    )(received)
    return (
        grid_out.reshape(1, 1, frame, frame),
        jnp.transpose(corrections[None], (2, 0, 1)),
    )


def solution(mesh):
    placed = (
        P("sec", "tile", None, None),
        P("sec", None, None),
        P("sec", None, None),
        P("sec", None, None),
        P("sec", None, None, None),
        P("tile", None, None),
    )
    return jax.shard_map(
        shards,
        mesh=mesh,
        in_specs=placed,
        out_specs=(P("sec", "tile", None, None), P(None, "sec", "tile")),
        check_vma=False,
    )
```

```python
import functools
import math

import jax
import jax.numpy as jnp
from jax import lax
from jax.experimental import pallas as pl
from jax.experimental.pallas import tpu as pltpu
from jax.sharding import PartitionSpec as P

BAND = 16
ITERS = 2
COUPLING = 0.25
LANES = 128
ROWS = 8
SPARE = 24
PACKED = 29
HBM = pl.BlockSpec(memory_space=pltpu.HBM)
SMEM = pl.BlockSpec(memory_space=pltpu.SMEM)
VMEM = pl.BlockSpec(memory_space=pltpu.VMEM)


def params(mebibytes):
    return pltpu.CompilerParams(vmem_limit_bytes=mebibytes * 1024 * 1024)


def cost(flops, size):
    return pl.CostEstimate(flops=flops, bytes_accessed=size, transcendentals=0)


def exact_dot(left, right):
    return lax.dot_general(
        left,
        right,
        (((1,), (1,)), ((), ())),
        precision=lax.Precision.HIGHEST,
        preferred_element_type=jnp.float32,
    )


def points_of(spots, zoom, frac, offset, axis, tile, ratio):
    scale = zoom[axis, tile] * ratio
    return (spots - offset[axis, tile].astype(jnp.float32) - frac[axis, tile]) / scale


def cover_of(points, source):
    return jnp.clip(jnp.minimum(points + 1.0, source - points), 0.0, 1.0)


def hat_weight(distance):
    return jnp.maximum(0.0, 1.0 - jnp.abs(distance))


def spots_along(shape, dim, start=0):
    return (lax.broadcasted_iota(jnp.int32, shape, dim) + start).astype(jnp.float32)


def coords(spots, frame):
    return (spots - (frame - 1) / 2.0) / (frame / 2.0)


def exchange_plan(devices):
    if devices == 8:
        outgoing = [[0], [2, 3], [4], [5], [6], [7], [1]]
        return outgoing, [(0, 0), (1, 2), (2, 4), (3, 5), (4, 6), (5, 7), (6, 1), (7, 3)]
    return [[d] for d in range(devices)], [(d, d) for d in range(devices)]


def is_packed(capacity, devices, distance):
    return devices == 8 and capacity == 16 and distance > 0


def spare_pieces():
    kept = LANES - SPARE
    pieces = [(4 * i + c, kept, 13 + i, SPARE * c, SPARE) for i in range(3) for c in range(4)]
    return pieces + [(12, kept + 8 * i, 13 + i, 4 * SPARE, 8) for i in range(3)]


def moved(value, start, goal):
    shift = (goal - start) % LANES
    return pltpu.roll(value, shift, 1) if shift else value


def lane_window(start, count):
    lane = lax.broadcasted_iota(jnp.int32, (BAND, LANES), 1)
    return (lane >= start) & (lane < start + count)


def pack_block(there, start, firsts, seconds):
    for k in range(16):
        there[start + k] = firsts(k)
    values = [seconds(k).astype(jnp.float32) for k in range(16)]
    for slot, lane, donor, goal, count in spare_pieces():
        values[slot] = jnp.where(
            lane_window(lane, count), moved(values[donor], goal, lane), values[slot]
        )
    for k in range(13):
        there[start + 16 + k] = values[k].astype(jnp.bfloat16)


def unpack_block(block):
    firsts = [block[k].astype(jnp.float32) for k in range(16)]
    seconds = [block[16 + k].astype(jnp.float32) for k in range(13)]
    seconds += [jnp.zeros((BAND, LANES), jnp.float32)] * 3
    for slot, lane, donor, start, count in spare_pieces():
        seconds[donor] = jnp.where(
            lane_window(start, count), moved(seconds[slot], lane, start), seconds[donor]
        )
    kept = lane_window(0, LANES - SPARE)
    seconds = [
        jnp.where(kept, second, moved(first, 0, LANES - SPARE))
        for first, second in zip(firsts, seconds)
    ]
    return list(zip(firsts, seconds))


def render_kernel(
    sizes, zoom_in, frac_in, offset_in, owner_in, patches_in, frames, *outgoing_and_scratch
):
    tiles, bands, frame, source, capacity, devices = sizes
    plan, _ = exchange_plan(devices)
    outgoing = outgoing_and_scratch[: len(plan)]
    zoom, frac, offset, owner, patches, named, rows, small_sems, patch_sems = (
        outgoing_and_scratch[len(plan) :]
    )
    me = lax.axis_index("tile")
    first_tile = me * tiles
    ratio = frame / source
    fetched = [
        pltpu.make_async_copy(patches_in.at[j], patches.at[j], patch_sems.at[j])
        for j in range(tiles)
    ]
    small = [
        pltpu.make_async_copy(there, here, small_sems.at[k])
        for k, (there, here) in enumerate(
            ((zoom_in, zoom), (frac_in, frac), (offset_in, offset), (owner_in, owner))
        )
    ]
    for copy in small + fetched:
        copy.start()
    for g in range(devices):
        named[g] = 0
    for slot in range(devices * capacity):
        rows[slot] = 0
    for copy in small:
        copy.wait()
    for j in range(tiles):
        tile = first_tile + j
        row_points = points_of(spots_along((frame, LANES), 0), zoom, frac, offset, 0, tile, ratio)
        row_weights = jnp.concatenate(
            [
                hat_weight(row_points - spots_along((frame, LANES), 1, p)).astype(jnp.bfloat16)
                for p in range(0, source, LANES)
            ],
            axis=1,
        )
        col_points = points_of(spots_along((ROWS, frame), 1), zoom, frac, offset, 1, tile, ratio)
        over = moved(col_points[:, frame - LANES :], LANES - SPARE, 0)
        lane = lax.broadcasted_iota(jnp.int32, over.shape, 1)
        folded = (lane < SPARE) & (cover_of(over, source) > 0.0)
        col_points = jnp.concatenate(
            [jnp.where(folded, over, col_points[:, :LANES]), col_points[:, LANES:]], axis=1
        )
        col_points = jnp.broadcast_to(col_points[:1], (source, frame))
        col_weights = hat_weight(col_points - spots_along((source, frame), 0)).astype(jnp.bfloat16)
        fetched[j].wait()
        half, quarter = source // 2, frame // 4
        upper = jnp.dot(
            row_weights[: 3 * quarter, :half],
            patches[j, :half],
            preferred_element_type=jnp.float32,
        )
        lower = jnp.dot(
            row_weights[quarter:, half:],
            patches[j, half:],
            preferred_element_type=jnp.float32,
        )
        halfway = jnp.concatenate(
            [upper[:quarter], upper[quarter:] + lower[: 2 * quarter], lower[2 * quarter :]]
        )
        rendered = jnp.dot(
            halfway.astype(jnp.bfloat16), col_weights, preferred_element_type=jnp.float32
        ).astype(jnp.bfloat16)
        frames[j * bands : (j + 1) * bands] = rendered.reshape(bands, BAND, frame)
        for band in range(bands):
            target = owner[band, 0, tile]
            slot = named[target]
            named[target] = slot + 1
            rows[target * capacity + slot] = j * bands + band
    for there, group in zip(outgoing, plan):
        for position, distance in enumerate(group):
            target = me ^ distance
            if is_packed(capacity, devices, distance):
                taken = [rows[target * capacity + slot] for slot in range(capacity)]
                pack_block(
                    there,
                    PACKED * position,
                    lambda k: frames[taken[k], :, :LANES],
                    lambda k: frames[taken[k], :, LANES:],
                )
                continue
            for slot in range(capacity):
                there[position * capacity + slot] = frames[rows[target * capacity + slot]]


def feature_rows(frame, wanted):
    shape = (ROWS, frame)
    x = coords(spots_along(shape, 1), frame)
    row = lax.broadcasted_iota(jnp.int32, shape, 0)
    rows = jnp.zeros(shape, jnp.float32)
    for r, power in wanted.items():
        rows = jnp.where(row == r, (jnp.ones_like(x), x, x * x)[power], rows)
    return rows


MOMENT_ROWS = ({0: 0, 1: 1, 3: 2}, {2: 0, 4: 1}, {5: 0})


def scan_kernel(sizes, owner, codes):
    tiles, bands, frame, source, capacity, devices = sizes
    me = lax.axis_index("tile")

    def scan(block, distance):
        count = 0
        for j in range(tiles):
            tile = (me ^ distance) * tiles + j
            named = [owner[band, 0, tile] for band in range(bands)]
            for band in range(bands):
                codes[block * capacity + count] = tile * bands + band
                count += (named[band] == me).astype(jnp.int32)

        def blank(position, carry):
            codes[block * capacity + position] = -1
            return carry

        lax.fori_loop(count, capacity, blank, 0)

    arriving = exchange_plan(devices)[1]
    if devices == 8:
        for block, (_, distance) in enumerate(arriving):
            scan(block, distance)
    else:
        pl.loop(0, devices)(lambda block: scan(block, block))


def slot_kernel(
    sizes, zoom, frac, offset, codes, cover_sum, col_cover, slot_lines, slot_bands
):
    tiles, bands, frame, source, capacity, devices = sizes
    slots = devices * capacity
    all_tiles = tiles * devices
    ratio = frame / source

    @pl.loop(0, all_tiles // ROWS)
    def _(group):
        for k in range(ROWS):
            tile = group * ROWS + k
            points = points_of(spots_along((1, frame), 1), zoom, frac, offset, 1, tile, ratio)
            col_cover[pl.ds(tile, 1), :] = cover_of(points, source)

    col_cover[all_tiles:] = jnp.zeros((ROWS, frame), jnp.float32)
    cover_sum[...] = jnp.zeros_like(cover_sum)
    unroll = math.gcd(slots, ROWS)

    @pl.loop(0, slots // unroll)
    def _(group):
        for k in range(unroll):
            slot = group * unroll + k
            used = codes[slot] >= 0
            code = jnp.maximum(codes[slot], 0)
            tile, band = code // bands, code % bands
            before = jnp.maximum(codes[jnp.maximum(slot - 1, 0)], 0) // bands
            place = jnp.where(used, band, bands)
            slot_bands[0, slot] = place
            slot_bands[1, slot] = jnp.where(used, tile, all_tiles)
            slot_bands[2, slot] = (used & (before == tile)).astype(jnp.int32)
            here = pl.ds(slot, 1)
            row = jnp.zeros((1, LANES), jnp.float32)
            start = row + (band * BAND).astype(jnp.float32)
            shift = row + (offset[0, tile].astype(jnp.float32) + frac[0, tile])
            inverse = 1.0 / (row + zoom[0, tile] * ratio)
            slope = jnp.broadcast_to(inverse, (BAND, LANES))
            first = (start - shift) * inverse
            slot_lines[0, here, :] = inverse
            slot_lines[1, here, :] = first
            slot_lines[2, here, :] = coords(start, frame)
            cover = cover_of(spots_along((BAND, LANES), 0) * slope + first, source)
            columns = col_cover[pl.ds(tile, 1), :]
            for half in range(frame // LANES):
                part = slice(half * LANES, (half + 1) * LANES)
                cover_sum[place, :, part] += cover * columns[:, part]


def moment_kernel(sizes, zoom, frac, offset, frames, base, parts):
    tiles, bands, frame, source, capacity, devices = sizes
    me = lax.axis_index("tile")
    sec = lax.axis_index("sec")
    sections = lax.axis_size("sec")
    all_tiles = tiles * devices
    ratio = frame / source
    parts[...] = jnp.zeros_like(parts)
    for j in range(tiles):
        tile = me * tiles + j
        spots = spots_along((frame, frame), 0)
        y = coords(spots, frame)
        cover = cover_of(points_of(spots, zoom, frac, offset, 0, tile, ratio), source)
        level = frames[j * bands : (j + 1) * bands].reshape(frame, frame).astype(jnp.float32)
        columns = points_of(spots_along((1, frame), 1), zoom, frac, offset, 1, tile, ratio)
        columns = cover_of(columns, source)
        weighted = (cover, cover * y, cover * y * y)
        for power, image in enumerate((None, level, level * level)):
            block = (sec + 1 + power) % sections
            place = block * all_tiles + tile
            for a, rows in enumerate(weighted):
                total = rows if image is None else rows * image
                parts[a, pl.ds(place, 1), :] = columns * jnp.sum(total, axis=0, keepdims=True)
    total = exact_dot(feature_rows(frame, MOMENT_ROWS[0]), parts[0])
    for a in (1, 2):
        total += exact_dot(feature_rows(frame, MOMENT_ROWS[a]), parts[a])
    base[...] = total


def add_blocks(sizes, chosen, slot_bands, col_cover, blocks, whole, total):
    tiles, bands, frame, source, capacity, devices = sizes
    whole = iter(whole)
    for (block, distance), values in zip(chosen, blocks):
        packed = is_packed(capacity, devices, distance)
        if packed:
            unpacked, levels = next(whole), unpack_block(values)
        for k in range(capacity):
            slot = block * capacity + k
            columns = col_cover[pl.ds(slot_bands[1, slot], 1), :]
            for half in range(frame // LANES):
                part = slice(half * LANES, (half + 1) * LANES)
                level = levels[k][half] if packed else values[k, :, part].astype(jnp.float32)
                if packed or half == 0:
                    level = jnp.where(columns[:, part] > 0.0, level, 0.0)
                total[slot_bands[0, slot], :, part] += level
                if packed:
                    unpacked[k, :, part] = level.astype(jnp.bfloat16)


def first_blend_kernel(sizes, chosen, slot_bands, col_cover, *refs):
    blocks, (total, *whole) = refs[: len(chosen)], refs[len(chosen) :]
    total[...] = jnp.zeros_like(total)
    add_blocks(sizes, chosen, slot_bands, col_cover, blocks, whole, total)


def last_blend_kernel(sizes, chosen, slot_bands, col_cover, cover_sum, before, *refs):
    bands = sizes[1]
    blocks, (grid, *whole, total) = refs[: len(chosen)], refs[len(chosen) :]
    total[...] = before[...]
    add_blocks(sizes, chosen, slot_bands, col_cover, blocks, whole, total)
    grid[...] = (total[:bands] / (1.0 + cover_sum[:bands])).astype(jnp.bfloat16)


GRADIENT_ROWS = ({0: 0, 1: 1}, {2: 0}, {3: 0, 4: 1}, {5: 0})


def gradient_kernel(
    sizes, slot_bands, from_next, top_grid, col_cover, slot_lines, base, grid, *blocks_and_rest
):
    tiles, bands, frame, source, capacity, devices = sizes
    *blocks, payload, grid_out, above, sums, grid_sem = blocks_and_rest
    written = pltpu.make_async_copy(grid, grid_out, grid_sem)
    written.start()
    sec = lax.axis_index("sec")
    all_tiles = tiles * devices
    lanes = base.shape[1]

    @pl.when(sec == lax.axis_size("sec") - 1)
    def _():
        above[:bands] = top_grid[...].astype(jnp.float32)

    @pl.when(sec != lax.axis_size("sec") - 1)
    def _():
        above[:bands] = from_next[...].astype(jnp.float32)

    above[bands] = jnp.zeros((BAND, frame), jnp.float32)
    sums[...] = jnp.zeros_like(sums)
    spots = spots_along((BAND, LANES), 0)
    raised = spots * (2.0 / frame)
    halves = range(frame // LANES)

    for block, (array, _) in enumerate(exchange_plan(devices)[1]):
        running = None
        for k in range(capacity):
            slot = block * capacity + k
            here = slice(slot, slot + 1)
            points = spots * slot_lines[0, here] + slot_lines[1, here]
            cover = cover_of(points, source)
            lifted = cover * (raised + slot_lines[2, here])
            level = blocks[array][k].astype(jnp.float32)
            error = above[slot_bands[0, slot]] - level
            product = error * level
            terms = []
            for half in halves:
                part = slice(half * LANES, (half + 1) * LANES)
                for weight, value in (
                    (cover, error),
                    (lifted, error),
                    (cover, product),
                    (lifted, product),
                ):
                    term = weight * value[:, part]
                    terms.append(term[:ROWS] + term[ROWS:])
            if running is not None:
                same = slot_bands[2, slot] == 1
                terms = [
                    term + jnp.where(same, before, 0.0) for term, before in zip(terms, running)
                ]
            running = terms
            rows = pl.ds(pl.multiple_of(slot_bands[1, slot] * ROWS, ROWS), ROWS)
            for index, term in enumerate(terms):
                sums[index, rows, :] = term

    values = [jnp.zeros((all_tiles, 1), jnp.float32)] * 6
    for half in halves:
        columns = col_cover[:all_tiles, half * LANES : (half + 1) * LANES]
        x = coords(spots_along((all_tiles, LANES), 1, half * LANES), frame)
        for kind, wanted in enumerate(GRADIENT_ROWS):
            index = half * len(GRADIENT_ROWS) + kind
            value = sums[index, pl.ds(0, all_tiles, stride=ROWS), :]
            for r in range(1, ROWS):
                value += sums[index, pl.ds(r, all_tiles, stride=ROWS), :]
            value = value * columns
            for row, power in wanted.items():
                term = value * x if power else value
                values[row] += jnp.sum(term, axis=1, keepdims=True)
    total = []
    tile = lax.broadcasted_iota(jnp.int32, (all_tiles, LANES), 0) + sec * all_tiles
    for first in range(0, lanes, LANES):
        lane = lax.broadcasted_iota(jnp.int32, (all_tiles, LANES), 1) + first
        places = (tile == lane).astype(jnp.float32)
        rows = [jnp.sum(places * value, axis=0, keepdims=True) for value in values]
        total.append(jnp.concatenate(rows + [jnp.zeros_like(rows[0])] * (ROWS - 6), axis=0))
    total = base[...] + jnp.concatenate(total, axis=1)
    payload[...] = jnp.broadcast_to(total[None], payload.shape)
    written.wait()


def solve_kernel(sizes, received, corrections):
    tiles, bands, frame, source, capacity, devices = sizes
    sec, me = lax.axis_index("sec"), lax.axis_index("tile")
    sections = lax.axis_size("sec")
    all_tiles = tiles * devices
    lanes = sections * all_tiles
    lane = lax.broadcasted_iota(jnp.int32, (ROWS, lanes), 1)
    within = lane % all_tiles
    area = frame * frame

    gradients = jnp.zeros((ROWS, lanes), jnp.float32)
    moments = [jnp.zeros((ROWS, lanes), jnp.float32) for _ in range(3)]
    for s in range(sections):
        own = received[s * devices]
        for t in range(1, devices):
            own += received[s * devices + t]
        here = lane // all_tiles == s
        gradients = jnp.where(here, own, gradients)
        for power in range(3):
            shift = ((sections - 1 - power) * all_tiles) % lanes
            moved = pltpu.roll(own, shift, 1) if shift else own
            moments[power] = jnp.where(here, moved, moments[power])
    gradients = gradients * (1.0 / area)
    moments = [m * (1.0 / area) for m in moments]

    where = ((0, 1, 2), (1, 3, 4), (2, 4, 5))
    row = lax.broadcasted_iota(jnp.int32, (ROWS, lanes), 0)

    def entry(f, g):
        kind = moments[(f >= 3) + (g >= 3)]
        index = where[f % 3][g % 3]
        return kind[index : index + 1]

    def stacked(rows):
        result = jnp.zeros((ROWS, lanes), jnp.float32)
        for f, value in enumerate(rows):
            result = jnp.where(row == f, value, result)
        return result

    normal = [stacked([entry(f, g) for f in range(6)]) for g in range(6)]
    diagonal = stacked([entry(f, f) for f in range(6)])
    precond = 1.0 / (diagonal + 4.0 * COUPLING)

    def total(values):
        return jnp.sum(jnp.sum(values, axis=1, keepdims=True), axis=0, keepdims=True)

    def operator(vector):
        beside = jnp.where(within < all_tiles - 1, pltpu.roll(vector, lanes - 1, 1), 0.0)
        beside += jnp.where(within > 0, pltpu.roll(vector, 1, 1), 0.0)
        upward = pltpu.roll(vector, lanes - all_tiles, 1)
        beside += jnp.where(lane < lanes - all_tiles, upward, 0.0)
        beside += jnp.where(lane >= all_tiles, pltpu.roll(vector, all_tiles, 1), 0.0)
        image = COUPLING * (4.0 * vector - beside)
        for g in range(6):
            image += normal[g] * vector[g : g + 1]
        return image

    answer = jnp.zeros((ROWS, lanes), jnp.float32)
    residual = gradients
    scaled = precond * residual
    direction = scaled
    current = total(residual * scaled)
    for step in range(ITERS):
        image = operator(direction)
        alpha = current / total(direction * image)
        answer = answer + alpha * direction
        if step + 1 < ITERS:
            residual = residual - alpha * image
            scaled = precond * residual
            following = total(residual * scaled)
            direction = scaled + following / current * direction
            current = following

    first = sec * all_tiles + me * tiles
    chosen = (row + first == lane).astype(jnp.float32)
    place = lax.broadcasted_iota(jnp.int32, (ROWS, LANES), 1)
    own = jnp.zeros((ROWS, LANES), jnp.float32)
    for f in range(6):
        value = jnp.sum(chosen * answer[f : f + 1], axis=1, keepdims=True)
        own = jnp.where(place == f, value, own)
    corrections[...] = own[:tiles, :6]


def shards(patches, zoom, frac, offset, owner, top_grid):
    _, tiles, source, _ = patches.shape
    frame = top_grid.shape[1]
    devices, sections = lax.axis_size("tile"), lax.axis_size("sec")
    bands = frame // BAND
    capacity = max(2, 2 * tiles * bands // devices)
    slots = devices * capacity
    all_tiles = tiles * devices
    lanes = sections * all_tiles
    sizes = (tiles, bands, frame, source, capacity, devices)
    place = (zoom[0], frac[0], offset[0])
    routes = jnp.transpose(owner, (0, 2, 3, 1))[0]

    rows = tiles * bands
    plan, arriving = exchange_plan(devices)
    blocks = [
        jax.ShapeDtypeStruct(
            (len(group) * PACKED, BAND, LANES)
            if is_packed(capacity, devices, group[0])
            else (len(group) * capacity, BAND, frame),
            jnp.bfloat16,
        )
        for group in plan
    ]
    frames, *outgoing = pl.pallas_call(
        functools.partial(render_kernel, sizes),
        name="render",
        in_specs=[HBM] * 5,
        out_specs=[VMEM] * (1 + len(plan)),
        out_shape=[jax.ShapeDtypeStruct((rows, BAND, frame), jnp.bfloat16)] + blocks,
        scratch_shapes=[
            pltpu.SMEM(place[0].shape, jnp.float32),
            pltpu.SMEM(place[1].shape, jnp.float32),
            pltpu.SMEM(place[2].shape, jnp.int32),
            pltpu.SMEM(routes.shape, jnp.int32),
            pltpu.VMEM((tiles, source, source), jnp.bfloat16),
            pltpu.SMEM((devices,), jnp.int32),
            pltpu.SMEM((slots,), jnp.int32),
            pltpu.SemaphoreType.DMA((4,)),
            pltpu.SemaphoreType.DMA((tiles,)),
        ],
        compiler_params=params(24),
        cost_estimate=cost(800_000_000, 4 << 20),
    )(*(pltpu.with_memory_space_constraint(x, pltpu.HBM) for x in (*place, routes, patches[0])))

    base = pl.pallas_call(
        functools.partial(moment_kernel, sizes),
        name="moments",
        in_specs=[SMEM] * 3 + [VMEM],
        out_specs=VMEM,
        out_shape=jax.ShapeDtypeStruct((ROWS, lanes), jnp.float32),
        scratch_shapes=[pltpu.VMEM((3, lanes, frame), jnp.float32)],
        compiler_params=params(24),
        cost_estimate=cost(20_000_000, 1 << 20),
    )(*place, frames)

    codes = pl.pallas_call(
        functools.partial(scan_kernel, sizes),
        name="scan",
        in_specs=[SMEM],
        out_specs=SMEM,
        out_shape=jax.ShapeDtypeStruct((slots + 1,), jnp.int32),
        compiler_params=params(24),
        cost_estimate=cost(20_000_000, 1 << 20),
    )(routes)

    cover_sum, col_cover, slot_lines, slot_bands = pl.pallas_call(
        functools.partial(slot_kernel, sizes),
        name="slots",
        in_specs=[SMEM] * 4,
        out_specs=[VMEM] * 3 + [SMEM],
        out_shape=[
            jax.ShapeDtypeStruct((bands + 1, BAND, frame), jnp.float32),
            jax.ShapeDtypeStruct((all_tiles + ROWS, frame), jnp.float32),
            jax.ShapeDtypeStruct((3, slots, LANES), jnp.float32),
            pltpu.SMEM((3, slots), jnp.int32),
        ],
        compiler_params=params(24),
        cost_estimate=cost(20_000_000, 1 << 20),
    )(*place, codes)

    def swapped(block, distance):
        return lax.ppermute(block, "tile", [(i, i ^ distance) for i in range(devices)])

    incoming = [outgoing[0]]
    for block, group in zip(outgoing[1:], plan[1:]):
        incoming.append(swapped(block, group[0]))
        if len(group) == 2:
            passed_on = incoming[-1][incoming[-1].shape[0] // 2 :]
    if devices == 8:
        incoming.append(swapped(passed_on, 1))

    slot_bands = pltpu.with_memory_space_constraint(slot_bands, pltpu.SMEM)
    total = jax.ShapeDtypeStruct((bands + 1, BAND, frame), jnp.float32)

    def blend(kernel, name, chosen, results, scratch, *operands):
        distances = [(block, arriving[block][1]) for block in chosen]
        arrays = [arriving[block][0] for block in chosen]
        packed = [
            array
            for array, (_, distance) in zip(arrays, distances)
            if is_packed(capacity, devices, distance)
        ]
        whole = jax.ShapeDtypeStruct((capacity, BAND, frame), jnp.bfloat16)
        result, *unpacked = pl.pallas_call(
            functools.partial(kernel, sizes, distances),
            name=name,
            in_specs=[SMEM] + [VMEM] * (len(operands) + len(chosen)),
            out_specs=[VMEM] * (1 + len(packed)),
            out_shape=[results] + [whole] * len(packed),
            scratch_shapes=scratch,
            compiler_params=params(24),
            cost_estimate=cost(1_000_000, 2 << 20),
        )(slot_bands, *operands, *(incoming[array] for array in arrays))
        for array, block in zip(packed, unpacked):
            incoming[array] = block
        return result

    last = (4, 5) if devices == 8 else range(devices - devices // 4, devices)
    early = [block for block in range(devices) if block not in last]
    before = blend(first_blend_kernel, "first_blend", early, total, [], col_cover)
    grid = blend(
        last_blend_kernel,
        "last_blend",
        last,
        jax.ShapeDtypeStruct((bands, BAND, frame), jnp.bfloat16),
        [pltpu.VMEM(total.shape, total.dtype)],
        col_cover,
        cover_sum,
        before,
    )

    from_next = lax.ppermute(grid, "sec", [(i, (i - 1) % sections) for i in range(sections)])

    payload, grid_out = pl.pallas_call(
        functools.partial(gradient_kernel, sizes),
        name="gradient",
        in_specs=[SMEM] + [VMEM] * (6 + len(incoming)),
        out_specs=[VMEM, HBM],
        out_shape=[
            jax.ShapeDtypeStruct((sections * devices, ROWS, lanes), jnp.float32),
            jax.ShapeDtypeStruct((bands, BAND, frame), jnp.bfloat16),
        ],
        scratch_shapes=[
            pltpu.VMEM((bands + 1, BAND, frame), jnp.float32),
            pltpu.VMEM((4 * frame // LANES, (all_tiles + 1) * ROWS, LANES), jnp.float32),
            pltpu.SemaphoreType.DMA,
        ],
        compiler_params=params(24),
        cost_estimate=cost(8_000_000, 2 << 20),
    )(
        slot_bands,
        from_next,
        top_grid.reshape(bands, BAND, frame),
        col_cover,
        slot_lines,
        base,
        grid,
        *incoming,
    )

    received = lax.all_to_all(
        payload, ("sec", "tile"), split_axis=0, concat_axis=0, tiled=True
    )

    corrections = pl.pallas_call(
        functools.partial(solve_kernel, sizes),
        name="solve",
        in_specs=[VMEM],
        out_specs=VMEM,
        out_shape=jax.ShapeDtypeStruct((tiles, 6), jnp.float32),
        compiler_params=params(24),
        cost_estimate=cost(100_000, 1 << 18),
    )(received)
    return (
        grid_out.reshape(1, 1, frame, frame),
        jnp.transpose(corrections[None], (2, 0, 1)),
    )


def solution(mesh):
    placed = (
        P("sec", "tile", None, None),
        P("sec", None, None),
        P("sec", None, None),
        P("sec", None, None),
        P("sec", None, None, None),
        P("tile", None, None),
    )
    return jax.shard_map(
        shards,
        mesh=mesh,
        in_specs=placed,
        out_specs=(P("sec", "tile", None, None), P(None, "sec", "tile")),
        check_vma=False,
    )
```

```python
import functools
import math

import jax
import jax.numpy as jnp
from jax import lax
from jax.experimental import pallas as pl
from jax.experimental.pallas import tpu as pltpu
from jax.sharding import PartitionSpec as P

BAND = 16
ITERS = 2
COUPLING = 0.25
LANES = 128
ROWS = 8
SPARE = 24
PACKED = 29
HBM = pl.BlockSpec(memory_space=pltpu.HBM)
SMEM = pl.BlockSpec(memory_space=pltpu.SMEM)
VMEM = pl.BlockSpec(memory_space=pltpu.VMEM)


def params(mebibytes):
    return pltpu.CompilerParams(vmem_limit_bytes=mebibytes * 1024 * 1024)


def cost(flops, size):
    return pl.CostEstimate(flops=flops, bytes_accessed=size, transcendentals=0)


def exact_dot(left, right):
    return lax.dot_general(
        left,
        right,
        (((1,), (1,)), ((), ())),
        precision=lax.Precision.HIGHEST,
        preferred_element_type=jnp.float32,
    )


def points_of(spots, zoom, frac, offset, axis, tile, ratio):
    scale = zoom[axis, tile] * ratio
    return (spots - offset[axis, tile].astype(jnp.float32) - frac[axis, tile]) / scale


def cover_of(points, source):
    return jnp.clip(jnp.minimum(points + 1.0, source - points), 0.0, 1.0)


def hat_weight(distance):
    return jnp.maximum(0.0, 1.0 - jnp.abs(distance))


def spots_along(shape, dim, start=0):
    return (lax.broadcasted_iota(jnp.int32, shape, dim) + start).astype(jnp.float32)


def coords(spots, frame):
    return (spots - (frame - 1) / 2.0) / (frame / 2.0)


def exchange_plan(devices):
    if devices == 8:
        outgoing = [[0], [2, 3], [4], [5], [6], [7], [1]]
        return outgoing, [(0, 0), (1, 2), (2, 4), (3, 5), (4, 6), (5, 7), (6, 1), (7, 3)]
    return [[d] for d in range(devices)], [(d, d) for d in range(devices)]


def is_packed(capacity, devices, distance):
    return devices == 8 and capacity == 16 and distance > 0


def spare_pieces():
    kept = LANES - SPARE
    pieces = [(4 * i + c, kept, 13 + i, SPARE * c, SPARE) for i in range(3) for c in range(4)]
    return pieces + [(12, kept + 8 * i, 13 + i, 4 * SPARE, 8) for i in range(3)]


def moved(value, start, goal):
    shift = (goal - start) % LANES
    return pltpu.roll(value, shift, 1) if shift else value


def lane_window(start, count):
    lane = lax.broadcasted_iota(jnp.int32, (BAND, LANES), 1)
    return (lane >= start) & (lane < start + count)


def pack_block(there, start, firsts, seconds):
    for k in range(16):
        there[start + k] = firsts(k)
    values = [seconds(k).astype(jnp.float32) for k in range(16)]
    for slot, lane, donor, goal, count in spare_pieces():
        values[slot] = jnp.where(
            lane_window(lane, count), moved(values[donor], goal, lane), values[slot]
        )
    for k in range(13):
        there[start + 16 + k] = values[k].astype(jnp.bfloat16)


def unpack_block(block):
    firsts = [block[k].astype(jnp.float32) for k in range(16)]
    seconds = [block[16 + k].astype(jnp.float32) for k in range(13)]
    seconds += [jnp.zeros((BAND, LANES), jnp.float32)] * 3
    for slot, lane, donor, start, count in spare_pieces():
        seconds[donor] = jnp.where(
            lane_window(start, count), moved(seconds[slot], lane, start), seconds[donor]
        )
    kept = lane_window(0, LANES - SPARE)
    seconds = [
        jnp.where(kept, second, moved(first, 0, LANES - SPARE))
        for first, second in zip(firsts, seconds)
    ]
    return list(zip(firsts, seconds))


def render_kernel(
    sizes, zoom_in, frac_in, offset_in, owner_in, patches_in, frames, *outgoing_and_scratch
):
    tiles, bands, frame, source, capacity, devices = sizes
    plan, _ = exchange_plan(devices)
    outgoing = outgoing_and_scratch[: len(plan)]
    zoom, frac, offset, owner, patches, named, rows, small_sems, patch_sems = (
        outgoing_and_scratch[len(plan) :]
    )
    me = lax.axis_index("tile")
    first_tile = me * tiles
    ratio = frame / source
    fetched = [
        pltpu.make_async_copy(patches_in.at[j], patches.at[j], patch_sems.at[j])
        for j in range(tiles)
    ]
    small = [
        pltpu.make_async_copy(there, here, small_sems.at[k])
        for k, (there, here) in enumerate(
            ((zoom_in, zoom), (frac_in, frac), (offset_in, offset), (owner_in, owner))
        )
    ]
    for copy in small + fetched:
        copy.start()
    for g in range(devices):
        named[g] = 0
    for slot in range(devices * capacity):
        rows[slot] = 0
    for copy in small:
        copy.wait()
    for j in range(tiles):
        tile = first_tile + j
        row_points = points_of(spots_along((frame, LANES), 0), zoom, frac, offset, 0, tile, ratio)
        row_weights = jnp.concatenate(
            [
                hat_weight(row_points - spots_along((frame, LANES), 1, p)).astype(jnp.bfloat16)
                for p in range(0, source, LANES)
            ],
            axis=1,
        )
        col_points = points_of(spots_along((ROWS, frame), 1), zoom, frac, offset, 1, tile, ratio)
        over = moved(col_points[:, frame - LANES :], LANES - SPARE, 0)
        lane = lax.broadcasted_iota(jnp.int32, over.shape, 1)
        folded = (lane < SPARE) & (cover_of(over, source) > 0.0)
        col_points = jnp.concatenate(
            [jnp.where(folded, over, col_points[:, :LANES]), col_points[:, LANES:]], axis=1
        )
        col_points = jnp.broadcast_to(col_points[:1], (source, frame))
        col_weights = hat_weight(col_points - spots_along((source, frame), 0)).astype(jnp.bfloat16)
        fetched[j].wait()
        half, quarter = source // 2, frame // 4
        upper = jnp.dot(
            row_weights[: 3 * quarter, :half],
            patches[j, :half],
            preferred_element_type=jnp.float32,
        )
        lower = jnp.dot(
            row_weights[quarter:, half:],
            patches[j, half:],
            preferred_element_type=jnp.float32,
        )
        halfway = jnp.concatenate(
            [upper[:quarter], upper[quarter:] + lower[: 2 * quarter], lower[2 * quarter :]]
        )
        rendered = jnp.dot(
            halfway.astype(jnp.bfloat16), col_weights, preferred_element_type=jnp.float32
        ).astype(jnp.bfloat16)
        frames[j * bands : (j + 1) * bands] = rendered.reshape(bands, BAND, frame)
        for band in range(bands):
            target = owner[band, 0, tile]
            slot = named[target]
            named[target] = slot + 1
            rows[target * capacity + slot] = j * bands + band
    for there, group in zip(outgoing, plan):
        for position, distance in enumerate(group):
            target = me ^ distance
            if is_packed(capacity, devices, distance):
                taken = [rows[target * capacity + slot] for slot in range(capacity)]
                pack_block(
                    there,
                    PACKED * position,
                    lambda k: frames[taken[k], :, :LANES],
                    lambda k: frames[taken[k], :, LANES:],
                )
                continue
            for slot in range(capacity):
                there[position * capacity + slot] = frames[rows[target * capacity + slot]]


def feature_rows(frame, wanted):
    shape = (ROWS, frame)
    x = coords(spots_along(shape, 1), frame)
    row = lax.broadcasted_iota(jnp.int32, shape, 0)
    rows = jnp.zeros(shape, jnp.float32)
    for r, power in wanted.items():
        rows = jnp.where(row == r, (jnp.ones_like(x), x, x * x)[power], rows)
    return rows


MOMENT_ROWS = ((0, 0, {0: 0, 1: 1}), (0, 1, {2: 0}), (1, 0, {0: 2}), (1, 1, {1: 1}), (1, 2, {2: 0}))
PAYLOAD_ROWS = 4


def scan_kernel(sizes, owner, codes):
    tiles, bands, frame, source, capacity, devices = sizes
    me = lax.axis_index("tile")

    def scan(block, distance):
        count = 0
        for j in range(tiles):
            tile = (me ^ distance) * tiles + j
            named = [owner[band, 0, tile] for band in range(bands)]
            for band in range(bands):
                codes[block * capacity + count] = tile * bands + band
                count += (named[band] == me).astype(jnp.int32)

        def blank(position, carry):
            codes[block * capacity + position] = -1
            return carry

        lax.fori_loop(count, capacity, blank, 0)

    arriving = exchange_plan(devices)[1]
    if devices == 8:
        for block, (_, distance) in enumerate(arriving):
            scan(block, distance)
    else:
        pl.loop(0, devices)(lambda block: scan(block, block))


def slot_kernel(
    sizes, zoom, frac, offset, codes, cover_sum, col_cover, slot_lines, slot_bands
):
    tiles, bands, frame, source, capacity, devices = sizes
    slots = devices * capacity
    all_tiles = tiles * devices
    ratio = frame / source

    @pl.loop(0, all_tiles // ROWS)
    def _(group):
        for k in range(ROWS):
            tile = group * ROWS + k
            points = points_of(spots_along((1, frame), 1), zoom, frac, offset, 1, tile, ratio)
            col_cover[pl.ds(tile, 1), :] = cover_of(points, source)

    col_cover[all_tiles:] = jnp.zeros((ROWS, frame), jnp.float32)
    cover_sum[...] = jnp.zeros_like(cover_sum)
    unroll = math.gcd(slots, ROWS)

    @pl.loop(0, slots // unroll)
    def _(group):
        for k in range(unroll):
            slot = group * unroll + k
            used = codes[slot] >= 0
            code = jnp.maximum(codes[slot], 0)
            tile, band = code // bands, code % bands
            before = jnp.maximum(codes[jnp.maximum(slot - 1, 0)], 0) // bands
            place = jnp.where(used, band, bands)
            slot_bands[0, slot] = place
            slot_bands[1, slot] = jnp.where(used, tile, all_tiles)
            slot_bands[2, slot] = (used & (before == tile)).astype(jnp.int32)
            here = pl.ds(slot, 1)
            row = jnp.zeros((1, LANES), jnp.float32)
            start = row + (band * BAND).astype(jnp.float32)
            shift = row + (offset[0, tile].astype(jnp.float32) + frac[0, tile])
            inverse = 1.0 / (row + zoom[0, tile] * ratio)
            slope = jnp.broadcast_to(inverse, (BAND, LANES))
            first = (start - shift) * inverse
            slot_lines[0, here, :] = inverse
            slot_lines[1, here, :] = first
            slot_lines[2, here, :] = coords(start, frame)
            cover = cover_of(spots_along((BAND, LANES), 0) * slope + first, source)
            columns = col_cover[pl.ds(tile, 1), :]
            for half in range(frame // LANES):
                part = slice(half * LANES, (half + 1) * LANES)
                cover_sum[place, :, part] += cover * columns[:, part]


def payload_lanes(tiles, devices):
    return pl.cdiv(2 * tiles * devices + 6 * tiles, LANES) * LANES


def moment_kernel(sizes, zoom, frac, offset, frames, base, parts):
    tiles, bands, frame, source, capacity, devices = sizes
    me = lax.axis_index("tile")
    all_tiles = tiles * devices
    ratio = frame / source
    parts[...] = jnp.zeros_like(parts)
    for j in range(tiles):
        tile = me * tiles + j
        spots = spots_along((frame, frame), 0)
        y = coords(spots, frame)
        cover = cover_of(points_of(spots, zoom, frac, offset, 0, tile, ratio), source)
        level = frames[j * bands : (j + 1) * bands].reshape(frame, frame).astype(jnp.float32)
        columns = points_of(spots_along((1, frame), 1), zoom, frac, offset, 1, tile, ratio)
        columns = cover_of(columns, source)
        weighted = (cover, cover * y, cover * y * y)
        for power, image in enumerate((None, level, level * level)):
            sums = [
                columns * jnp.sum(rows if image is None else rows * image, axis=0, keepdims=True)
                for rows in weighted
            ]
            for k, (half, a, _) in enumerate(MOMENT_ROWS):
                place = 2 * all_tiles + tiles * (2 * power + half) + j
                parts[k, place : place + 1, :] = sums[a]
    total = 0.0
    for k, (_, _, wanted) in enumerate(MOMENT_ROWS):
        total += exact_dot(feature_rows(frame, wanted), parts[k])
    base[...] = total[:PAYLOAD_ROWS]


def add_blocks(sizes, chosen, slot_bands, col_cover, blocks, whole, total):
    tiles, bands, frame, source, capacity, devices = sizes
    whole = iter(whole)
    for (block, distance), values in zip(chosen, blocks):
        packed = is_packed(capacity, devices, distance)
        if packed:
            unpacked, levels = next(whole), unpack_block(values)
        for k in range(capacity):
            slot = block * capacity + k
            columns = col_cover[pl.ds(slot_bands[1, slot], 1), :]
            for half in range(frame // LANES):
                part = slice(half * LANES, (half + 1) * LANES)
                level = levels[k][half] if packed else values[k, :, part].astype(jnp.float32)
                if packed or half == 0:
                    level = jnp.where(columns[:, part] > 0.0, level, 0.0)
                total[slot_bands[0, slot], :, part] += level
                if packed:
                    unpacked[k, :, part] = level.astype(jnp.bfloat16)


def first_blend_kernel(sizes, chosen, slot_bands, col_cover, *refs):
    blocks, (total, *whole) = refs[: len(chosen)], refs[len(chosen) :]
    total[...] = jnp.zeros_like(total)
    add_blocks(sizes, chosen, slot_bands, col_cover, blocks, whole, total)


def last_blend_kernel(sizes, chosen, slot_bands, col_cover, cover_sum, before, *refs):
    bands = sizes[1]
    blocks, (grid, *whole, total) = refs[: len(chosen)], refs[len(chosen) :]
    total[...] = before[...]
    add_blocks(sizes, chosen, slot_bands, col_cover, blocks, whole, total)
    grid[...] = (total[:bands] / (1.0 + cover_sum[:bands])).astype(jnp.bfloat16)


GRADIENT_ROWS = ({0: 0, 1: 1}, {2: 0}, {3: 0, 4: 1}, {5: 0})


def gradient_kernel(
    sizes, slot_bands, from_next, top_grid, col_cover, slot_lines, base, grid, *blocks_and_rest
):
    tiles, bands, frame, source, capacity, devices = sizes
    *blocks, payload, grid_out, above, sums, grid_sem = blocks_and_rest
    written = pltpu.make_async_copy(grid, grid_out, grid_sem)
    written.start()
    sec = lax.axis_index("sec")
    all_tiles = tiles * devices

    @pl.when(sec == lax.axis_size("sec") - 1)
    def _():
        above[:bands] = top_grid[...].astype(jnp.float32)

    @pl.when(sec != lax.axis_size("sec") - 1)
    def _():
        above[:bands] = from_next[...].astype(jnp.float32)

    above[bands] = jnp.zeros((BAND, frame), jnp.float32)
    sums[...] = jnp.zeros_like(sums)
    spots = spots_along((BAND, LANES), 0)
    raised = spots * (2.0 / frame)
    halves = range(frame // LANES)

    for block, (array, _) in enumerate(exchange_plan(devices)[1]):
        running = None
        for k in range(capacity):
            slot = block * capacity + k
            here = slice(slot, slot + 1)
            points = spots * slot_lines[0, here] + slot_lines[1, here]
            cover = cover_of(points, source)
            lifted = cover * (raised + slot_lines[2, here])
            level = blocks[array][k].astype(jnp.float32)
            error = above[slot_bands[0, slot]] - level
            product = error * level
            terms = []
            for half in halves:
                part = slice(half * LANES, (half + 1) * LANES)
                for weight, value in (
                    (cover, error),
                    (lifted, error),
                    (cover, product),
                    (lifted, product),
                ):
                    term = weight * value[:, part]
                    terms.append(term[:ROWS] + term[ROWS:])
            if running is not None:
                same = slot_bands[2, slot] == 1
                terms = [
                    term + jnp.where(same, before, 0.0) for term, before in zip(terms, running)
                ]
            running = terms
            rows = pl.ds(pl.multiple_of(slot_bands[1, slot] * ROWS, ROWS), ROWS)
            for index, term in enumerate(terms):
                sums[index, rows, :] = term

    values = [jnp.zeros((all_tiles, 1), jnp.float32)] * 6
    for half in halves:
        columns = col_cover[:all_tiles, half * LANES : (half + 1) * LANES]
        x = coords(spots_along((all_tiles, LANES), 1, half * LANES), frame)
        for kind, wanted in enumerate(GRADIENT_ROWS):
            index = half * len(GRADIENT_ROWS) + kind
            value = sums[index, pl.ds(0, all_tiles, stride=ROWS), :]
            for r in range(1, ROWS):
                value += sums[index, pl.ds(r, all_tiles, stride=ROWS), :]
            value = value * columns
            for row, power in wanted.items():
                term = value * x if power else value
                values[row] += jnp.sum(term, axis=1, keepdims=True)
    total = []
    tile = lax.broadcasted_iota(jnp.int32, (all_tiles, LANES), 0)
    for start in range(0, base.shape[1], LANES):
        lane = lax.broadcasted_iota(jnp.int32, (all_tiles, LANES), 1) + start
        placed = [
            sum(jnp.where(lane == tile + k * all_tiles, values[3 * k + r], 0.0) for k in range(2))
            for r in range(3)
        ]
        rows = [jnp.sum(value, axis=0, keepdims=True) for value in placed]
        total.append(jnp.concatenate(rows + [jnp.zeros_like(rows[0])], axis=0))
    total = base[...] + jnp.concatenate(total, axis=1)
    payload[...] = jnp.broadcast_to(total[None], payload.shape)
    written.wait()


def solve_kernel(sizes, received, corrections):
    tiles, bands, frame, source, capacity, devices = sizes
    sec, me = lax.axis_index("sec"), lax.axis_index("tile")
    sections = lax.axis_size("sec")
    all_tiles = tiles * devices
    lanes = sections * all_tiles
    lane = lax.broadcasted_iota(jnp.int32, (ROWS, lanes), 1)
    within = lane % all_tiles
    area = frame * frame

    width = max(lanes, received.shape[2])

    def rolled(value, shift):
        return pltpu.roll(value, shift % width, 1)

    def fetched(source):
        value = received[source]
        if value.shape[1] < width:
            value = jnp.pad(value, ((0, 0), (0, width - value.shape[1])))
        return jnp.concatenate([value, rolled(value, width - tiles)], axis=0)

    wide = lax.broadcasted_iota(jnp.int32, (ROWS, width), 1)
    gradients = [jnp.zeros((ROWS, width), jnp.float32)] * 2
    moments = [jnp.zeros((ROWS, width), jnp.float32)] * 3
    for s in range(sections):

        def gather(t, carry):
            own, *moments = carry
            value = fetched(s * devices + t)
            place = s * all_tiles + t * tiles
            here = (wide >= place) & (wide < place + tiles)
            for power in range(3):
                start = 2 * all_tiles + 2 * power * tiles
                moment = rolled(value, place - start + 2 * width)
                moments[power] = jnp.where(here, moment, moments[power])
            return (own + value, *moments)

        carry = (jnp.zeros((ROWS, width), jnp.float32), *moments)
        if devices <= 8:
            for t in range(devices):
                carry = gather(t, carry)
        else:
            carry = lax.fori_loop(0, devices, gather, carry)
        own, *moments = carry
        here = wide // all_tiles == s
        for k in range(2):
            part = rolled(own, (s - k) * all_tiles)
            gradients[k] = jnp.where(here, part, gradients[k])
    gradients = [value[:, :lanes] * (1.0 / area) for value in gradients]
    moments = [value[:, :lanes] * (1.0 / area) for value in moments]

    where = ((0, 1, 2), (1, 4, 5), (2, 5, 6))
    row = lax.broadcasted_iota(jnp.int32, (ROWS, lanes), 0)

    def entry(f, g):
        kind = moments[(f >= 3) + (g >= 3)]
        index = where[f % 3][g % 3]
        return kind[index : index + 1]

    def stacked(rows):
        result = jnp.zeros((ROWS, lanes), jnp.float32)
        for f, value in enumerate(rows):
            result = jnp.where(row == f, value, result)
        return result

    normal = [stacked([entry(f, g) for f in range(6)]) for g in range(6)]
    diagonal = stacked([entry(f, f) for f in range(6)])
    gradients = stacked([gradients[f // 3][f % 3 : f % 3 + 1] for f in range(6)])
    precond = 1.0 / (diagonal + 4.0 * COUPLING)

    def total(values):
        return jnp.sum(jnp.sum(values, axis=1, keepdims=True), axis=0, keepdims=True)

    def operator(vector):
        beside = jnp.where(within < all_tiles - 1, pltpu.roll(vector, lanes - 1, 1), 0.0)
        beside += jnp.where(within > 0, pltpu.roll(vector, 1, 1), 0.0)
        upward = pltpu.roll(vector, lanes - all_tiles, 1)
        beside += jnp.where(lane < lanes - all_tiles, upward, 0.0)
        beside += jnp.where(lane >= all_tiles, pltpu.roll(vector, all_tiles, 1), 0.0)
        image = COUPLING * (4.0 * vector - beside)
        for g in range(6):
            image += normal[g] * vector[g : g + 1]
        return image

    answer = jnp.zeros((ROWS, lanes), jnp.float32)
    residual = gradients
    scaled = precond * residual
    direction = scaled
    current = total(residual * scaled)
    for step in range(ITERS):
        image = operator(direction)
        alpha = current / total(direction * image)
        answer = answer + alpha * direction
        if step + 1 < ITERS:
            residual = residual - alpha * image
            scaled = precond * residual
            following = total(residual * scaled)
            direction = scaled + following / current * direction
            current = following

    first = sec * all_tiles + me * tiles
    chosen = (row + first == lane).astype(jnp.float32)
    place = lax.broadcasted_iota(jnp.int32, (ROWS, LANES), 1)
    own = jnp.zeros((ROWS, LANES), jnp.float32)
    for f in range(6):
        value = jnp.sum(chosen * answer[f : f + 1], axis=1, keepdims=True)
        own = jnp.where(place == f, value, own)
    corrections[...] = own[:tiles, :6]


def shards(patches, zoom, frac, offset, owner, top_grid):
    _, tiles, source, _ = patches.shape
    frame = top_grid.shape[1]
    devices, sections = lax.axis_size("tile"), lax.axis_size("sec")
    bands = frame // BAND
    capacity = max(2, 2 * tiles * bands // devices)
    slots = devices * capacity
    all_tiles = tiles * devices
    width = payload_lanes(tiles, devices)
    sizes = (tiles, bands, frame, source, capacity, devices)
    place = (zoom[0], frac[0], offset[0])
    routes = jnp.transpose(owner, (0, 2, 3, 1))[0]

    rows = tiles * bands
    plan, arriving = exchange_plan(devices)
    blocks = [
        jax.ShapeDtypeStruct(
            (len(group) * PACKED, BAND, LANES)
            if is_packed(capacity, devices, group[0])
            else (len(group) * capacity, BAND, frame),
            jnp.bfloat16,
        )
        for group in plan
    ]
    frames, *outgoing = pl.pallas_call(
        functools.partial(render_kernel, sizes),
        name="render",
        in_specs=[HBM] * 5,
        out_specs=[VMEM] * (1 + len(plan)),
        out_shape=[jax.ShapeDtypeStruct((rows, BAND, frame), jnp.bfloat16)] + blocks,
        scratch_shapes=[
            pltpu.SMEM(place[0].shape, jnp.float32),
            pltpu.SMEM(place[1].shape, jnp.float32),
            pltpu.SMEM(place[2].shape, jnp.int32),
            pltpu.SMEM(routes.shape, jnp.int32),
            pltpu.VMEM((tiles, source, source), jnp.bfloat16),
            pltpu.SMEM((devices,), jnp.int32),
            pltpu.SMEM((slots,), jnp.int32),
            pltpu.SemaphoreType.DMA((4,)),
            pltpu.SemaphoreType.DMA((tiles,)),
        ],
        compiler_params=params(24),
        cost_estimate=cost(800_000_000, 4 << 20),
    )(*(pltpu.with_memory_space_constraint(x, pltpu.HBM) for x in (*place, routes, patches[0])))

    base = pl.pallas_call(
        functools.partial(moment_kernel, sizes),
        name="moments",
        in_specs=[SMEM] * 3 + [VMEM],
        out_specs=VMEM,
        out_shape=jax.ShapeDtypeStruct((PAYLOAD_ROWS, width), jnp.float32),
        scratch_shapes=[pltpu.VMEM((len(MOMENT_ROWS), width, frame), jnp.float32)],
        compiler_params=params(24),
        cost_estimate=cost(20_000_000, 1 << 20),
    )(*place, frames)

    codes = pl.pallas_call(
        functools.partial(scan_kernel, sizes),
        name="scan",
        in_specs=[SMEM],
        out_specs=SMEM,
        out_shape=jax.ShapeDtypeStruct((slots + 1,), jnp.int32),
        compiler_params=params(24),
        cost_estimate=cost(20_000_000, 1 << 20),
    )(routes)

    cover_sum, col_cover, slot_lines, slot_bands = pl.pallas_call(
        functools.partial(slot_kernel, sizes),
        name="slots",
        in_specs=[SMEM] * 4,
        out_specs=[VMEM] * 3 + [SMEM],
        out_shape=[
            jax.ShapeDtypeStruct((bands + 1, BAND, frame), jnp.float32),
            jax.ShapeDtypeStruct((all_tiles + ROWS, frame), jnp.float32),
            jax.ShapeDtypeStruct((3, slots, LANES), jnp.float32),
            pltpu.SMEM((3, slots), jnp.int32),
        ],
        compiler_params=params(24),
        cost_estimate=cost(20_000_000, 1 << 20),
    )(*place, codes)

    def swapped(block, distance):
        return lax.ppermute(block, "tile", [(i, i ^ distance) for i in range(devices)])

    incoming = [outgoing[0]]
    for block, group in zip(outgoing[1:], plan[1:]):
        incoming.append(swapped(block, group[0]))
        if len(group) == 2:
            passed_on = incoming[-1][incoming[-1].shape[0] // 2 :]
    if devices == 8:
        incoming.append(swapped(passed_on, 1))

    slot_bands = pltpu.with_memory_space_constraint(slot_bands, pltpu.SMEM)
    total = jax.ShapeDtypeStruct((bands + 1, BAND, frame), jnp.float32)

    def blend(kernel, name, chosen, results, scratch, *operands):
        distances = [(block, arriving[block][1]) for block in chosen]
        arrays = [arriving[block][0] for block in chosen]
        packed = [
            array
            for array, (_, distance) in zip(arrays, distances)
            if is_packed(capacity, devices, distance)
        ]
        whole = jax.ShapeDtypeStruct((capacity, BAND, frame), jnp.bfloat16)
        result, *unpacked = pl.pallas_call(
            functools.partial(kernel, sizes, distances),
            name=name,
            in_specs=[SMEM] + [VMEM] * (len(operands) + len(chosen)),
            out_specs=[VMEM] * (1 + len(packed)),
            out_shape=[results] + [whole] * len(packed),
            scratch_shapes=scratch,
            compiler_params=params(24),
            cost_estimate=cost(1_000_000, 2 << 20),
        )(slot_bands, *operands, *(incoming[array] for array in arrays))
        for array, block in zip(packed, unpacked):
            incoming[array] = block
        return result

    last = [5] if devices == 8 else range(devices - devices // 4, devices)
    early = [block for block in range(devices) if block not in last]
    before = blend(first_blend_kernel, "first_blend", early, total, [], col_cover)
    grid = blend(
        last_blend_kernel,
        "last_blend",
        last,
        jax.ShapeDtypeStruct((bands, BAND, frame), jnp.bfloat16),
        [pltpu.VMEM(total.shape, total.dtype)],
        col_cover,
        cover_sum,
        before,
    )

    from_next = lax.ppermute(grid, "sec", [(i, (i - 1) % sections) for i in range(sections)])

    payload, grid_out = pl.pallas_call(
        functools.partial(gradient_kernel, sizes),
        name="gradient",
        in_specs=[SMEM] + [VMEM] * (6 + len(incoming)),
        out_specs=[VMEM, HBM],
        out_shape=[
            jax.ShapeDtypeStruct((sections * devices, PAYLOAD_ROWS, width), jnp.float32),
            jax.ShapeDtypeStruct((bands, BAND, frame), jnp.bfloat16),
        ],
        scratch_shapes=[
            pltpu.VMEM((bands + 1, BAND, frame), jnp.float32),
            pltpu.VMEM((4 * frame // LANES, (all_tiles + 1) * ROWS, LANES), jnp.float32),
            pltpu.SemaphoreType.DMA,
        ],
        compiler_params=params(24),
        cost_estimate=cost(8_000_000, 2 << 20),
    )(
        slot_bands,
        from_next,
        top_grid.reshape(bands, BAND, frame),
        col_cover,
        slot_lines,
        base,
        grid,
        *incoming,
    )

    received = lax.all_to_all(
        payload, ("sec", "tile"), split_axis=0, concat_axis=0, tiled=True
    )

    corrections = pl.pallas_call(
        functools.partial(solve_kernel, sizes),
        name="solve",
        in_specs=[VMEM],
        out_specs=VMEM,
        out_shape=jax.ShapeDtypeStruct((tiles, 6), jnp.float32),
        compiler_params=params(24),
        cost_estimate=cost(100_000, 1 << 18),
    )(received)
    return (
        grid_out.reshape(1, 1, frame, frame),
        jnp.transpose(corrections[None], (2, 0, 1)),
    )


def solution(mesh):
    placed = (
        P("sec", "tile", None, None),
        P("sec", None, None),
        P("sec", None, None),
        P("sec", None, None),
        P("sec", None, None, None),
        P("tile", None, None),
    )
    return jax.shard_map(
        shards,
        mesh=mesh,
        in_specs=placed,
        out_specs=(P("sec", "tile", None, None), P(None, "sec", "tile")),
        check_vma=False,
    )
```

```python
import functools
import math

import jax
import jax.numpy as jnp
from jax import lax
from jax.experimental import pallas as pl
from jax.experimental.pallas import tpu as pltpu
from jax.sharding import PartitionSpec as P

BAND = 16
ITERS = 2
COUPLING = 0.25
LANES = 128
ROWS = 8
SPARE = 24
PACKED = 29
HBM = pl.BlockSpec(memory_space=pltpu.HBM)
SMEM = pl.BlockSpec(memory_space=pltpu.SMEM)
VMEM = pl.BlockSpec(memory_space=pltpu.VMEM)


def params(mebibytes):
    return pltpu.CompilerParams(vmem_limit_bytes=mebibytes * 1024 * 1024)


def cost(flops, size):
    return pl.CostEstimate(flops=flops, bytes_accessed=size, transcendentals=0)


def exact_dot(left, right):
    return lax.dot_general(
        left,
        right,
        (((1,), (1,)), ((), ())),
        precision=lax.Precision.HIGHEST,
        preferred_element_type=jnp.float32,
    )


def points_of(spots, zoom, frac, offset, axis, tile, ratio):
    scale = zoom[axis, tile] * ratio
    return (spots - offset[axis, tile].astype(jnp.float32) - frac[axis, tile]) / scale


def cover_of(points, source):
    return jnp.clip(jnp.minimum(points + 1.0, source - points), 0.0, 1.0)


def hat_weight(distance):
    return jnp.maximum(0.0, 1.0 - jnp.abs(distance))


def spots_along(shape, dim, start=0):
    return (lax.broadcasted_iota(jnp.int32, shape, dim) + start).astype(jnp.float32)


def coords(spots, frame):
    return (spots - (frame - 1) / 2.0) / (frame / 2.0)


def exchange_plan(devices):
    if devices == 8:
        outgoing = [[0], [2, 3], [4], [5], [6], [7], [1]]
        return outgoing, [(0, 0), (1, 2), (2, 4), (3, 5), (4, 6), (5, 7), (6, 1), (7, 3)]
    return [[d] for d in range(devices)], [(d, d) for d in range(devices)]


def is_packed(capacity, devices, distance):
    return devices == 8 and capacity == 16 and distance > 0


def spare_pieces():
    kept = LANES - SPARE
    pieces = [(4 * i + c, kept, 13 + i, SPARE * c, SPARE) for i in range(3) for c in range(4)]
    return pieces + [(12, kept + 8 * i, 13 + i, 4 * SPARE, 8) for i in range(3)]


def moved(value, start, goal):
    shift = (goal - start) % LANES
    return pltpu.roll(value, shift, 1) if shift else value


def lane_window(start, count):
    lane = lax.broadcasted_iota(jnp.int32, (BAND, LANES), 1)
    return (lane >= start) & (lane < start + count)


def pack_block(there, start, firsts, seconds):
    for k in range(16):
        there[start + k] = firsts(k)
    values = [seconds(k).astype(jnp.float32) for k in range(16)]
    for slot, lane, donor, goal, count in spare_pieces():
        values[slot] = jnp.where(
            lane_window(lane, count), moved(values[donor], goal, lane), values[slot]
        )
    for k in range(13):
        there[start + 16 + k] = values[k].astype(jnp.bfloat16)


def unpack_block(block):
    firsts = [block[k].astype(jnp.float32) for k in range(16)]
    seconds = [block[16 + k].astype(jnp.float32) for k in range(13)]
    seconds += [jnp.zeros((BAND, LANES), jnp.float32)] * 3
    for slot, lane, donor, start, count in spare_pieces():
        seconds[donor] = jnp.where(
            lane_window(start, count), moved(seconds[slot], lane, start), seconds[donor]
        )
    kept = lane_window(0, LANES - SPARE)
    seconds = [
        jnp.where(kept, second, moved(first, 0, LANES - SPARE))
        for first, second in zip(firsts, seconds)
    ]
    return list(zip(firsts, seconds))


def render_kernel(
    sizes, zoom_in, frac_in, offset_in, owner_in, patches_in, frames, *outgoing_and_scratch
):
    tiles, bands, frame, source, capacity, devices = sizes
    plan, _ = exchange_plan(devices)
    outgoing = outgoing_and_scratch[: len(plan)]
    zoom, frac, offset, owner, patches, named, rows, small_sems, patch_sems = (
        outgoing_and_scratch[len(plan) :]
    )
    me = lax.axis_index("tile")
    first_tile = me * tiles
    ratio = frame / source
    fetched = [
        pltpu.make_async_copy(patches_in.at[j], patches.at[j], patch_sems.at[j])
        for j in range(tiles)
    ]
    small = [
        pltpu.make_async_copy(there, here, small_sems.at[k])
        for k, (there, here) in enumerate(
            ((zoom_in, zoom), (frac_in, frac), (offset_in, offset), (owner_in, owner))
        )
    ]
    for copy in small + fetched:
        copy.start()
    for g in range(devices):
        named[g] = 0
    for slot in range(devices * capacity):
        rows[slot] = 0
    for copy in small:
        copy.wait()
    for j in range(tiles):
        tile = first_tile + j
        row_points = points_of(spots_along((frame, LANES), 0), zoom, frac, offset, 0, tile, ratio)
        row_weights = jnp.concatenate(
            [
                hat_weight(row_points - spots_along((frame, LANES), 1, p)).astype(jnp.bfloat16)
                for p in range(0, source, LANES)
            ],
            axis=1,
        )
        col_points = points_of(spots_along((ROWS, frame), 1), zoom, frac, offset, 1, tile, ratio)
        over = moved(col_points[:, frame - LANES :], LANES - SPARE, 0)
        lane = lax.broadcasted_iota(jnp.int32, over.shape, 1)
        folded = (lane < SPARE) & (cover_of(over, source) > 0.0)
        col_points = jnp.concatenate(
            [jnp.where(folded, over, col_points[:, :LANES]), col_points[:, LANES:]], axis=1
        )
        col_points = jnp.broadcast_to(col_points[:1], (source, frame))
        col_weights = hat_weight(col_points - spots_along((source, frame), 0)).astype(jnp.bfloat16)
        fetched[j].wait()
        half, quarter = source // 2, frame // 4
        upper = jnp.dot(
            row_weights[: 3 * quarter, :half],
            patches[j, :half],
            preferred_element_type=jnp.float32,
        )
        lower = jnp.dot(
            row_weights[quarter:, half:],
            patches[j, half:],
            preferred_element_type=jnp.float32,
        )
        halfway = jnp.concatenate(
            [upper[:quarter], upper[quarter:] + lower[: 2 * quarter], lower[2 * quarter :]]
        )
        rendered = jnp.dot(
            halfway.astype(jnp.bfloat16), col_weights, preferred_element_type=jnp.float32
        ).astype(jnp.bfloat16)
        frames[j * bands : (j + 1) * bands] = rendered.reshape(bands, BAND, frame)
        for band in range(bands):
            target = owner[band, 0, tile]
            slot = named[target]
            named[target] = slot + 1
            rows[target * capacity + slot] = j * bands + band
    for there, group in zip(outgoing, plan):
        for position, distance in enumerate(group):
            target = me ^ distance
            if is_packed(capacity, devices, distance):
                taken = [rows[target * capacity + slot] for slot in range(capacity)]
                pack_block(
                    there,
                    PACKED * position,
                    lambda k: frames[taken[k], :, :LANES],
                    lambda k: frames[taken[k], :, LANES:],
                )
                continue
            for slot in range(capacity):
                there[position * capacity + slot] = frames[rows[target * capacity + slot]]


def feature_rows(frame, wanted):
    shape = (ROWS, frame)
    x = coords(spots_along(shape, 1), frame)
    row = lax.broadcasted_iota(jnp.int32, shape, 0)
    rows = jnp.zeros(shape, jnp.float32)
    for r, power in wanted.items():
        rows = jnp.where(row == r, (jnp.ones_like(x), x, x * x)[power], rows)
    return rows


MOMENT_ROWS = ((0, 0, {0: 0, 1: 1}), (0, 1, {2: 0}), (1, 0, {0: 2}), (1, 1, {1: 1}), (1, 2, {2: 0}))
PAYLOAD_ROWS = 4


def scan_kernel(sizes, owner, codes):
    tiles, bands, frame, source, capacity, devices = sizes
    me = lax.axis_index("tile")

    def scan(block, distance):
        count = 0
        for j in range(tiles):
            tile = (me ^ distance) * tiles + j
            named = [owner[band, 0, tile] for band in range(bands)]
            for band in range(bands):
                codes[block * capacity + count] = tile * bands + band
                count += (named[band] == me).astype(jnp.int32)

        def blank(position, carry):
            codes[block * capacity + position] = -1
            return carry

        lax.fori_loop(count, capacity, blank, 0)

    arriving = exchange_plan(devices)[1]
    if devices == 8:
        for block, (_, distance) in enumerate(arriving):
            scan(block, distance)
    else:
        pl.loop(0, devices)(lambda block: scan(block, block))


def slot_kernel(
    sizes, zoom, frac, offset, codes, cover_sum, col_cover, slot_lines, slot_bands
):
    tiles, bands, frame, source, capacity, devices = sizes
    slots = devices * capacity
    all_tiles = tiles * devices
    ratio = frame / source

    @pl.loop(0, all_tiles // ROWS)
    def _(group):
        for k in range(ROWS):
            tile = group * ROWS + k
            points = points_of(spots_along((1, frame), 1), zoom, frac, offset, 1, tile, ratio)
            col_cover[pl.ds(tile, 1), :] = cover_of(points, source)

    col_cover[all_tiles:] = jnp.zeros((ROWS, frame), jnp.float32)
    cover_sum[...] = jnp.zeros_like(cover_sum)
    unroll = math.gcd(slots, ROWS)

    @pl.loop(0, slots // unroll)
    def _(group):
        for k in range(unroll):
            slot = group * unroll + k
            used = codes[slot] >= 0
            code = jnp.maximum(codes[slot], 0)
            tile, band = code // bands, code % bands
            before = jnp.maximum(codes[jnp.maximum(slot - 1, 0)], 0) // bands
            place = jnp.where(used, band, bands)
            slot_bands[0, slot] = place
            slot_bands[1, slot] = jnp.where(used, tile, all_tiles)
            slot_bands[2, slot] = (used & (before == tile)).astype(jnp.int32)
            here = pl.ds(slot, 1)
            row = jnp.zeros((1, LANES), jnp.float32)
            start = row + (band * BAND).astype(jnp.float32)
            shift = row + (offset[0, tile].astype(jnp.float32) + frac[0, tile])
            inverse = 1.0 / (row + zoom[0, tile] * ratio)
            slope = jnp.broadcast_to(inverse, (BAND, LANES))
            first = (start - shift) * inverse
            slot_lines[0, here, :] = inverse
            slot_lines[1, here, :] = first
            slot_lines[2, here, :] = coords(start, frame)
            cover = cover_of(spots_along((BAND, LANES), 0) * slope + first, source)
            columns = col_cover[pl.ds(tile, 1), :]
            for half in range(frame // LANES):
                part = slice(half * LANES, (half + 1) * LANES)
                cover_sum[place, :, part] += cover * columns[:, part]


def payload_lanes(tiles, devices):
    return pl.cdiv(2 * tiles * devices + 6 * tiles, LANES) * LANES


def moment_kernel(sizes, zoom, frac, offset, frames, base, parts):
    tiles, bands, frame, source, capacity, devices = sizes
    me = lax.axis_index("tile")
    all_tiles = tiles * devices
    ratio = frame / source
    parts[...] = jnp.zeros_like(parts)
    for j in range(tiles):
        tile = me * tiles + j
        spots = spots_along((frame, frame), 0)
        y = coords(spots, frame)
        cover = cover_of(points_of(spots, zoom, frac, offset, 0, tile, ratio), source)
        level = frames[j * bands : (j + 1) * bands].reshape(frame, frame).astype(jnp.float32)
        columns = points_of(spots_along((1, frame), 1), zoom, frac, offset, 1, tile, ratio)
        columns = cover_of(columns, source)
        weighted = (cover, cover * y, cover * y * y)
        for power, image in enumerate((None, level, level * level)):
            sums = [
                columns * jnp.sum(rows if image is None else rows * image, axis=0, keepdims=True)
                for rows in weighted
            ]
            for k, (half, a, _) in enumerate(MOMENT_ROWS):
                place = 2 * all_tiles + tiles * (2 * power + half) + j
                parts[k, place : place + 1, :] = sums[a]
    total = 0.0
    for k, (_, _, wanted) in enumerate(MOMENT_ROWS):
        total += exact_dot(feature_rows(frame, wanted), parts[k])
    base[...] = total[:PAYLOAD_ROWS]


def add_blocks(sizes, chosen, slot_bands, col_cover, blocks, whole, total):
    tiles, bands, frame, source, capacity, devices = sizes
    whole = iter(whole)
    for (block, distance), values in zip(chosen, blocks):
        packed = is_packed(capacity, devices, distance)
        if packed:
            unpacked, levels = next(whole), unpack_block(values)
        for k in range(capacity):
            slot = block * capacity + k
            columns = col_cover[pl.ds(slot_bands[1, slot], 1), :]
            for half in range(frame // LANES):
                part = slice(half * LANES, (half + 1) * LANES)
                level = levels[k][half] if packed else values[k, :, part].astype(jnp.float32)
                if packed or half == 0:
                    level = jnp.where(columns[:, part] > 0.0, level, 0.0)
                total[slot_bands[0, slot], :, part] += level
                if packed:
                    unpacked[k, :, part] = level.astype(jnp.bfloat16)


def first_blend_kernel(sizes, chosen, slot_bands, col_cover, *refs):
    blocks, (total, *whole) = refs[: len(chosen)], refs[len(chosen) :]
    total[...] = jnp.zeros_like(total)
    add_blocks(sizes, chosen, slot_bands, col_cover, blocks, whole, total)


def last_blend_kernel(sizes, chosen, slot_bands, col_cover, cover_sum, before, *refs):
    bands = sizes[1]
    blocks, (grid, *whole, total) = refs[: len(chosen)], refs[len(chosen) :]
    total[...] = before[...]
    add_blocks(sizes, chosen, slot_bands, col_cover, blocks, whole, total)
    grid[...] = (total[:bands] / (1.0 + cover_sum[:bands])).astype(jnp.bfloat16)


def weight_kernel(sizes, slot_lines, weights, sums):
    tiles, bands, frame, source, capacity, devices = sizes
    sums[...] = jnp.zeros_like(sums)
    spots = spots_along((BAND, LANES), 0)
    raised = spots * (2.0 / frame)

    @pl.loop(0, devices * capacity // ROWS)
    def _(group):
        for k in range(ROWS):
            slot = group * ROWS + k
            here = pl.ds(slot, 1)
            cover = cover_of(spots * slot_lines[0, here, :] + slot_lines[1, here, :], source)
            weights[0, slot] = cover
            weights[1, slot] = cover * (raised + slot_lines[2, here, :])


GRADIENT_ROWS = ({0: 0, 1: 1}, {2: 0}, {3: 0, 4: 1}, {5: 0})


def gradient_kernel(
    sizes, slot_bands, from_next, top_grid, col_cover, weights, _, base, grid, *blocks_and_rest
):
    tiles, bands, frame, source, capacity, devices = sizes
    *blocks, payload, grid_out, sums, above, grid_sem = blocks_and_rest
    written = pltpu.make_async_copy(grid, grid_out, grid_sem)
    written.start()
    sec = lax.axis_index("sec")
    all_tiles = tiles * devices

    @pl.when(sec == lax.axis_size("sec") - 1)
    def _():
        above[:bands] = top_grid[...].astype(jnp.float32)

    @pl.when(sec != lax.axis_size("sec") - 1)
    def _():
        above[:bands] = from_next[...].astype(jnp.float32)

    above[bands] = jnp.zeros((BAND, frame), jnp.float32)
    halves = range(frame // LANES)

    for block, (array, _) in enumerate(exchange_plan(devices)[1]):
        running = None
        for k in range(capacity):
            slot = block * capacity + k
            cover, lifted = weights[0, slot], weights[1, slot]
            level = blocks[array][k].astype(jnp.float32)
            error = above[slot_bands[0, slot]] - level
            product = error * level
            terms = []
            for half in halves:
                part = slice(half * LANES, (half + 1) * LANES)
                for weight, value in (
                    (cover, error),
                    (lifted, error),
                    (cover, product),
                    (lifted, product),
                ):
                    term = weight * value[:, part]
                    terms.append(term[:ROWS] + term[ROWS:])
            if running is not None:
                same = slot_bands[2, slot] == 1
                terms = [
                    term + jnp.where(same, before, 0.0) for term, before in zip(terms, running)
                ]
            running = terms
            rows = pl.ds(pl.multiple_of(slot_bands[1, slot] * ROWS, ROWS), ROWS)
            for index, term in enumerate(terms):
                sums[index, rows, :] = term

    values = [jnp.zeros((all_tiles, 1), jnp.float32)] * 6
    for half in halves:
        columns = col_cover[:all_tiles, half * LANES : (half + 1) * LANES]
        x = coords(spots_along((all_tiles, LANES), 1, half * LANES), frame)
        for kind, wanted in enumerate(GRADIENT_ROWS):
            index = half * len(GRADIENT_ROWS) + kind
            value = sums[index, pl.ds(0, all_tiles, stride=ROWS), :]
            for r in range(1, ROWS):
                value += sums[index, pl.ds(r, all_tiles, stride=ROWS), :]
            value = value * columns
            for row, power in wanted.items():
                term = value * x if power else value
                values[row] += jnp.sum(term, axis=1, keepdims=True)
    total = []
    tile = lax.broadcasted_iota(jnp.int32, (all_tiles, LANES), 0)
    for start in range(0, base.shape[1], LANES):
        lane = lax.broadcasted_iota(jnp.int32, (all_tiles, LANES), 1) + start
        placed = [
            sum(jnp.where(lane == tile + k * all_tiles, values[3 * k + r], 0.0) for k in range(2))
            for r in range(3)
        ]
        rows = [jnp.sum(value, axis=0, keepdims=True) for value in placed]
        total.append(jnp.concatenate(rows + [jnp.zeros_like(rows[0])], axis=0))
    total = base[...] + jnp.concatenate(total, axis=1)
    payload[...] = jnp.broadcast_to(total[None], payload.shape)
    written.wait()


def solve_kernel(sizes, received, corrections):
    tiles, bands, frame, source, capacity, devices = sizes
    sec, me = lax.axis_index("sec"), lax.axis_index("tile")
    sections = lax.axis_size("sec")
    all_tiles = tiles * devices
    lanes = sections * all_tiles
    lane = lax.broadcasted_iota(jnp.int32, (ROWS, lanes), 1)
    within = lane % all_tiles
    area = frame * frame

    width = max(lanes, received.shape[2])

    def rolled(value, shift):
        return pltpu.roll(value, shift % width, 1)

    def fetched(source):
        value = received[source]
        if value.shape[1] < width:
            value = jnp.pad(value, ((0, 0), (0, width - value.shape[1])))
        return jnp.concatenate([value, rolled(value, width - tiles)], axis=0)

    wide = lax.broadcasted_iota(jnp.int32, (ROWS, width), 1)
    gradients = [jnp.zeros((ROWS, width), jnp.float32)] * 2
    moments = [jnp.zeros((ROWS, width), jnp.float32)] * 3
    for s in range(sections):

        def gather(t, carry):
            own, *moments = carry
            value = fetched(s * devices + t)
            place = s * all_tiles + t * tiles
            here = (wide >= place) & (wide < place + tiles)
            for power in range(3):
                start = 2 * all_tiles + 2 * power * tiles
                moment = rolled(value, place - start + 2 * width)
                moments[power] = jnp.where(here, moment, moments[power])
            return (own + value, *moments)

        carry = (jnp.zeros((ROWS, width), jnp.float32), *moments)
        if devices <= 8:
            for t in range(devices):
                carry = gather(t, carry)
        else:
            carry = lax.fori_loop(0, devices, gather, carry)
        own, *moments = carry
        here = wide // all_tiles == s
        for k in range(2):
            part = rolled(own, (s - k) * all_tiles)
            gradients[k] = jnp.where(here, part, gradients[k])
    gradients = [value[:, :lanes] * (1.0 / area) for value in gradients]
    moments = [value[:, :lanes] * (1.0 / area) for value in moments]

    where = ((0, 1, 2), (1, 4, 5), (2, 5, 6))
    row = lax.broadcasted_iota(jnp.int32, (ROWS, lanes), 0)

    def entry(f, g):
        kind = moments[(f >= 3) + (g >= 3)]
        index = where[f % 3][g % 3]
        return kind[index : index + 1]

    def stacked(rows):
        result = jnp.zeros((ROWS, lanes), jnp.float32)
        for f, value in enumerate(rows):
            result = jnp.where(row == f, value, result)
        return result

    normal = [stacked([entry(f, g) for f in range(6)]) for g in range(6)]
    diagonal = stacked([entry(f, f) for f in range(6)])
    gradients = stacked([gradients[f // 3][f % 3 : f % 3 + 1] for f in range(6)])
    precond = 1.0 / (diagonal + 4.0 * COUPLING)

    def total(values):
        return jnp.sum(jnp.sum(values, axis=1, keepdims=True), axis=0, keepdims=True)

    def operator(vector):
        beside = jnp.where(within < all_tiles - 1, pltpu.roll(vector, lanes - 1, 1), 0.0)
        beside += jnp.where(within > 0, pltpu.roll(vector, 1, 1), 0.0)
        upward = pltpu.roll(vector, lanes - all_tiles, 1)
        beside += jnp.where(lane < lanes - all_tiles, upward, 0.0)
        beside += jnp.where(lane >= all_tiles, pltpu.roll(vector, all_tiles, 1), 0.0)
        image = COUPLING * (4.0 * vector - beside)
        for g in range(6):
            image += normal[g] * vector[g : g + 1]
        return image

    answer = jnp.zeros((ROWS, lanes), jnp.float32)
    residual = gradients
    scaled = precond * residual
    direction = scaled
    current = total(residual * scaled)
    for step in range(ITERS):
        image = operator(direction)
        alpha = current / total(direction * image)
        answer = answer + alpha * direction
        if step + 1 < ITERS:
            residual = residual - alpha * image
            scaled = precond * residual
            following = total(residual * scaled)
            direction = scaled + following / current * direction
            current = following

    first = sec * all_tiles + me * tiles
    chosen = (row + first == lane).astype(jnp.float32)
    place = lax.broadcasted_iota(jnp.int32, (ROWS, LANES), 1)
    own = jnp.zeros((ROWS, LANES), jnp.float32)
    for f in range(6):
        value = jnp.sum(chosen * answer[f : f + 1], axis=1, keepdims=True)
        own = jnp.where(place == f, value, own)
    corrections[...] = own[:tiles, :6]


def shards(patches, zoom, frac, offset, owner, top_grid):
    _, tiles, source, _ = patches.shape
    frame = top_grid.shape[1]
    devices, sections = lax.axis_size("tile"), lax.axis_size("sec")
    bands = frame // BAND
    capacity = max(2, 2 * tiles * bands // devices)
    slots = devices * capacity
    all_tiles = tiles * devices
    width = payload_lanes(tiles, devices)
    sizes = (tiles, bands, frame, source, capacity, devices)
    place = (zoom[0], frac[0], offset[0])
    routes = jnp.transpose(owner, (0, 2, 3, 1))[0]

    rows = tiles * bands
    plan, arriving = exchange_plan(devices)
    blocks = [
        jax.ShapeDtypeStruct(
            (len(group) * PACKED, BAND, LANES)
            if is_packed(capacity, devices, group[0])
            else (len(group) * capacity, BAND, frame),
            jnp.bfloat16,
        )
        for group in plan
    ]
    frames, *outgoing = pl.pallas_call(
        functools.partial(render_kernel, sizes),
        name="render",
        in_specs=[HBM] * 5,
        out_specs=[VMEM] * (1 + len(plan)),
        out_shape=[jax.ShapeDtypeStruct((rows, BAND, frame), jnp.bfloat16)] + blocks,
        scratch_shapes=[
            pltpu.SMEM(place[0].shape, jnp.float32),
            pltpu.SMEM(place[1].shape, jnp.float32),
            pltpu.SMEM(place[2].shape, jnp.int32),
            pltpu.SMEM(routes.shape, jnp.int32),
            pltpu.VMEM((tiles, source, source), jnp.bfloat16),
            pltpu.SMEM((devices,), jnp.int32),
            pltpu.SMEM((slots,), jnp.int32),
            pltpu.SemaphoreType.DMA((4,)),
            pltpu.SemaphoreType.DMA((tiles,)),
        ],
        compiler_params=params(24),
        cost_estimate=cost(800_000_000, 4 << 20),
    )(*(pltpu.with_memory_space_constraint(x, pltpu.HBM) for x in (*place, routes, patches[0])))

    base = pl.pallas_call(
        functools.partial(moment_kernel, sizes),
        name="moments",
        in_specs=[SMEM] * 3 + [VMEM],
        out_specs=VMEM,
        out_shape=jax.ShapeDtypeStruct((PAYLOAD_ROWS, width), jnp.float32),
        scratch_shapes=[pltpu.VMEM((len(MOMENT_ROWS), width, frame), jnp.float32)],
        compiler_params=params(24),
        cost_estimate=cost(20_000_000, 1 << 20),
    )(*place, frames)

    codes = pl.pallas_call(
        functools.partial(scan_kernel, sizes),
        name="scan",
        in_specs=[SMEM],
        out_specs=SMEM,
        out_shape=jax.ShapeDtypeStruct((slots + 1,), jnp.int32),
        compiler_params=params(24),
        cost_estimate=cost(20_000_000, 1 << 20),
    )(routes)

    cover_sum, col_cover, slot_lines, slot_bands = pl.pallas_call(
        functools.partial(slot_kernel, sizes),
        name="slots",
        in_specs=[SMEM] * 4,
        out_specs=[VMEM] * 3 + [SMEM],
        out_shape=[
            jax.ShapeDtypeStruct((bands + 1, BAND, frame), jnp.float32),
            jax.ShapeDtypeStruct((all_tiles + ROWS, frame), jnp.float32),
            jax.ShapeDtypeStruct((3, slots, LANES), jnp.float32),
            pltpu.SMEM((3, slots), jnp.int32),
        ],
        compiler_params=params(24),
        cost_estimate=cost(20_000_000, 1 << 20),
    )(*place, codes)

    def swapped(block, distance):
        return lax.ppermute(block, "tile", [(i, i ^ distance) for i in range(devices)])

    incoming = [outgoing[0]]
    for block, group in zip(outgoing[1:], plan[1:]):
        incoming.append(swapped(block, group[0]))
        if len(group) == 2:
            passed_on = incoming[-1][incoming[-1].shape[0] // 2 :]
    if devices == 8:
        incoming.append(swapped(passed_on, 1))

    slot_bands = pltpu.with_memory_space_constraint(slot_bands, pltpu.SMEM)
    total = jax.ShapeDtypeStruct((bands + 1, BAND, frame), jnp.float32)

    def blend(kernel, name, chosen, results, scratch, *operands):
        distances = [(block, arriving[block][1]) for block in chosen]
        arrays = [arriving[block][0] for block in chosen]
        packed = [
            array
            for array, (_, distance) in zip(arrays, distances)
            if is_packed(capacity, devices, distance)
        ]
        whole = jax.ShapeDtypeStruct((capacity, BAND, frame), jnp.bfloat16)
        result, *unpacked = pl.pallas_call(
            functools.partial(kernel, sizes, distances),
            name=name,
            in_specs=[SMEM] + [VMEM] * (len(operands) + len(chosen)),
            out_specs=[VMEM] * (1 + len(packed)),
            out_shape=[results] + [whole] * len(packed),
            scratch_shapes=scratch,
            compiler_params=params(24),
            cost_estimate=cost(1_000_000, 2 << 20),
        )(slot_bands, *operands, *(incoming[array] for array in arrays))
        for array, block in zip(packed, unpacked):
            incoming[array] = block
        return result

    last = [5] if devices == 8 else range(devices - devices // 4, devices)
    early = [block for block in range(devices) if block not in last]
    before = blend(first_blend_kernel, "first_blend", early, total, [], col_cover)
    grid = blend(
        last_blend_kernel,
        "last_blend",
        last,
        jax.ShapeDtypeStruct((bands, BAND, frame), jnp.bfloat16),
        [pltpu.VMEM(total.shape, total.dtype)],
        col_cover,
        cover_sum,
        before,
    )

    from_next = lax.ppermute(grid, "sec", [(i, (i - 1) % sections) for i in range(sections)])

    sums = jax.ShapeDtypeStruct((4 * frame // LANES, (all_tiles + 1) * ROWS, LANES), jnp.float32)
    weights, zeros = pl.pallas_call(
        functools.partial(weight_kernel, sizes),
        name="weights",
        in_specs=[VMEM],
        out_specs=[VMEM] * 2,
        out_shape=[jax.ShapeDtypeStruct((2, slots, BAND, LANES), jnp.float32), sums],
        compiler_params=params(24),
        cost_estimate=cost(1_000_000, 1 << 20),
    )(slot_lines)

    payload, grid_out, _ = pl.pallas_call(
        functools.partial(gradient_kernel, sizes),
        name="gradient",
        in_specs=[SMEM] + [VMEM] * (7 + len(incoming)),
        out_specs=[VMEM, HBM, VMEM],
        out_shape=[
            jax.ShapeDtypeStruct((sections * devices, PAYLOAD_ROWS, width), jnp.float32),
            jax.ShapeDtypeStruct((bands, BAND, frame), jnp.bfloat16),
            sums,
        ],
        scratch_shapes=[
            pltpu.VMEM((bands + 1, BAND, frame), jnp.float32),
            pltpu.SemaphoreType.DMA,
        ],
        input_output_aliases={5: 2},
        compiler_params=params(24),
        cost_estimate=cost(8_000_000, 2 << 20),
    )(
        slot_bands,
        from_next,
        top_grid.reshape(bands, BAND, frame),
        col_cover,
        weights,
        zeros,
        base,
        grid,
        *incoming,
    )

    received = lax.all_to_all(
        payload, ("sec", "tile"), split_axis=0, concat_axis=0, tiled=True
    )

    corrections = pl.pallas_call(
        functools.partial(solve_kernel, sizes),
        name="solve",
        in_specs=[VMEM],
        out_specs=VMEM,
        out_shape=jax.ShapeDtypeStruct((tiles, 6), jnp.float32),
        compiler_params=params(24),
        cost_estimate=cost(100_000, 1 << 18),
    )(received)
    return (
        grid_out.reshape(1, 1, frame, frame),
        jnp.transpose(corrections[None], (2, 0, 1)),
    )


def solution(mesh):
    placed = (
        P("sec", "tile", None, None),
        P("sec", None, None),
        P("sec", None, None),
        P("sec", None, None),
        P("sec", None, None, None),
        P("tile", None, None),
    )
    return jax.shard_map(
        shards,
        mesh=mesh,
        in_specs=placed,
        out_specs=(P("sec", "tile", None, None), P(None, "sec", "tile")),
        check_vma=False,
    )
```

```python
import functools
import math

import jax
import jax.numpy as jnp
from jax import lax
from jax.experimental import pallas as pl
from jax.experimental.pallas import tpu as pltpu
from jax.sharding import PartitionSpec as P

BAND = 16
ITERS = 2
COUPLING = 0.25
LANES = 128
ROWS = 8
SPARE = 24
PACKED = 29
HBM = pl.BlockSpec(memory_space=pltpu.HBM)
SMEM = pl.BlockSpec(memory_space=pltpu.SMEM)
VMEM = pl.BlockSpec(memory_space=pltpu.VMEM)


def params(mebibytes):
    return pltpu.CompilerParams(vmem_limit_bytes=mebibytes * 1024 * 1024)


def cost(flops, size):
    return pl.CostEstimate(flops=flops, bytes_accessed=size, transcendentals=0)


def exact_dot(left, right):
    return lax.dot_general(
        left,
        right,
        (((1,), (1,)), ((), ())),
        precision=lax.Precision.HIGHEST,
        preferred_element_type=jnp.float32,
    )


def points_of(spots, zoom, frac, offset, axis, tile, ratio):
    scale = zoom[axis, tile] * ratio
    return (spots - offset[axis, tile].astype(jnp.float32) - frac[axis, tile]) / scale


def cover_of(points, source):
    return jnp.clip(jnp.minimum(points + 1.0, source - points), 0.0, 1.0)


def hat_weight(distance):
    return jnp.maximum(0.0, 1.0 - jnp.abs(distance))


def spots_along(shape, dim, start=0):
    return (lax.broadcasted_iota(jnp.int32, shape, dim) + start).astype(jnp.float32)


def coords(spots, frame):
    return (spots - (frame - 1) / 2.0) / (frame / 2.0)


def exchange_plan(devices):
    if devices == 8:
        outgoing = [[0], [2, 3], [4], [5], [6], [7], [1]]
        return outgoing, [(0, 0), (1, 2), (2, 4), (3, 5), (4, 6), (5, 7), (6, 1), (7, 3)]
    return [[d] for d in range(devices)], [(d, d) for d in range(devices)]


def is_packed(capacity, devices, distance):
    return devices == 8 and capacity == 16 and distance > 0


def spare_pieces():
    kept = LANES - SPARE
    pieces = [(4 * i + c, kept, 13 + i, SPARE * c, SPARE) for i in range(3) for c in range(4)]
    return pieces + [(12, kept + 8 * i, 13 + i, 4 * SPARE, 8) for i in range(3)]


def moved(value, start, goal):
    shift = (goal - start) % LANES
    return pltpu.roll(value, shift, 1) if shift else value


def lane_window(start, count):
    lane = lax.broadcasted_iota(jnp.int32, (BAND, LANES), 1)
    return (lane >= start) & (lane < start + count)


def pack_block(there, start, firsts, seconds):
    for k in range(16):
        there[start + k] = firsts(k)
    values = [seconds(k).astype(jnp.float32) for k in range(16)]
    for slot, lane, donor, goal, count in spare_pieces():
        values[slot] = jnp.where(
            lane_window(lane, count), moved(values[donor], goal, lane), values[slot]
        )
    for k in range(13):
        there[start + 16 + k] = values[k].astype(jnp.bfloat16)


def unpack_block(block):
    firsts = [block[k].astype(jnp.float32) for k in range(16)]
    seconds = [block[16 + k].astype(jnp.float32) for k in range(13)]
    seconds += [jnp.zeros((BAND, LANES), jnp.float32)] * 3
    for slot, lane, donor, start, count in spare_pieces():
        seconds[donor] = jnp.where(
            lane_window(start, count), moved(seconds[slot], lane, start), seconds[donor]
        )
    kept = lane_window(0, LANES - SPARE)
    seconds = [
        jnp.where(kept, second, moved(first, 0, LANES - SPARE))
        for first, second in zip(firsts, seconds)
    ]
    return list(zip(firsts, seconds))


def render_kernel(
    sizes, zoom_in, frac_in, offset_in, owner_in, patches_in, frames, *outgoing_and_scratch
):
    tiles, bands, frame, source, capacity, devices = sizes
    plan, _ = exchange_plan(devices)
    outgoing = outgoing_and_scratch[: len(plan)]
    zoom, frac, offset, owner, patches, named, rows, small_sems, patch_sems = (
        outgoing_and_scratch[len(plan) :]
    )
    me = lax.axis_index("tile")
    first_tile = me * tiles
    ratio = frame / source
    fetched = [
        pltpu.make_async_copy(patches_in.at[j], patches.at[j], patch_sems.at[j])
        for j in range(tiles)
    ]
    small = [
        pltpu.make_async_copy(there, here, small_sems.at[k])
        for k, (there, here) in enumerate(
            ((zoom_in, zoom), (frac_in, frac), (offset_in, offset), (owner_in, owner))
        )
    ]
    for copy in small + fetched:
        copy.start()
    for g in range(devices):
        named[g] = 0
    for slot in range(devices * capacity):
        rows[slot] = 0
    for copy in small:
        copy.wait()
    halves = []
    for j in range(tiles):
        tile = first_tile + j
        row_points = points_of(spots_along((frame, LANES), 0), zoom, frac, offset, 0, tile, ratio)
        row_weights = jnp.concatenate(
            [
                hat_weight(row_points - spots_along((frame, LANES), 1, p)).astype(jnp.bfloat16)
                for p in range(0, source, LANES)
            ],
            axis=1,
        )
        fetched[j].wait()
        half, quarter = source // 2, frame // 4
        upper = jnp.dot(
            row_weights[: 3 * quarter, :half],
            patches[j, :half],
            preferred_element_type=jnp.float32,
        )
        lower = jnp.dot(
            row_weights[quarter:, half:],
            patches[j, half:],
            preferred_element_type=jnp.float32,
        )
        halfway = jnp.concatenate(
            [upper[:quarter], upper[quarter:] + lower[: 2 * quarter], lower[2 * quarter :]]
        ).astype(jnp.bfloat16)
        for band in range(bands):
            target = owner[band, 0, tile]
            slot = named[target]
            named[target] = slot + 1
            rows[target * capacity + slot] = j * bands + band
        halves.append(halfway)
    for j in range(tiles):
        tile = first_tile + j
        col_points = points_of(spots_along((ROWS, frame), 1), zoom, frac, offset, 1, tile, ratio)
        over = moved(col_points[:, frame - LANES :], LANES - SPARE, 0)
        lane = lax.broadcasted_iota(jnp.int32, over.shape, 1)
        folded = (lane < SPARE) & (cover_of(over, source) > 0.0)
        col_points = jnp.concatenate(
            [jnp.where(folded, over, col_points[:, :LANES]), col_points[:, LANES:]], axis=1
        )
        col_points = jnp.broadcast_to(col_points[:1], (source, frame))
        col_weights = hat_weight(col_points - spots_along((source, frame), 0)).astype(jnp.bfloat16)
        halfway = halves[j]
        rendered = jnp.dot(
            halfway, col_weights, preferred_element_type=jnp.float32
        ).astype(jnp.bfloat16)
        frames[j * bands : (j + 1) * bands] = rendered.reshape(bands, BAND, frame)
    for there, group in zip(outgoing, plan):
        for position, distance in enumerate(group):
            target = me ^ distance
            if is_packed(capacity, devices, distance):
                taken = [rows[target * capacity + slot] for slot in range(capacity)]
                pack_block(
                    there,
                    PACKED * position,
                    lambda k: frames[taken[k], :, :LANES],
                    lambda k: frames[taken[k], :, LANES:],
                )
                continue
            for slot in range(capacity):
                there[position * capacity + slot] = frames[rows[target * capacity + slot]]


def feature_rows(frame, wanted):
    shape = (ROWS, frame)
    x = coords(spots_along(shape, 1), frame)
    row = lax.broadcasted_iota(jnp.int32, shape, 0)
    rows = jnp.zeros(shape, jnp.float32)
    for r, power in wanted.items():
        rows = jnp.where(row == r, (jnp.ones_like(x), x, x * x)[power], rows)
    return rows


MOMENT_ROWS = ((0, 0, {0: 0, 1: 1}), (0, 1, {2: 0}), (1, 0, {0: 2}), (1, 1, {1: 1}), (1, 2, {2: 0}))
PAYLOAD_ROWS = 4


def scan_kernel(sizes, owner, codes):
    tiles, bands, frame, source, capacity, devices = sizes
    me = lax.axis_index("tile")

    def scan(block, distance):
        count = 0
        for j in range(tiles):
            tile = (me ^ distance) * tiles + j
            named = [owner[band, 0, tile] for band in range(bands)]
            for band in range(bands):
                codes[block * capacity + count] = tile * bands + band
                count += (named[band] == me).astype(jnp.int32)

        def blank(position, carry):
            codes[block * capacity + position] = -1
            return carry

        lax.fori_loop(count, capacity, blank, 0)

    arriving = exchange_plan(devices)[1]
    if devices == 8:
        for block, (_, distance) in enumerate(arriving):
            scan(block, distance)
    else:
        pl.loop(0, devices)(lambda block: scan(block, block))


def slot_kernel(
    sizes, zoom, frac, offset, codes, cover_sum, col_cover, slot_lines, slot_bands
):
    tiles, bands, frame, source, capacity, devices = sizes
    slots = devices * capacity
    all_tiles = tiles * devices
    ratio = frame / source

    @pl.loop(0, all_tiles // ROWS)
    def _(group):
        for k in range(ROWS):
            tile = group * ROWS + k
            points = points_of(spots_along((1, frame), 1), zoom, frac, offset, 1, tile, ratio)
            col_cover[pl.ds(tile, 1), :] = cover_of(points, source)

    col_cover[all_tiles:] = jnp.zeros((ROWS, frame), jnp.float32)
    cover_sum[...] = jnp.zeros_like(cover_sum)
    unroll = math.gcd(slots, ROWS)

    @pl.loop(0, slots // unroll)
    def _(group):
        for k in range(unroll):
            slot = group * unroll + k
            used = codes[slot] >= 0
            code = jnp.maximum(codes[slot], 0)
            tile, band = code // bands, code % bands
            before = jnp.maximum(codes[jnp.maximum(slot - 1, 0)], 0) // bands
            place = jnp.where(used, band, bands)
            slot_bands[0, slot] = place
            slot_bands[1, slot] = jnp.where(used, tile, all_tiles)
            slot_bands[2, slot] = (used & (before == tile)).astype(jnp.int32)
            here = pl.ds(slot, 1)
            row = jnp.zeros((1, LANES), jnp.float32)
            start = row + (band * BAND).astype(jnp.float32)
            shift = row + (offset[0, tile].astype(jnp.float32) + frac[0, tile])
            inverse = 1.0 / (row + zoom[0, tile] * ratio)
            slope = jnp.broadcast_to(inverse, (BAND, LANES))
            first = (start - shift) * inverse
            slot_lines[0, here, :] = inverse
            slot_lines[1, here, :] = first
            slot_lines[2, here, :] = coords(start, frame)
            cover = cover_of(spots_along((BAND, LANES), 0) * slope + first, source)
            columns = col_cover[pl.ds(tile, 1), :]
            for half in range(frame // LANES):
                part = slice(half * LANES, (half + 1) * LANES)
                cover_sum[place, :, part] += cover * columns[:, part]


def payload_lanes(tiles, devices):
    return pl.cdiv(2 * tiles * devices + 6 * tiles, LANES) * LANES


def moment_kernel(sizes, zoom, frac, offset, frames, base, parts):
    tiles, bands, frame, source, capacity, devices = sizes
    me = lax.axis_index("tile")
    all_tiles = tiles * devices
    ratio = frame / source
    parts[...] = jnp.zeros_like(parts)
    for j in range(tiles):
        tile = me * tiles + j
        spots = spots_along((frame, frame), 0)
        y = coords(spots, frame)
        cover = cover_of(points_of(spots, zoom, frac, offset, 0, tile, ratio), source)
        level = frames[j * bands : (j + 1) * bands].reshape(frame, frame).astype(jnp.float32)
        columns = points_of(spots_along((1, frame), 1), zoom, frac, offset, 1, tile, ratio)
        columns = cover_of(columns, source)
        weighted = (cover, cover * y, cover * y * y)
        for power, image in enumerate((None, level, level * level)):
            sums = [
                columns * jnp.sum(rows if image is None else rows * image, axis=0, keepdims=True)
                for rows in weighted
            ]
            for k, (half, a, _) in enumerate(MOMENT_ROWS):
                place = 2 * all_tiles + tiles * (2 * power + half) + j
                parts[k, place : place + 1, :] = sums[a]
    total = 0.0
    for k, (_, _, wanted) in enumerate(MOMENT_ROWS):
        total += exact_dot(feature_rows(frame, wanted), parts[k])
    base[...] = total[:PAYLOAD_ROWS]


def add_blocks(sizes, chosen, slot_bands, col_cover, blocks, whole, total):
    tiles, bands, frame, source, capacity, devices = sizes
    whole = iter(whole)
    for (block, distance), values in zip(chosen, blocks):
        packed = is_packed(capacity, devices, distance)
        if packed:
            unpacked, levels = next(whole), unpack_block(values)
        for k in range(capacity):
            slot = block * capacity + k
            columns = col_cover[pl.ds(slot_bands[1, slot], 1), :]
            for half in range(frame // LANES):
                part = slice(half * LANES, (half + 1) * LANES)
                level = levels[k][half] if packed else values[k, :, part].astype(jnp.float32)
                if packed or half == 0:
                    level = jnp.where(columns[:, part] > 0.0, level, 0.0)
                total[slot_bands[0, slot], :, part] += level
                if packed:
                    unpacked[k, :, part] = level.astype(jnp.bfloat16)


def first_blend_kernel(sizes, chosen, slot_bands, col_cover, *refs):
    blocks, (total, *whole) = refs[: len(chosen)], refs[len(chosen) :]
    total[...] = jnp.zeros_like(total)
    add_blocks(sizes, chosen, slot_bands, col_cover, blocks, whole, total)


def last_blend_kernel(sizes, chosen, slot_bands, col_cover, cover_sum, before, *refs):
    bands = sizes[1]
    blocks, (grid, *whole, total) = refs[: len(chosen)], refs[len(chosen) :]
    total[...] = before[...]
    add_blocks(sizes, chosen, slot_bands, col_cover, blocks, whole, total)
    grid[...] = (total[:bands] / (1.0 + cover_sum[:bands])).astype(jnp.bfloat16)


def weight_kernel(sizes, slot_lines, weights, sums):
    tiles, bands, frame, source, capacity, devices = sizes
    sums[...] = jnp.zeros_like(sums)
    spots = spots_along((BAND, LANES), 0)
    raised = spots * (2.0 / frame)

    @pl.loop(0, devices * capacity // ROWS)
    def _(group):
        for k in range(ROWS):
            slot = group * ROWS + k
            here = pl.ds(slot, 1)
            cover = cover_of(spots * slot_lines[0, here, :] + slot_lines[1, here, :], source)
            weights[0, slot] = cover
            weights[1, slot] = cover * (raised + slot_lines[2, here, :])


GRADIENT_ROWS = ({0: 0, 1: 1}, {2: 0}, {3: 0, 4: 1}, {5: 0})


def gradient_kernel(
    sizes, slot_bands, from_next, top_grid, col_cover, weights, _, base, grid, *blocks_and_rest
):
    tiles, bands, frame, source, capacity, devices = sizes
    *blocks, payload, grid_out, sums, above, grid_sem = blocks_and_rest
    written = pltpu.make_async_copy(grid, grid_out, grid_sem)
    written.start()
    sec = lax.axis_index("sec")
    all_tiles = tiles * devices

    @pl.when(sec == lax.axis_size("sec") - 1)
    def _():
        above[:bands] = top_grid[...].astype(jnp.float32)

    @pl.when(sec != lax.axis_size("sec") - 1)
    def _():
        above[:bands] = from_next[...].astype(jnp.float32)

    above[bands] = jnp.zeros((BAND, frame), jnp.float32)
    halves = range(frame // LANES)

    for block, (array, _) in enumerate(exchange_plan(devices)[1]):
        running = None
        for k in range(capacity):
            slot = block * capacity + k
            cover, lifted = weights[0, slot], weights[1, slot]
            level = blocks[array][k].astype(jnp.float32)
            error = above[slot_bands[0, slot]] - level
            product = error * level
            terms = []
            for half in halves:
                part = slice(half * LANES, (half + 1) * LANES)
                for weight, value in (
                    (cover, error),
                    (lifted, error),
                    (cover, product),
                    (lifted, product),
                ):
                    term = weight * value[:, part]
                    terms.append(term[:ROWS] + term[ROWS:])
            if running is not None:
                same = slot_bands[2, slot] == 1
                terms = [
                    term + jnp.where(same, before, 0.0) for term, before in zip(terms, running)
                ]
            running = terms
            rows = pl.ds(pl.multiple_of(slot_bands[1, slot] * ROWS, ROWS), ROWS)
            for index, term in enumerate(terms):
                sums[index, rows, :] = term

    values = [jnp.zeros((all_tiles, 1), jnp.float32)] * 6
    for half in halves:
        columns = col_cover[:all_tiles, half * LANES : (half + 1) * LANES]
        x = coords(spots_along((all_tiles, LANES), 1, half * LANES), frame)
        for kind, wanted in enumerate(GRADIENT_ROWS):
            index = half * len(GRADIENT_ROWS) + kind
            value = sums[index, pl.ds(0, all_tiles, stride=ROWS), :]
            for r in range(1, ROWS):
                value += sums[index, pl.ds(r, all_tiles, stride=ROWS), :]
            value = value * columns
            for row, power in wanted.items():
                term = value * x if power else value
                values[row] += jnp.sum(term, axis=1, keepdims=True)
    total = []
    tile = lax.broadcasted_iota(jnp.int32, (all_tiles, LANES), 0)
    for start in range(0, base.shape[1], LANES):
        lane = lax.broadcasted_iota(jnp.int32, (all_tiles, LANES), 1) + start
        placed = [
            sum(jnp.where(lane == tile + k * all_tiles, values[3 * k + r], 0.0) for k in range(2))
            for r in range(3)
        ]
        rows = [jnp.sum(value, axis=0, keepdims=True) for value in placed]
        total.append(jnp.concatenate(rows + [jnp.zeros_like(rows[0])], axis=0))
    total = base[...] + jnp.concatenate(total, axis=1)
    payload[...] = jnp.broadcast_to(total[None], payload.shape)
    written.wait()


def solve_kernel(sizes, received, corrections):
    tiles, bands, frame, source, capacity, devices = sizes
    sec, me = lax.axis_index("sec"), lax.axis_index("tile")
    sections = lax.axis_size("sec")
    all_tiles = tiles * devices
    lanes = sections * all_tiles
    lane = lax.broadcasted_iota(jnp.int32, (ROWS, lanes), 1)
    within = lane % all_tiles
    area = frame * frame

    width = max(lanes, received.shape[2])

    def rolled(value, shift):
        return pltpu.roll(value, shift % width, 1)

    def fetched(source):
        value = received[source]
        if value.shape[1] < width:
            value = jnp.pad(value, ((0, 0), (0, width - value.shape[1])))
        return jnp.concatenate([value, rolled(value, width - tiles)], axis=0)

    wide = lax.broadcasted_iota(jnp.int32, (ROWS, width), 1)
    gradients = [jnp.zeros((ROWS, width), jnp.float32)] * 2
    moments = [jnp.zeros((ROWS, width), jnp.float32)] * 3
    for s in range(sections):

        def gather(t, carry):
            own, *moments = carry
            value = fetched(s * devices + t)
            place = s * all_tiles + t * tiles
            here = (wide >= place) & (wide < place + tiles)
            for power in range(3):
                start = 2 * all_tiles + 2 * power * tiles
                moment = rolled(value, place - start + 2 * width)
                moments[power] = jnp.where(here, moment, moments[power])
            return (own + value, *moments)

        carry = (jnp.zeros((ROWS, width), jnp.float32), *moments)
        if devices <= 8:
            for t in range(devices):
                carry = gather(t, carry)
        else:
            carry = lax.fori_loop(0, devices, gather, carry)
        own, *moments = carry
        here = wide // all_tiles == s
        for k in range(2):
            part = rolled(own, (s - k) * all_tiles)
            gradients[k] = jnp.where(here, part, gradients[k])
    gradients = [value[:, :lanes] * (1.0 / area) for value in gradients]
    moments = [value[:, :lanes] * (1.0 / area) for value in moments]

    where = ((0, 1, 2), (1, 4, 5), (2, 5, 6))
    row = lax.broadcasted_iota(jnp.int32, (ROWS, lanes), 0)

    def entry(f, g):
        kind = moments[(f >= 3) + (g >= 3)]
        index = where[f % 3][g % 3]
        return kind[index : index + 1]

    def stacked(rows):
        result = jnp.zeros((ROWS, lanes), jnp.float32)
        for f, value in enumerate(rows):
            result = jnp.where(row == f, value, result)
        return result

    normal = [stacked([entry(f, g) for f in range(6)]) for g in range(6)]
    diagonal = stacked([entry(f, f) for f in range(6)])
    gradients = stacked([gradients[f // 3][f % 3 : f % 3 + 1] for f in range(6)])
    precond = 1.0 / (diagonal + 4.0 * COUPLING)

    def total(values):
        return jnp.sum(jnp.sum(values, axis=1, keepdims=True), axis=0, keepdims=True)

    def operator(vector):
        beside = jnp.where(within < all_tiles - 1, pltpu.roll(vector, lanes - 1, 1), 0.0)
        beside += jnp.where(within > 0, pltpu.roll(vector, 1, 1), 0.0)
        upward = pltpu.roll(vector, lanes - all_tiles, 1)
        beside += jnp.where(lane < lanes - all_tiles, upward, 0.0)
        beside += jnp.where(lane >= all_tiles, pltpu.roll(vector, all_tiles, 1), 0.0)
        image = COUPLING * (4.0 * vector - beside)
        for g in range(6):
            image += normal[g] * vector[g : g + 1]
        return image

    answer = jnp.zeros((ROWS, lanes), jnp.float32)
    residual = gradients
    scaled = precond * residual
    direction = scaled
    current = total(residual * scaled)
    for step in range(ITERS):
        image = operator(direction)
        alpha = current / total(direction * image)
        answer = answer + alpha * direction
        if step + 1 < ITERS:
            residual = residual - alpha * image
            scaled = precond * residual
            following = total(residual * scaled)
            direction = scaled + following / current * direction
            current = following

    first = sec * all_tiles + me * tiles
    chosen = (row + first == lane).astype(jnp.float32)
    place = lax.broadcasted_iota(jnp.int32, (ROWS, LANES), 1)
    own = jnp.zeros((ROWS, LANES), jnp.float32)
    for f in range(6):
        value = jnp.sum(chosen * answer[f : f + 1], axis=1, keepdims=True)
        own = jnp.where(place == f, value, own)
    corrections[...] = own[:tiles, :6]


def shards(patches, zoom, frac, offset, owner, top_grid):
    _, tiles, source, _ = patches.shape
    frame = top_grid.shape[1]
    devices, sections = lax.axis_size("tile"), lax.axis_size("sec")
    bands = frame // BAND
    capacity = max(2, 2 * tiles * bands // devices)
    slots = devices * capacity
    all_tiles = tiles * devices
    width = payload_lanes(tiles, devices)
    sizes = (tiles, bands, frame, source, capacity, devices)
    place = (zoom[0], frac[0], offset[0])
    routes = jnp.transpose(owner, (0, 2, 3, 1))[0]

    rows = tiles * bands
    plan, arriving = exchange_plan(devices)
    blocks = [
        jax.ShapeDtypeStruct(
            (len(group) * PACKED, BAND, LANES)
            if is_packed(capacity, devices, group[0])
            else (len(group) * capacity, BAND, frame),
            jnp.bfloat16,
        )
        for group in plan
    ]
    frames, *outgoing = pl.pallas_call(
        functools.partial(render_kernel, sizes),
        name="render",
        in_specs=[HBM] * 5,
        out_specs=[VMEM] * (1 + len(plan)),
        out_shape=[jax.ShapeDtypeStruct((rows, BAND, frame), jnp.bfloat16)] + blocks,
        scratch_shapes=[
            pltpu.SMEM(place[0].shape, jnp.float32),
            pltpu.SMEM(place[1].shape, jnp.float32),
            pltpu.SMEM(place[2].shape, jnp.int32),
            pltpu.SMEM(routes.shape, jnp.int32),
            pltpu.VMEM((tiles, source, source), jnp.bfloat16),
            pltpu.SMEM((devices,), jnp.int32),
            pltpu.SMEM((slots,), jnp.int32),
            pltpu.SemaphoreType.DMA((4,)),
            pltpu.SemaphoreType.DMA((tiles,)),
        ],
        compiler_params=params(24),
        cost_estimate=cost(800_000_000, 4 << 20),
    )(*(pltpu.with_memory_space_constraint(x, pltpu.HBM) for x in (*place, routes, patches[0])))

    base = pl.pallas_call(
        functools.partial(moment_kernel, sizes),
        name="moments",
        in_specs=[SMEM] * 3 + [VMEM],
        out_specs=VMEM,
        out_shape=jax.ShapeDtypeStruct((PAYLOAD_ROWS, width), jnp.float32),
        scratch_shapes=[pltpu.VMEM((len(MOMENT_ROWS), width, frame), jnp.float32)],
        compiler_params=params(24),
        cost_estimate=cost(20_000_000, 1 << 20),
    )(*place, frames)

    codes = pl.pallas_call(
        functools.partial(scan_kernel, sizes),
        name="scan",
        in_specs=[SMEM],
        out_specs=SMEM,
        out_shape=jax.ShapeDtypeStruct((slots + 1,), jnp.int32),
        compiler_params=params(24),
        cost_estimate=cost(20_000_000, 1 << 20),
    )(routes)

    cover_sum, col_cover, slot_lines, slot_bands = pl.pallas_call(
        functools.partial(slot_kernel, sizes),
        name="slots",
        in_specs=[SMEM] * 4,
        out_specs=[VMEM] * 3 + [SMEM],
        out_shape=[
            jax.ShapeDtypeStruct((bands + 1, BAND, frame), jnp.float32),
            jax.ShapeDtypeStruct((all_tiles + ROWS, frame), jnp.float32),
            jax.ShapeDtypeStruct((3, slots, LANES), jnp.float32),
            pltpu.SMEM((3, slots), jnp.int32),
        ],
        compiler_params=params(24),
        cost_estimate=cost(20_000_000, 1 << 20),
    )(*place, codes)

    def swapped(block, distance):
        return lax.ppermute(block, "tile", [(i, i ^ distance) for i in range(devices)])

    incoming = [outgoing[0]]
    for block, group in zip(outgoing[1:], plan[1:]):
        incoming.append(swapped(block, group[0]))
        if len(group) == 2:
            passed_on = incoming[-1][incoming[-1].shape[0] // 2 :]
    if devices == 8:
        incoming.append(swapped(passed_on, 1))

    slot_bands = pltpu.with_memory_space_constraint(slot_bands, pltpu.SMEM)
    total = jax.ShapeDtypeStruct((bands + 1, BAND, frame), jnp.float32)

    def blend(kernel, name, chosen, results, scratch, *operands):
        distances = [(block, arriving[block][1]) for block in chosen]
        arrays = [arriving[block][0] for block in chosen]
        packed = [
            array
            for array, (_, distance) in zip(arrays, distances)
            if is_packed(capacity, devices, distance)
        ]
        whole = jax.ShapeDtypeStruct((capacity, BAND, frame), jnp.bfloat16)
        result, *unpacked = pl.pallas_call(
            functools.partial(kernel, sizes, distances),
            name=name,
            in_specs=[SMEM] + [VMEM] * (len(operands) + len(chosen)),
            out_specs=[VMEM] * (1 + len(packed)),
            out_shape=[results] + [whole] * len(packed),
            scratch_shapes=scratch,
            compiler_params=params(24),
            cost_estimate=cost(1_000_000, 2 << 20),
        )(slot_bands, *operands, *(incoming[array] for array in arrays))
        for array, block in zip(packed, unpacked):
            incoming[array] = block
        return result

    last = [5] if devices == 8 else range(devices - devices // 4, devices)
    early = [block for block in range(devices) if block not in last]
    before = blend(first_blend_kernel, "first_blend", early, total, [], col_cover)
    grid = blend(
        last_blend_kernel,
        "last_blend",
        last,
        jax.ShapeDtypeStruct((bands, BAND, frame), jnp.bfloat16),
        [pltpu.VMEM(total.shape, total.dtype)],
        col_cover,
        cover_sum,
        before,
    )

    from_next = lax.ppermute(grid, "sec", [(i, (i - 1) % sections) for i in range(sections)])

    sums = jax.ShapeDtypeStruct((4 * frame // LANES, (all_tiles + 1) * ROWS, LANES), jnp.float32)
    weights, zeros = pl.pallas_call(
        functools.partial(weight_kernel, sizes),
        name="weights",
        in_specs=[VMEM],
        out_specs=[VMEM] * 2,
        out_shape=[jax.ShapeDtypeStruct((2, slots, BAND, LANES), jnp.float32), sums],
        compiler_params=params(24),
        cost_estimate=cost(1_000_000, 1 << 20),
    )(slot_lines)

    payload, grid_out, _ = pl.pallas_call(
        functools.partial(gradient_kernel, sizes),
        name="gradient",
        in_specs=[SMEM] + [VMEM] * (7 + len(incoming)),
        out_specs=[VMEM, HBM, VMEM],
        out_shape=[
            jax.ShapeDtypeStruct((sections * devices, PAYLOAD_ROWS, width), jnp.float32),
            jax.ShapeDtypeStruct((bands, BAND, frame), jnp.bfloat16),
            sums,
        ],
        scratch_shapes=[
            pltpu.VMEM((bands + 1, BAND, frame), jnp.float32),
            pltpu.SemaphoreType.DMA,
        ],
        input_output_aliases={5: 2},
        compiler_params=params(24),
        cost_estimate=cost(8_000_000, 2 << 20),
    )(
        slot_bands,
        from_next,
        top_grid.reshape(bands, BAND, frame),
        col_cover,
        weights,
        zeros,
        base,
        grid,
        *incoming,
    )

    received = lax.all_to_all(
        payload, ("sec", "tile"), split_axis=0, concat_axis=0, tiled=True
    )

    corrections = pl.pallas_call(
        functools.partial(solve_kernel, sizes),
        name="solve",
        in_specs=[VMEM],
        out_specs=VMEM,
        out_shape=jax.ShapeDtypeStruct((tiles, 6), jnp.float32),
        compiler_params=params(24),
        cost_estimate=cost(100_000, 1 << 18),
    )(received)
    return (
        grid_out.reshape(1, 1, frame, frame),
        jnp.transpose(corrections[None], (2, 0, 1)),
    )


def solution(mesh):
    placed = (
        P("sec", "tile", None, None),
        P("sec", None, None),
        P("sec", None, None),
        P("sec", None, None),
        P("sec", None, None, None),
        P("tile", None, None),
    )
    return jax.shard_map(
        shards,
        mesh=mesh,
        in_specs=placed,
        out_specs=(P("sec", "tile", None, None), P(None, "sec", "tile")),
        check_vma=False,
    )
```

```python
import functools
import math

import jax
import jax.numpy as jnp
from jax import lax
from jax.experimental import pallas as pl
from jax.experimental.pallas import tpu as pltpu
from jax.sharding import PartitionSpec as P

BAND = 16
ITERS = 2
COUPLING = 0.25
LANES = 128
ROWS = 8
SPARE = 24
PACKED = 29
HBM = pl.BlockSpec(memory_space=pltpu.HBM)
SMEM = pl.BlockSpec(memory_space=pltpu.SMEM)
VMEM = pl.BlockSpec(memory_space=pltpu.VMEM)


def params(mebibytes):
    return pltpu.CompilerParams(vmem_limit_bytes=mebibytes * 1024 * 1024)


def cost(flops, size):
    return pl.CostEstimate(flops=flops, bytes_accessed=size, transcendentals=0)


def exact_dot(left, right):
    return lax.dot_general(
        left,
        right,
        (((1,), (1,)), ((), ())),
        precision=lax.Precision.HIGHEST,
        preferred_element_type=jnp.float32,
    )


def points_of(spots, zoom, frac, offset, axis, tile, ratio):
    scale = zoom[axis, tile] * ratio
    return (spots - offset[axis, tile].astype(jnp.float32) - frac[axis, tile]) / scale


def cover_of(points, source):
    return jnp.clip(jnp.minimum(points + 1.0, source - points), 0.0, 1.0)


def hat_weight(distance):
    return jnp.maximum(0.0, 1.0 - jnp.abs(distance))


def spots_along(shape, dim, start=0):
    return (lax.broadcasted_iota(jnp.int32, shape, dim) + start).astype(jnp.float32)


def coords(spots, frame):
    return (spots - (frame - 1) / 2.0) / (frame / 2.0)


def exchange_plan(devices):
    if devices == 8:
        outgoing = [[0], [2, 3], [4], [5], [6], [7], [1]]
        return outgoing, [(0, 0), (1, 2), (2, 4), (3, 5), (4, 6), (5, 7), (6, 1), (7, 3)]
    return [[d] for d in range(devices)], [(d, d) for d in range(devices)]


def is_packed(capacity, devices, distance):
    return devices == 8 and capacity == 16 and distance > 0


def spare_pieces():
    kept = LANES - SPARE
    pieces = [(4 * i + c, kept, 13 + i, SPARE * c, SPARE) for i in range(3) for c in range(4)]
    return pieces + [(12, kept + 8 * i, 13 + i, 4 * SPARE, 8) for i in range(3)]


def moved(value, start, goal):
    shift = (goal - start) % LANES
    return pltpu.roll(value, shift, 1) if shift else value


def lane_window(start, count):
    lane = lax.broadcasted_iota(jnp.int32, (BAND, LANES), 1)
    return (lane >= start) & (lane < start + count)


def pack_block(there, start, firsts, seconds):
    for k in range(16):
        there[start + k] = firsts(k)
    values = [seconds(k).astype(jnp.float32) for k in range(16)]
    for slot, lane, donor, goal, count in spare_pieces():
        values[slot] = jnp.where(
            lane_window(lane, count), moved(values[donor], goal, lane), values[slot]
        )
    for k in range(13):
        there[start + 16 + k] = values[k].astype(jnp.bfloat16)


def unpack_block(block):
    firsts = [block[k].astype(jnp.float32) for k in range(16)]
    seconds = [block[16 + k].astype(jnp.float32) for k in range(13)]
    seconds += [jnp.zeros((BAND, LANES), jnp.float32)] * 3
    for slot, lane, donor, start, count in spare_pieces():
        seconds[donor] = jnp.where(
            lane_window(start, count), moved(seconds[slot], lane, start), seconds[donor]
        )
    kept = lane_window(0, LANES - SPARE)
    seconds = [
        jnp.where(kept, second, moved(first, 0, LANES - SPARE))
        for first, second in zip(firsts, seconds)
    ]
    return list(zip(firsts, seconds))


def render_kernel(
    sizes, zoom_in, frac_in, offset_in, owner_in, patches_in, frames, *outgoing_and_scratch
):
    tiles, bands, frame, source, capacity, devices = sizes
    plan, _ = exchange_plan(devices)
    outgoing = outgoing_and_scratch[: len(plan)]
    zoom, frac, offset, owner, patches, named, rows, small_sems, patch_sems = (
        outgoing_and_scratch[len(plan) :]
    )
    me = lax.axis_index("tile")
    first_tile = me * tiles
    ratio = frame / source
    fetched = [
        pltpu.make_async_copy(patches_in.at[j], patches.at[j], patch_sems.at[j])
        for j in range(tiles)
    ]
    small = [
        pltpu.make_async_copy(there, here, small_sems.at[k])
        for k, (there, here) in enumerate(
            ((zoom_in, zoom), (frac_in, frac), (offset_in, offset), (owner_in, owner))
        )
    ]
    for copy in small + fetched:
        copy.start()
    for g in range(devices):
        named[g] = 0
    for slot in range(devices * capacity):
        rows[slot] = 0
    for copy in small:
        copy.wait()
    halves = []
    for j in range(tiles):
        tile = first_tile + j
        row_points = points_of(spots_along((frame, LANES), 0), zoom, frac, offset, 0, tile, ratio)
        row_weights = jnp.concatenate(
            [
                hat_weight(row_points - spots_along((frame, LANES), 1, p)).astype(jnp.bfloat16)
                for p in range(0, source, LANES)
            ],
            axis=1,
        )
        fetched[j].wait()
        half, quarter = source // 2, frame // 4
        upper = jnp.dot(
            row_weights[: 3 * quarter, :half],
            patches[j, :half],
            preferred_element_type=jnp.float32,
        )
        lower = jnp.dot(
            row_weights[quarter:, half:],
            patches[j, half:],
            preferred_element_type=jnp.float32,
        )
        halfway = jnp.concatenate(
            [upper[:quarter], upper[quarter:] + lower[: 2 * quarter], lower[2 * quarter :]]
        ).astype(jnp.bfloat16)
        for band in range(bands):
            target = owner[band, 0, tile]
            slot = named[target]
            named[target] = slot + 1
            rows[target * capacity + slot] = j * bands + band
        halves.append(halfway)
    for j in range(tiles):
        tile = first_tile + j
        col_points = points_of(spots_along((ROWS, frame), 1), zoom, frac, offset, 1, tile, ratio)
        over = moved(col_points[:, frame - LANES :], LANES - SPARE, 0)
        lane = lax.broadcasted_iota(jnp.int32, over.shape, 1)
        folded = (lane < SPARE) & (cover_of(over, source) > 0.0)
        col_points = jnp.concatenate(
            [jnp.where(folded, over, col_points[:, :LANES]), col_points[:, LANES:]], axis=1
        )
        col_points = jnp.broadcast_to(col_points[:1], (source, frame))
        col_weights = hat_weight(col_points - spots_along((source, frame), 0)).astype(jnp.bfloat16)
        halfway = halves[j]
        rendered = jnp.dot(
            halfway, col_weights, preferred_element_type=jnp.float32
        ).astype(jnp.bfloat16)
        frames[j * bands : (j + 1) * bands] = rendered.reshape(bands, BAND, frame)
    for there, group in zip(outgoing, plan):
        for position, distance in enumerate(group):
            target = me ^ distance
            if is_packed(capacity, devices, distance):
                taken = [rows[target * capacity + slot] for slot in range(capacity)]
                pack_block(
                    there,
                    PACKED * position,
                    lambda k: frames[taken[k], :, :LANES],
                    lambda k: frames[taken[k], :, LANES:],
                )
                continue
            for slot in range(capacity):
                there[position * capacity + slot] = frames[rows[target * capacity + slot]]


def feature_rows(frame, wanted):
    shape = (ROWS, frame)
    x = coords(spots_along(shape, 1), frame)
    row = lax.broadcasted_iota(jnp.int32, shape, 0)
    rows = jnp.zeros(shape, jnp.float32)
    for r, power in wanted.items():
        rows = jnp.where(row == r, (jnp.ones_like(x), x, x * x)[power], rows)
    return rows


MOMENT_ROWS = ((0, 0, {0: 0, 1: 1}), (0, 1, {2: 0}), (1, 0, {0: 2}), (1, 1, {1: 1}), (1, 2, {2: 0}))
PAYLOAD_ROWS = 4


def scan_kernel(sizes, owner, codes):
    tiles, bands, frame, source, capacity, devices = sizes
    me = lax.axis_index("tile")

    def scan(block, distance):
        count = 0
        for j in range(tiles):
            tile = (me ^ distance) * tiles + j
            named = [owner[band, 0, tile] for band in range(bands)]
            for band in range(bands):
                codes[block * capacity + count] = tile * bands + band
                count += (named[band] == me).astype(jnp.int32)

        def blank(position, carry):
            codes[block * capacity + position] = -1
            return carry

        lax.fori_loop(count, capacity, blank, 0)

    arriving = exchange_plan(devices)[1]
    if devices == 8:
        for block, (_, distance) in enumerate(arriving):
            scan(block, distance)
    else:
        pl.loop(0, devices)(lambda block: scan(block, block))


def slot_kernel(
    sizes, zoom, frac, offset, codes, cover_sum, col_cover, slot_lines, slot_bands
):
    tiles, bands, frame, source, capacity, devices = sizes
    slots = devices * capacity
    all_tiles = tiles * devices
    ratio = frame / source

    @pl.loop(0, all_tiles // ROWS)
    def _(group):
        for k in range(ROWS):
            tile = group * ROWS + k
            points = points_of(spots_along((1, frame), 1), zoom, frac, offset, 1, tile, ratio)
            col_cover[pl.ds(tile, 1), :] = cover_of(points, source)

    col_cover[all_tiles:] = jnp.zeros((ROWS, frame), jnp.float32)
    cover_sum[...] = jnp.zeros_like(cover_sum)
    unroll = math.gcd(slots, ROWS)

    @pl.loop(0, slots // unroll)
    def _(group):
        for k in range(unroll):
            slot = group * unroll + k
            used = codes[slot] >= 0
            code = jnp.maximum(codes[slot], 0)
            tile, band = code // bands, code % bands
            before = jnp.maximum(codes[jnp.maximum(slot - 1, 0)], 0) // bands
            place = jnp.where(used, band, bands)
            slot_bands[0, slot] = place
            slot_bands[1, slot] = jnp.where(used, tile, all_tiles)
            slot_bands[2, slot] = (used & (before == tile)).astype(jnp.int32)
            here = pl.ds(slot, 1)
            row = jnp.zeros((1, LANES), jnp.float32)
            start = row + (band * BAND).astype(jnp.float32)
            shift = row + (offset[0, tile].astype(jnp.float32) + frac[0, tile])
            inverse = 1.0 / (row + zoom[0, tile] * ratio)
            slope = jnp.broadcast_to(inverse, (BAND, LANES))
            first = (start - shift) * inverse
            slot_lines[0, here, :] = inverse
            slot_lines[1, here, :] = first
            slot_lines[2, here, :] = coords(start, frame)
            cover = cover_of(spots_along((BAND, LANES), 0) * slope + first, source)
            columns = col_cover[pl.ds(tile, 1), :]
            for half in range(frame // LANES):
                part = slice(half * LANES, (half + 1) * LANES)
                cover_sum[place, :, part] += cover * columns[:, part]


def payload_lanes(tiles, devices):
    return pl.cdiv(2 * tiles * devices + 6 * tiles, LANES) * LANES


def moment_kernel(sizes, zoom, frac, offset, frames, base, parts):
    tiles, bands, frame, source, capacity, devices = sizes
    me = lax.axis_index("tile")
    all_tiles = tiles * devices
    ratio = frame / source
    parts[...] = jnp.zeros_like(parts)
    for j in range(tiles):
        tile = me * tiles + j
        spots = spots_along((frame, frame), 0)
        y = coords(spots, frame)
        cover = cover_of(points_of(spots, zoom, frac, offset, 0, tile, ratio), source)
        level = frames[j * bands : (j + 1) * bands].reshape(frame, frame).astype(jnp.float32)
        columns = points_of(spots_along((1, frame), 1), zoom, frac, offset, 1, tile, ratio)
        columns = cover_of(columns, source)
        weighted = (cover, cover * y, cover * y * y)
        for power, image in enumerate((None, level, level * level)):
            sums = [
                columns * jnp.sum(rows if image is None else rows * image, axis=0, keepdims=True)
                for rows in weighted
            ]
            for k, (half, a, _) in enumerate(MOMENT_ROWS):
                place = 2 * all_tiles + tiles * (2 * power + half) + j
                parts[k, place : place + 1, :] = sums[a]
    total = 0.0
    for k, (_, _, wanted) in enumerate(MOMENT_ROWS):
        total += exact_dot(feature_rows(frame, wanted), parts[k])
    base[...] = total[:PAYLOAD_ROWS]


def add_blocks(sizes, chosen, slot_bands, col_cover, blocks, whole, total):
    tiles, bands, frame, source, capacity, devices = sizes
    whole = iter(whole)
    for (block, distance), values in zip(chosen, blocks):
        packed = is_packed(capacity, devices, distance)
        if packed:
            unpacked, levels = next(whole), unpack_block(values)
        for k in range(capacity):
            slot = block * capacity + k
            columns = col_cover[pl.ds(slot_bands[1, slot], 1), :]
            for half in range(frame // LANES):
                part = slice(half * LANES, (half + 1) * LANES)
                level = levels[k][half] if packed else values[k, :, part].astype(jnp.float32)
                if packed or half == 0:
                    level = jnp.where(columns[:, part] > 0.0, level, 0.0)
                total[slot_bands[0, slot], :, part] += level
                if packed:
                    unpacked[k, :, part] = level.astype(jnp.bfloat16)


def first_blend_kernel(sizes, chosen, slot_bands, col_cover, *refs):
    blocks, (total, *whole) = refs[: len(chosen)], refs[len(chosen) :]
    total[...] = jnp.zeros_like(total)
    add_blocks(sizes, chosen, slot_bands, col_cover, blocks, whole, total)


def last_blend_kernel(sizes, chosen, slot_bands, col_cover, cover_sum, before, *refs):
    bands, frame = sizes[1], sizes[2]
    blocks, (left, right, *whole, total) = refs[: len(chosen)], refs[len(chosen) :]
    total[...] = before[...]
    add_blocks(sizes, chosen, slot_bands, col_cover, blocks, whole, total)
    grid = (total[:bands] / (1.0 + cover_sum[:bands])).astype(jnp.bfloat16)
    left[...] = grid[:, :, : frame // 2]
    right[...] = grid[:, :, frame // 2 :]


def weight_kernel(sizes, slot_lines, weights, *sums):
    tiles, bands, frame, source, capacity, devices = sizes
    for ref in sums:
        ref[...] = jnp.zeros_like(ref)
    spots = spots_along((BAND, LANES), 0)
    raised = spots * (2.0 / frame)

    @pl.loop(0, devices * capacity // ROWS)
    def _(group):
        for k in range(ROWS):
            slot = group * ROWS + k
            here = pl.ds(slot, 1)
            cover = cover_of(spots * slot_lines[0, here, :] + slot_lines[1, here, :], source)
            weights[0, slot] = cover
            weights[1, slot] = cover * (raised + slot_lines[2, here, :])


GRADIENT_ROWS = ({0: 0, 1: 1}, {2: 0}, {3: 0, 4: 1}, {5: 0})


def add_gradients(sizes, half, slot_bands, from_next, top_grid, weights, blocks, sums, above):
    tiles, bands, frame, source, capacity, devices = sizes
    part = slice(half * LANES, (half + 1) * LANES)
    at_top = lax.axis_index("sec") == lax.axis_size("sec") - 1

    @pl.when(at_top)
    def _():
        above[:bands] = top_grid[:, :, part].astype(jnp.float32)

    @pl.when(jnp.logical_not(at_top))
    def _():
        above[:bands] = from_next[...].astype(jnp.float32)

    above[bands] = jnp.zeros((BAND, LANES), jnp.float32)

    for block, (array, _) in enumerate(exchange_plan(devices)[1]):
        running = None
        for k in range(capacity):
            slot = block * capacity + k
            cover, lifted = weights[0, slot], weights[1, slot]
            level = blocks[array][k, :, part].astype(jnp.float32)
            error = above[slot_bands[0, slot]] - level
            product = error * level
            terms = [cover * error, lifted * error, cover * product, lifted * product]
            terms = [term[:ROWS] + term[ROWS:] for term in terms]
            if running is not None:
                same = slot_bands[2, slot] == 1
                terms = [
                    term + jnp.where(same, before, 0.0) for term, before in zip(terms, running)
                ]
            running = terms
            rows = pl.ds(pl.multiple_of(slot_bands[1, slot] * ROWS, ROWS), ROWS)
            for kind, term in enumerate(terms):
                sums[kind, rows, :] = term


def left_gradient_kernel(sizes, slot_bands, from_next, top_grid, weights, _, *refs):
    *blocks, sums, above = refs
    add_gradients(sizes, 0, slot_bands, from_next, top_grid, weights, blocks, sums, above)


def gradient_kernel(
    sizes,
    slot_bands,
    from_next,
    top_grid,
    weights,
    _,
    left_sums,
    col_cover,
    base,
    left_grid,
    right_grid,
    *refs,
):
    tiles, bands, frame, source, capacity, devices = sizes
    *blocks, payload, grid_out, sums, above, grid_sems = refs
    halves = range(frame // LANES)
    written = [
        pltpu.make_async_copy(
            grid, grid_out.at[:, :, pl.ds(half * LANES, LANES)], grid_sems.at[half]
        )
        for half, grid in enumerate((left_grid, right_grid))
    ]
    for copy in written:
        copy.start()
    all_tiles = tiles * devices
    add_gradients(sizes, 1, slot_bands, from_next, top_grid, weights, blocks, sums, above)

    values = [jnp.zeros((all_tiles, 1), jnp.float32)] * 6
    for half in halves:
        columns = col_cover[:all_tiles, half * LANES : (half + 1) * LANES]
        x = coords(spots_along((all_tiles, LANES), 1, half * LANES), frame)
        for kind, wanted in enumerate(GRADIENT_ROWS):
            ref = (left_sums, sums)[half]
            value = ref[kind, pl.ds(0, all_tiles, stride=ROWS), :]
            for r in range(1, ROWS):
                value += ref[kind, pl.ds(r, all_tiles, stride=ROWS), :]
            value = value * columns
            for row, power in wanted.items():
                term = value * x if power else value
                values[row] += jnp.sum(term, axis=1, keepdims=True)
    total = []
    tile = lax.broadcasted_iota(jnp.int32, (all_tiles, LANES), 0)
    for start in range(0, base.shape[1], LANES):
        lane = lax.broadcasted_iota(jnp.int32, (all_tiles, LANES), 1) + start
        placed = [
            sum(jnp.where(lane == tile + k * all_tiles, values[3 * k + r], 0.0) for k in range(2))
            for r in range(3)
        ]
        rows = [jnp.sum(value, axis=0, keepdims=True) for value in placed]
        total.append(jnp.concatenate(rows + [jnp.zeros_like(rows[0])], axis=0))
    total = base[...] + jnp.concatenate(total, axis=1)
    payload[...] = jnp.broadcast_to(total[None], payload.shape)
    for copy in written:
        copy.wait()


def solve_kernel(sizes, received, corrections):
    tiles, bands, frame, source, capacity, devices = sizes
    sec, me = lax.axis_index("sec"), lax.axis_index("tile")
    sections = lax.axis_size("sec")
    all_tiles = tiles * devices
    lanes = sections * all_tiles
    lane = lax.broadcasted_iota(jnp.int32, (ROWS, lanes), 1)
    within = lane % all_tiles
    area = frame * frame

    width = max(lanes, received.shape[2])

    def rolled(value, shift):
        return pltpu.roll(value, shift % width, 1)

    def fetched(source):
        value = received[source]
        if value.shape[1] < width:
            value = jnp.pad(value, ((0, 0), (0, width - value.shape[1])))
        return jnp.concatenate([value, rolled(value, width - tiles)], axis=0)

    wide = lax.broadcasted_iota(jnp.int32, (ROWS, width), 1)
    gradients = [jnp.zeros((ROWS, width), jnp.float32)] * 2
    moments = [jnp.zeros((ROWS, width), jnp.float32)] * 3
    for s in range(sections):

        def gather(t, carry):
            own, *moments = carry
            value = fetched(s * devices + t)
            place = s * all_tiles + t * tiles
            here = (wide >= place) & (wide < place + tiles)
            for power in range(3):
                start = 2 * all_tiles + 2 * power * tiles
                moment = rolled(value, place - start + 2 * width)
                moments[power] = jnp.where(here, moment, moments[power])
            return (own + value, *moments)

        carry = (jnp.zeros((ROWS, width), jnp.float32), *moments)
        if devices <= 8:
            for t in range(devices):
                carry = gather(t, carry)
        else:
            carry = lax.fori_loop(0, devices, gather, carry)
        own, *moments = carry
        here = wide // all_tiles == s
        for k in range(2):
            part = rolled(own, (s - k) * all_tiles)
            gradients[k] = jnp.where(here, part, gradients[k])
    gradients = [value[:, :lanes] * (1.0 / area) for value in gradients]
    moments = [value[:, :lanes] * (1.0 / area) for value in moments]

    where = ((0, 1, 2), (1, 4, 5), (2, 5, 6))
    row = lax.broadcasted_iota(jnp.int32, (ROWS, lanes), 0)

    def entry(f, g):
        kind = moments[(f >= 3) + (g >= 3)]
        index = where[f % 3][g % 3]
        return kind[index : index + 1]

    def stacked(rows):
        result = jnp.zeros((ROWS, lanes), jnp.float32)
        for f, value in enumerate(rows):
            result = jnp.where(row == f, value, result)
        return result

    normal = [stacked([entry(f, g) for f in range(6)]) for g in range(6)]
    diagonal = stacked([entry(f, f) for f in range(6)])
    gradients = stacked([gradients[f // 3][f % 3 : f % 3 + 1] for f in range(6)])
    precond = 1.0 / (diagonal + 4.0 * COUPLING)

    def total(values):
        return jnp.sum(jnp.sum(values, axis=1, keepdims=True), axis=0, keepdims=True)

    def operator(vector):
        beside = jnp.where(within < all_tiles - 1, pltpu.roll(vector, lanes - 1, 1), 0.0)
        beside += jnp.where(within > 0, pltpu.roll(vector, 1, 1), 0.0)
        upward = pltpu.roll(vector, lanes - all_tiles, 1)
        beside += jnp.where(lane < lanes - all_tiles, upward, 0.0)
        beside += jnp.where(lane >= all_tiles, pltpu.roll(vector, all_tiles, 1), 0.0)
        image = COUPLING * (4.0 * vector - beside)
        for g in range(6):
            image += normal[g] * vector[g : g + 1]
        return image

    answer = jnp.zeros((ROWS, lanes), jnp.float32)
    residual = gradients
    scaled = precond * residual
    direction = scaled
    current = total(residual * scaled)
    for step in range(ITERS):
        image = operator(direction)
        alpha = current / total(direction * image)
        answer = answer + alpha * direction
        if step + 1 < ITERS:
            residual = residual - alpha * image
            scaled = precond * residual
            following = total(residual * scaled)
            direction = scaled + following / current * direction
            current = following

    first = sec * all_tiles + me * tiles
    chosen = (row + first == lane).astype(jnp.float32)
    place = lax.broadcasted_iota(jnp.int32, (ROWS, LANES), 1)
    own = jnp.zeros((ROWS, LANES), jnp.float32)
    for f in range(6):
        value = jnp.sum(chosen * answer[f : f + 1], axis=1, keepdims=True)
        own = jnp.where(place == f, value, own)
    corrections[...] = own[:tiles, :6]


def shards(patches, zoom, frac, offset, owner, top_grid):
    _, tiles, source, _ = patches.shape
    frame = top_grid.shape[1]
    devices, sections = lax.axis_size("tile"), lax.axis_size("sec")
    bands = frame // BAND
    capacity = max(2, 2 * tiles * bands // devices)
    slots = devices * capacity
    all_tiles = tiles * devices
    width = payload_lanes(tiles, devices)
    sizes = (tiles, bands, frame, source, capacity, devices)
    place = (zoom[0], frac[0], offset[0])
    routes = jnp.transpose(owner, (0, 2, 3, 1))[0]

    rows = tiles * bands
    plan, arriving = exchange_plan(devices)
    blocks = [
        jax.ShapeDtypeStruct(
            (len(group) * PACKED, BAND, LANES)
            if is_packed(capacity, devices, group[0])
            else (len(group) * capacity, BAND, frame),
            jnp.bfloat16,
        )
        for group in plan
    ]
    frames, *outgoing = pl.pallas_call(
        functools.partial(render_kernel, sizes),
        name="render",
        in_specs=[HBM] * 5,
        out_specs=[VMEM] * (1 + len(plan)),
        out_shape=[jax.ShapeDtypeStruct((rows, BAND, frame), jnp.bfloat16)] + blocks,
        scratch_shapes=[
            pltpu.SMEM(place[0].shape, jnp.float32),
            pltpu.SMEM(place[1].shape, jnp.float32),
            pltpu.SMEM(place[2].shape, jnp.int32),
            pltpu.SMEM(routes.shape, jnp.int32),
            pltpu.VMEM((tiles, source, source), jnp.bfloat16),
            pltpu.SMEM((devices,), jnp.int32),
            pltpu.SMEM((slots,), jnp.int32),
            pltpu.SemaphoreType.DMA((4,)),
            pltpu.SemaphoreType.DMA((tiles,)),
        ],
        compiler_params=params(24),
        cost_estimate=cost(800_000_000, 4 << 20),
    )(*(pltpu.with_memory_space_constraint(x, pltpu.HBM) for x in (*place, routes, patches[0])))

    base = pl.pallas_call(
        functools.partial(moment_kernel, sizes),
        name="moments",
        in_specs=[SMEM] * 3 + [VMEM],
        out_specs=VMEM,
        out_shape=jax.ShapeDtypeStruct((PAYLOAD_ROWS, width), jnp.float32),
        scratch_shapes=[pltpu.VMEM((len(MOMENT_ROWS), width, frame), jnp.float32)],
        compiler_params=params(24),
        cost_estimate=cost(20_000_000, 1 << 20),
    )(*place, frames)

    codes = pl.pallas_call(
        functools.partial(scan_kernel, sizes),
        name="scan",
        in_specs=[SMEM],
        out_specs=SMEM,
        out_shape=jax.ShapeDtypeStruct((slots + 1,), jnp.int32),
        compiler_params=params(24),
        cost_estimate=cost(20_000_000, 1 << 20),
    )(routes)

    cover_sum, col_cover, slot_lines, slot_bands = pl.pallas_call(
        functools.partial(slot_kernel, sizes),
        name="slots",
        in_specs=[SMEM] * 4,
        out_specs=[VMEM] * 3 + [SMEM],
        out_shape=[
            jax.ShapeDtypeStruct((bands + 1, BAND, frame), jnp.float32),
            jax.ShapeDtypeStruct((all_tiles + ROWS, frame), jnp.float32),
            jax.ShapeDtypeStruct((3, slots, LANES), jnp.float32),
            pltpu.SMEM((3, slots), jnp.int32),
        ],
        compiler_params=params(24),
        cost_estimate=cost(20_000_000, 1 << 20),
    )(*place, codes)

    def swapped(block, distance):
        return lax.ppermute(block, "tile", [(i, i ^ distance) for i in range(devices)])

    incoming = [outgoing[0]]
    for block, group in zip(outgoing[1:], plan[1:]):
        incoming.append(swapped(block, group[0]))
        if len(group) == 2:
            passed_on = incoming[-1][incoming[-1].shape[0] // 2 :]
    if devices == 8:
        incoming.append(swapped(passed_on, 1))

    slot_bands = pltpu.with_memory_space_constraint(slot_bands, pltpu.SMEM)
    total = jax.ShapeDtypeStruct((bands + 1, BAND, frame), jnp.float32)

    def blend(kernel, name, chosen, results, scratch, *operands):
        distances = [(block, arriving[block][1]) for block in chosen]
        arrays = [arriving[block][0] for block in chosen]
        packed = [
            array
            for array, (_, distance) in zip(arrays, distances)
            if is_packed(capacity, devices, distance)
        ]
        whole = jax.ShapeDtypeStruct((capacity, BAND, frame), jnp.bfloat16)
        found = pl.pallas_call(
            functools.partial(kernel, sizes, distances),
            name=name,
            in_specs=[SMEM] + [VMEM] * (len(operands) + len(chosen)),
            out_specs=[VMEM] * (len(results) + len(packed)),
            out_shape=results + [whole] * len(packed),
            scratch_shapes=scratch,
            compiler_params=params(24),
            cost_estimate=cost(1_000_000, 2 << 20),
        )(slot_bands, *operands, *(incoming[array] for array in arrays))
        for array, block in zip(packed, found[len(results) :]):
            incoming[array] = block
        return found[: len(results)]

    last = [5] if devices == 8 else range(devices - devices // 4, devices)
    early = [block for block in range(devices) if block not in last]
    (before,) = blend(first_blend_kernel, "first_blend", early, [total], [], col_cover)
    half = jax.ShapeDtypeStruct((bands, BAND, frame // 2), jnp.bfloat16)
    grids = blend(
        last_blend_kernel,
        "last_blend",
        last,
        [half, half],
        [pltpu.VMEM(total.shape, total.dtype)],
        col_cover,
        cover_sum,
        before,
    )

    ring = [(i, (i - 1) % sections) for i in range(sections)]
    from_next = [lax.ppermute(grid, "sec", ring) for grid in grids]

    sums = jax.ShapeDtypeStruct((4, (all_tiles + 1) * ROWS, LANES), jnp.float32)
    weights, *zeros = pl.pallas_call(
        functools.partial(weight_kernel, sizes),
        name="weights",
        in_specs=[VMEM],
        out_specs=[VMEM] * 3,
        out_shape=[jax.ShapeDtypeStruct((2, slots, BAND, LANES), jnp.float32), sums, sums],
        compiler_params=params(24),
        cost_estimate=cost(1_000_000, 1 << 20),
    )(slot_lines)

    top_bands = top_grid.reshape(bands, BAND, frame)
    above = pltpu.VMEM((bands + 1, BAND, LANES), jnp.float32)
    left_sums = pl.pallas_call(
        functools.partial(left_gradient_kernel, sizes),
        name="left_gradient",
        in_specs=[SMEM] + [VMEM] * (4 + len(incoming)),
        out_specs=VMEM,
        out_shape=sums,
        scratch_shapes=[above],
        input_output_aliases={4: 0},
        compiler_params=params(24),
        cost_estimate=cost(8_000_000, 2 << 20),
    )(slot_bands, from_next[0], top_bands, weights, zeros[0], *incoming)

    payload, grid_out, _ = pl.pallas_call(
        functools.partial(gradient_kernel, sizes),
        name="gradient",
        in_specs=[SMEM] + [VMEM] * (9 + len(incoming)),
        out_specs=[VMEM, HBM, VMEM],
        out_shape=[
            jax.ShapeDtypeStruct((sections * devices, PAYLOAD_ROWS, width), jnp.float32),
            jax.ShapeDtypeStruct((bands, BAND, frame), jnp.bfloat16),
            sums,
        ],
        scratch_shapes=[above, pltpu.SemaphoreType.DMA((2,))],
        input_output_aliases={4: 2},
        compiler_params=params(24),
        cost_estimate=cost(8_000_000, 2 << 20),
    )(
        slot_bands,
        from_next[1],
        top_bands,
        weights,
        zeros[1],
        left_sums,
        col_cover,
        base,
        *grids,
        *incoming,
    )

    received = lax.all_to_all(
        payload, ("sec", "tile"), split_axis=0, concat_axis=0, tiled=True
    )

    corrections = pl.pallas_call(
        functools.partial(solve_kernel, sizes),
        name="solve",
        in_specs=[VMEM],
        out_specs=VMEM,
        out_shape=jax.ShapeDtypeStruct((tiles, 6), jnp.float32),
        compiler_params=params(24),
        cost_estimate=cost(100_000, 1 << 18),
    )(received)
    return (
        grid_out.reshape(1, 1, frame, frame),
        jnp.transpose(corrections[None], (2, 0, 1)),
    )


def solution(mesh):
    placed = (
        P("sec", "tile", None, None),
        P("sec", None, None),
        P("sec", None, None),
        P("sec", None, None),
        P("sec", None, None, None),
        P("tile", None, None),
    )
    return jax.shard_map(
        shards,
        mesh=mesh,
        in_specs=placed,
        out_specs=(P("sec", "tile", None, None), P(None, "sec", "tile")),
        check_vma=False,
    )
```

```python
import functools
import math

import jax
import jax.numpy as jnp
from jax import lax
from jax.experimental import pallas as pl
from jax.experimental.pallas import tpu as pltpu
from jax.sharding import PartitionSpec as P

BAND = 16
ITERS = 2
COUPLING = 0.25
LANES = 128
ROWS = 8
SPARE = 24
PACKED = 29
HBM = pl.BlockSpec(memory_space=pltpu.HBM)
SMEM = pl.BlockSpec(memory_space=pltpu.SMEM)
VMEM = pl.BlockSpec(memory_space=pltpu.VMEM)


def params(mebibytes):
    return pltpu.CompilerParams(vmem_limit_bytes=mebibytes * 1024 * 1024)


def cost(flops, size):
    return pl.CostEstimate(flops=flops, bytes_accessed=size, transcendentals=0)


def points_of(spots, zoom, frac, offset, axis, tile, ratio):
    scale = zoom[axis, tile] * ratio
    return (spots - offset[axis, tile].astype(jnp.float32) - frac[axis, tile]) / scale


def cover_of(points, source):
    return jnp.clip(jnp.minimum(points + 1.0, source - points), 0.0, 1.0)


def hat_weight(distance):
    return jnp.maximum(0.0, 1.0 - jnp.abs(distance))


def spots_along(shape, dim, start=0):
    return (lax.broadcasted_iota(jnp.int32, shape, dim) + start).astype(jnp.float32)


def coords(spots, frame):
    return (spots - (frame - 1) / 2.0) / (frame / 2.0)


def exchange_plan(devices):
    if devices == 8:
        outgoing = [[0], [2, 3], [4], [5], [6], [7], [1]]
        return outgoing, [(0, 0), (1, 2), (2, 4), (3, 5), (4, 6), (5, 7), (6, 1), (7, 3)]
    return [[d] for d in range(devices)], [(d, d) for d in range(devices)]


def is_packed(capacity, devices, distance):
    return devices == 8 and capacity == 16 and distance > 0


def spare_pieces():
    kept = LANES - SPARE
    pieces = [(4 * i + c, kept, 13 + i, SPARE * c, SPARE) for i in range(3) for c in range(4)]
    return pieces + [(12, kept + 8 * i, 13 + i, 4 * SPARE, 8) for i in range(3)]


def moved(value, start, goal):
    shift = (goal - start) % LANES
    return pltpu.roll(value, shift, 1) if shift else value


def lane_window(start, count):
    lane = lax.broadcasted_iota(jnp.int32, (BAND, LANES), 1)
    return (lane >= start) & (lane < start + count)


def pack_block(there, start, firsts, seconds):
    for k in range(16):
        there[start + k] = firsts(k)
    values = [seconds(k).astype(jnp.float32) for k in range(16)]
    for slot, lane, donor, goal, count in spare_pieces():
        values[slot] = jnp.where(
            lane_window(lane, count), moved(values[donor], goal, lane), values[slot]
        )
    for k in range(13):
        there[start + 16 + k] = values[k].astype(jnp.bfloat16)


def unpack_block(block):
    firsts = [block[k].astype(jnp.float32) for k in range(16)]
    seconds = [block[16 + k].astype(jnp.float32) for k in range(13)]
    seconds += [jnp.zeros((BAND, LANES), jnp.float32)] * 3
    for slot, lane, donor, start, count in spare_pieces():
        seconds[donor] = jnp.where(
            lane_window(start, count), moved(seconds[slot], lane, start), seconds[donor]
        )
    kept = lane_window(0, LANES - SPARE)
    seconds = [
        jnp.where(kept, second, moved(first, 0, LANES - SPARE))
        for first, second in zip(firsts, seconds)
    ]
    return list(zip(firsts, seconds))


def render_kernel(
    sizes,
    zoom_in,
    frac_in,
    offset_in,
    owner_in,
    patches_in,
    frames,
    zoom,
    frac,
    offset,
    owner,
    *outgoing_and_scratch,
):
    tiles, bands, frame, source, capacity, devices = sizes
    plan, _ = exchange_plan(devices)
    outgoing = outgoing_and_scratch[: len(plan)]
    patches, named, rows, small_sems, patch_sems = outgoing_and_scratch[len(plan) :]
    me = lax.axis_index("tile")
    first_tile = me * tiles
    ratio = frame / source
    fetched = [
        pltpu.make_async_copy(patches_in.at[j], patches.at[j], patch_sems.at[j])
        for j in range(tiles)
    ]
    small = [
        pltpu.make_async_copy(there, here, small_sems.at[k])
        for k, (there, here) in enumerate(
            ((zoom_in, zoom), (frac_in, frac), (offset_in, offset), (owner_in, owner))
        )
    ]
    for copy in small + fetched:
        copy.start()
    for g in range(devices):
        named[g] = 0
    for slot in range(devices * capacity):
        rows[slot] = 0
    for copy in small:
        copy.wait()
    halves = []
    for j in range(tiles):
        tile = first_tile + j
        row_points = points_of(spots_along((frame, LANES), 0), zoom, frac, offset, 0, tile, ratio)
        row_weights = jnp.concatenate(
            [
                hat_weight(row_points - spots_along((frame, LANES), 1, p)).astype(jnp.bfloat16)
                for p in range(0, source, LANES)
            ],
            axis=1,
        )
        fetched[j].wait()
        half, quarter = source // 2, frame // 4
        upper = jnp.dot(
            row_weights[: 3 * quarter, :half],
            patches[j, :half],
            preferred_element_type=jnp.float32,
        )
        lower = jnp.dot(
            row_weights[quarter:, half:],
            patches[j, half:],
            preferred_element_type=jnp.float32,
        )
        halfway = jnp.concatenate(
            [upper[:quarter], upper[quarter:] + lower[: 2 * quarter], lower[2 * quarter :]]
        ).astype(jnp.bfloat16)
        for band in range(bands):
            target = owner[band, 0, tile]
            slot = named[target]
            named[target] = slot + 1
            rows[target * capacity + slot] = j * bands + band
        halves.append(halfway)
    for j in range(tiles):
        tile = first_tile + j
        col_points = points_of(spots_along((ROWS, frame), 1), zoom, frac, offset, 1, tile, ratio)
        over = moved(col_points[:, frame - LANES :], LANES - SPARE, 0)
        lane = lax.broadcasted_iota(jnp.int32, over.shape, 1)
        folded = (lane < SPARE) & (cover_of(over, source) > 0.0)
        col_points = jnp.concatenate(
            [jnp.where(folded, over, col_points[:, :LANES]), col_points[:, LANES:]], axis=1
        )
        col_points = jnp.broadcast_to(col_points[:1], (source, frame))
        col_weights = hat_weight(col_points - spots_along((source, frame), 0)).astype(jnp.bfloat16)
        halfway = halves[j]
        rendered = jnp.dot(
            halfway, col_weights, preferred_element_type=jnp.float32
        ).astype(jnp.bfloat16)
        frames[j * bands : (j + 1) * bands] = rendered.reshape(bands, BAND, frame)
    for there, group in zip(outgoing, plan):
        for position, distance in enumerate(group):
            target = me ^ distance
            if is_packed(capacity, devices, distance):
                taken = [rows[target * capacity + slot] for slot in range(capacity)]
                pack_block(
                    there,
                    PACKED * position,
                    lambda k: frames[taken[k], :, :LANES],
                    lambda k: frames[taken[k], :, LANES:],
                )
                continue
            for slot in range(capacity):
                there[position * capacity + slot] = frames[rows[target * capacity + slot]]


MOMENT_ROWS = ((0, 0, {0: 0, 1: 1}), (0, 1, {2: 0}), (1, 0, {0: 2}), (1, 1, {1: 1}), (1, 2, {2: 0}))
PAYLOAD_ROWS = 4


def scan_kernel(sizes, owner, codes):
    tiles, bands, frame, source, capacity, devices = sizes
    me = lax.axis_index("tile")

    def scan(block, distance):
        count = 0
        for j in range(tiles):
            tile = (me ^ distance) * tiles + j
            named = [owner[band, 0, tile] for band in range(bands)]
            for band in range(bands):
                codes[block * capacity + count] = tile * bands + band
                count += (named[band] == me).astype(jnp.int32)

        def blank(position, carry):
            codes[block * capacity + position] = -1
            return carry

        lax.fori_loop(count, capacity, blank, 0)

    arriving = exchange_plan(devices)[1]
    if devices == 8:
        for block, (_, distance) in enumerate(arriving):
            scan(block, distance)
    else:
        pl.loop(0, devices)(lambda block: scan(block, block))


def slot_kernel(
    sizes, zoom, frac, offset, codes, cover_sum, col_cover, slot_lines, slot_bands
):
    tiles, bands, frame, source, capacity, devices = sizes
    slots = devices * capacity
    all_tiles = tiles * devices
    ratio = frame / source

    @pl.loop(0, all_tiles // ROWS)
    def _(group):
        for k in range(ROWS):
            tile = group * ROWS + k
            points = points_of(spots_along((1, frame), 1), zoom, frac, offset, 1, tile, ratio)
            col_cover[pl.ds(tile, 1), :] = cover_of(points, source)

    col_cover[all_tiles:] = jnp.zeros((ROWS, frame), jnp.float32)
    cover_sum[...] = jnp.zeros_like(cover_sum)
    unroll = math.gcd(slots, ROWS)

    @pl.loop(0, slots // unroll)
    def _(group):
        for k in range(unroll):
            slot = group * unroll + k
            used = codes[slot] >= 0
            code = jnp.maximum(codes[slot], 0)
            tile, band = code // bands, code % bands
            before = jnp.maximum(codes[jnp.maximum(slot - 1, 0)], 0) // bands
            place = jnp.where(used, band, bands)
            slot_bands[0, slot] = place
            slot_bands[1, slot] = jnp.where(used, tile, all_tiles)
            slot_bands[2, slot] = (used & (before == tile)).astype(jnp.int32)
            here = pl.ds(slot, 1)
            row = jnp.zeros((1, LANES), jnp.float32)
            start = row + (band * BAND).astype(jnp.float32)
            shift = row + (offset[0, tile].astype(jnp.float32) + frac[0, tile])
            inverse = 1.0 / (row + zoom[0, tile] * ratio)
            slope = jnp.broadcast_to(inverse, (BAND, LANES))
            first = (start - shift) * inverse
            slot_lines[0, here, :] = inverse
            slot_lines[1, here, :] = first
            slot_lines[2, here, :] = coords(start, frame)
            cover = cover_of(spots_along((BAND, LANES), 0) * slope + first, source)
            columns = col_cover[pl.ds(tile, 1), :]
            for half in range(frame // LANES):
                part = slice(half * LANES, (half + 1) * LANES)
                cover_sum[place, :, part] += cover * columns[:, part]


def payload_lanes(tiles, devices):
    return pl.cdiv(2 * tiles * devices + 6 * tiles, LANES) * LANES


def moment_kernel(sizes, zoom, frac, offset, frames, base, parts):
    tiles, bands, frame, source, capacity, devices = sizes
    me = lax.axis_index("tile")
    all_tiles = tiles * devices
    ratio = frame / source
    x = coords(spots_along((1, frame), 1), frame)
    x_powers = (jnp.ones_like(x), x, x * x)
    for j in range(tiles):
        tile = me * tiles + j
        spots = spots_along((frame, frame), 0)
        y = coords(spots, frame)
        cover = cover_of(points_of(spots, zoom, frac, offset, 0, tile, ratio), source)
        level = frames[j * bands : (j + 1) * bands].reshape(frame, frame).astype(jnp.float32)
        columns = points_of(spots_along((1, frame), 1), zoom, frac, offset, 1, tile, ratio)
        columns = cover_of(columns, source)
        weighted = (cover, cover * y, cover * y * y)
        for power, image in enumerate((None, level, level * level)):
            sums = [
                columns * jnp.sum(rows if image is None else rows * image, axis=0, keepdims=True)
                for rows in weighted
            ]
            for half, a, wanted in MOMENT_ROWS:
                group = tiles * (2 * power + half) + j
                for r, degree in wanted.items():
                    parts[r, group : group + 1, :] = sums[a] * x_powers[degree]
    values = [jnp.sum(parts[r], axis=1, keepdims=True) for r in range(3)]
    count = parts.shape[1]
    place = lax.broadcasted_iota(jnp.int32, (count, LANES), 0) + 2 * all_tiles
    total = []
    for start in range(0, base.shape[1], LANES):
        here = lax.broadcasted_iota(jnp.int32, (count, LANES), 1) + start == place
        rows = [
            jnp.sum(jnp.where(here, value, 0.0), axis=0, keepdims=True) for value in values
        ]
        total.append(jnp.concatenate(rows + [jnp.zeros_like(rows[0])], axis=0))
    base[...] = jnp.concatenate(total, axis=1)


def add_blocks(sizes, chosen, slot_bands, col_cover, blocks, whole, total):
    tiles, bands, frame, source, capacity, devices = sizes
    whole = iter(whole)
    for (block, distance), values in zip(chosen, blocks):
        packed = is_packed(capacity, devices, distance)
        if packed:
            unpacked, levels = next(whole), unpack_block(values)
        for k in range(capacity):
            slot = block * capacity + k
            columns = col_cover[pl.ds(slot_bands[1, slot], 1), :]
            for half in range(frame // LANES):
                part = slice(half * LANES, (half + 1) * LANES)
                level = levels[k][half] if packed else values[k, :, part].astype(jnp.float32)
                if packed or half == 0:
                    level = jnp.where(columns[:, part] > 0.0, level, 0.0)
                total[slot_bands[0, slot], :, part] += level
                if packed:
                    unpacked[k, :, part] = level.astype(jnp.bfloat16)


def first_blend_kernel(sizes, chosen, slot_bands, col_cover, *refs):
    blocks, (total, *whole) = refs[: len(chosen)], refs[len(chosen) :]
    total[...] = jnp.zeros_like(total)
    add_blocks(sizes, chosen, slot_bands, col_cover, blocks, whole, total)


def middle_blend_kernel(sizes, chosen, slot_bands, col_cover, before, *refs):
    blocks, (total, *whole) = refs[: len(chosen)], refs[len(chosen) :]
    total[...] = before[...]
    add_blocks(sizes, chosen, slot_bands, col_cover, blocks, whole, total)


def last_blend_kernel(sizes, chosen, slot_bands, col_cover, cover_sum, before, *refs):
    bands, frame = sizes[1], sizes[2]
    blocks, (left, right, *whole, total) = refs[: len(chosen)], refs[len(chosen) :]
    total[...] = before[...]
    add_blocks(sizes, chosen, slot_bands, col_cover, blocks, whole, total)
    grid = (total[:bands] / (1.0 + cover_sum[:bands])).astype(jnp.bfloat16)
    left[...] = grid[:, :, : frame // 2]
    right[...] = grid[:, :, frame // 2 :]


def weight_kernel(sizes, slot_lines, weights, *sums):
    tiles, bands, frame, source, capacity, devices = sizes
    for ref in sums:
        ref[...] = jnp.zeros_like(ref)
    spots = spots_along((BAND, LANES), 0)
    raised = spots * (2.0 / frame)

    @pl.loop(0, devices * capacity // ROWS)
    def _(group):
        for k in range(ROWS):
            slot = group * ROWS + k
            here = pl.ds(slot, 1)
            cover = cover_of(spots * slot_lines[0, here, :] + slot_lines[1, here, :], source)
            weights[0, slot] = cover
            weights[1, slot] = cover * (raised + slot_lines[2, here, :])


GRADIENT_ROWS = ({0: 0, 1: 1}, {2: 0}, {3: 0, 4: 1}, {5: 0})


def add_gradients(sizes, half, slot_bands, from_next, top_grid, weights, blocks, sums, above):
    tiles, bands, frame, source, capacity, devices = sizes
    part = slice(half * LANES, (half + 1) * LANES)
    at_top = lax.axis_index("sec") == lax.axis_size("sec") - 1

    @pl.when(at_top)
    def _():
        above[:bands] = top_grid[:, :, part].astype(jnp.float32)

    @pl.when(jnp.logical_not(at_top))
    def _():
        above[:bands] = from_next[...].astype(jnp.float32)

    above[bands] = jnp.zeros((BAND, LANES), jnp.float32)

    for block, (array, _) in enumerate(exchange_plan(devices)[1]):
        running = None
        for k in range(capacity):
            slot = block * capacity + k
            cover, lifted = weights[0, slot], weights[1, slot]
            level = blocks[array][k, :, part].astype(jnp.float32)
            error = above[slot_bands[0, slot]] - level
            product = error * level
            terms = [cover * error, lifted * error, cover * product, lifted * product]
            terms = [term[:ROWS] + term[ROWS:] for term in terms]
            if running is not None:
                same = slot_bands[2, slot] == 1
                terms = [
                    term + jnp.where(same, before, 0.0) for term, before in zip(terms, running)
                ]
            running = terms
            rows = pl.ds(pl.multiple_of(slot_bands[1, slot] * ROWS, ROWS), ROWS)
            for kind, term in enumerate(terms):
                sums[kind, rows, :] = term


def left_gradient_kernel(sizes, slot_bands, from_next, top_grid, weights, _, *refs):
    *blocks, sums, above = refs
    add_gradients(sizes, 0, slot_bands, from_next, top_grid, weights, blocks, sums, above)


def gradient_kernel(
    sizes,
    slot_bands,
    from_next,
    top_grid,
    weights,
    _,
    left_sums,
    col_cover,
    base,
    left_grid,
    right_grid,
    *refs,
):
    tiles, bands, frame, source, capacity, devices = sizes
    *blocks, payload, grid_out, sums, above, grid_sems = refs
    halves = range(frame // LANES)
    written = [
        pltpu.make_async_copy(
            grid, grid_out.at[:, :, pl.ds(half * LANES, LANES)], grid_sems.at[half]
        )
        for half, grid in enumerate((left_grid, right_grid))
    ]
    for copy in written:
        copy.start()
    all_tiles = tiles * devices
    add_gradients(sizes, 1, slot_bands, from_next, top_grid, weights, blocks, sums, above)

    values = [jnp.zeros((all_tiles, 1), jnp.float32)] * 6
    for half in halves:
        columns = col_cover[:all_tiles, half * LANES : (half + 1) * LANES]
        x = coords(spots_along((all_tiles, LANES), 1, half * LANES), frame)
        for kind, wanted in enumerate(GRADIENT_ROWS):
            ref = (left_sums, sums)[half]
            value = ref[kind, pl.ds(0, all_tiles, stride=ROWS), :]
            for r in range(1, ROWS):
                value += ref[kind, pl.ds(r, all_tiles, stride=ROWS), :]
            value = value * columns
            for row, power in wanted.items():
                term = value * x if power else value
                values[row] += jnp.sum(term, axis=1, keepdims=True)
    total = []
    tile = lax.broadcasted_iota(jnp.int32, (all_tiles, LANES), 0)
    for start in range(0, base.shape[1], LANES):
        lane = lax.broadcasted_iota(jnp.int32, (all_tiles, LANES), 1) + start
        placed = [
            sum(jnp.where(lane == tile + k * all_tiles, values[3 * k + r], 0.0) for k in range(2))
            for r in range(3)
        ]
        rows = [jnp.sum(value, axis=0, keepdims=True) for value in placed]
        total.append(jnp.concatenate(rows + [jnp.zeros_like(rows[0])], axis=0))
    total = base[...] + jnp.concatenate(total, axis=1)
    payload[...] = jnp.broadcast_to(total[None], payload.shape)
    for copy in written:
        copy.wait()


def solve_kernel(sizes, received, corrections):
    tiles, bands, frame, source, capacity, devices = sizes
    sec, me = lax.axis_index("sec"), lax.axis_index("tile")
    sections = lax.axis_size("sec")
    all_tiles = tiles * devices
    lanes = sections * all_tiles
    lane = lax.broadcasted_iota(jnp.int32, (ROWS, lanes), 1)
    within = lane % all_tiles
    area = frame * frame

    width = max(lanes, received.shape[2])

    def rolled(value, shift):
        return pltpu.roll(value, shift % width, 1)

    def fetched(source):
        value = received[source]
        if value.shape[1] < width:
            value = jnp.pad(value, ((0, 0), (0, width - value.shape[1])))
        return jnp.concatenate([value, rolled(value, width - tiles)], axis=0)

    wide = lax.broadcasted_iota(jnp.int32, (ROWS, width), 1)
    gradients = [jnp.zeros((ROWS, width), jnp.float32)] * 2
    moments = [jnp.zeros((ROWS, width), jnp.float32)] * 3
    for s in range(sections):

        def gather(t, carry):
            own, *moments = carry
            value = fetched(s * devices + t)
            place = s * all_tiles + t * tiles
            here = (wide >= place) & (wide < place + tiles)
            for power in range(3):
                start = 2 * all_tiles + 2 * power * tiles
                moment = rolled(value, place - start + 2 * width)
                moments[power] = jnp.where(here, moment, moments[power])
            return (own + value, *moments)

        carry = (jnp.zeros((ROWS, width), jnp.float32), *moments)
        if devices <= 8:
            for t in range(devices):
                carry = gather(t, carry)
        else:
            carry = lax.fori_loop(0, devices, gather, carry)
        own, *moments = carry
        here = wide // all_tiles == s
        for k in range(2):
            part = rolled(own, (s - k) * all_tiles)
            gradients[k] = jnp.where(here, part, gradients[k])
    gradients = [value[:, :lanes] * (1.0 / area) for value in gradients]
    moments = [value[:, :lanes] * (1.0 / area) for value in moments]

    where = ((0, 1, 2), (1, 4, 5), (2, 5, 6))
    row = lax.broadcasted_iota(jnp.int32, (ROWS, lanes), 0)

    def entry(f, g):
        kind = moments[(f >= 3) + (g >= 3)]
        index = where[f % 3][g % 3]
        return kind[index : index + 1]

    def stacked(rows):
        result = jnp.zeros((ROWS, lanes), jnp.float32)
        for f, value in enumerate(rows):
            result = jnp.where(row == f, value, result)
        return result

    normal = [stacked([entry(f, g) for f in range(6)]) for g in range(6)]
    diagonal = stacked([entry(f, f) for f in range(6)])
    gradients = stacked([gradients[f // 3][f % 3 : f % 3 + 1] for f in range(6)])
    precond = 1.0 / (diagonal + 4.0 * COUPLING)

    def total(values):
        return jnp.sum(jnp.sum(values, axis=1, keepdims=True), axis=0, keepdims=True)

    def operator(vector):
        beside = jnp.where(within < all_tiles - 1, pltpu.roll(vector, lanes - 1, 1), 0.0)
        beside += jnp.where(within > 0, pltpu.roll(vector, 1, 1), 0.0)
        upward = pltpu.roll(vector, lanes - all_tiles, 1)
        beside += jnp.where(lane < lanes - all_tiles, upward, 0.0)
        beside += jnp.where(lane >= all_tiles, pltpu.roll(vector, all_tiles, 1), 0.0)
        image = COUPLING * (4.0 * vector - beside)
        for g in range(6):
            image += normal[g] * vector[g : g + 1]
        return image

    answer = jnp.zeros((ROWS, lanes), jnp.float32)
    residual = gradients
    scaled = precond * residual
    direction = scaled
    current = total(residual * scaled)
    for step in range(ITERS):
        image = operator(direction)
        alpha = current / total(direction * image)
        answer = answer + alpha * direction
        if step + 1 < ITERS:
            residual = residual - alpha * image
            scaled = precond * residual
            following = total(residual * scaled)
            direction = scaled + following / current * direction
            current = following

    first = sec * all_tiles + me * tiles
    chosen = (row + first == lane).astype(jnp.float32)
    place = lax.broadcasted_iota(jnp.int32, (ROWS, LANES), 1)
    own = jnp.zeros((ROWS, LANES), jnp.float32)
    for f in range(6):
        value = jnp.sum(chosen * answer[f : f + 1], axis=1, keepdims=True)
        own = jnp.where(place == f, value, own)
    corrections[...] = own[:tiles, :6]


def shards(patches, zoom, frac, offset, owner, top_grid):
    _, tiles, source, _ = patches.shape
    frame = top_grid.shape[1]
    devices, sections = lax.axis_size("tile"), lax.axis_size("sec")
    bands = frame // BAND
    capacity = max(2, 2 * tiles * bands // devices)
    slots = devices * capacity
    all_tiles = tiles * devices
    width = payload_lanes(tiles, devices)
    sizes = (tiles, bands, frame, source, capacity, devices)
    place = (zoom[0], frac[0], offset[0])
    routes = jnp.transpose(owner, (0, 2, 3, 1))[0]

    rows = tiles * bands
    plan, arriving = exchange_plan(devices)
    blocks = [
        jax.ShapeDtypeStruct(
            (len(group) * PACKED, BAND, LANES)
            if is_packed(capacity, devices, group[0])
            else (len(group) * capacity, BAND, frame),
            jnp.bfloat16,
        )
        for group in plan
    ]
    frames, zoom, frac, offset, routes, *outgoing = pl.pallas_call(
        functools.partial(render_kernel, sizes),
        name="render",
        in_specs=[HBM] * 5,
        out_specs=[VMEM] + [SMEM] * 4 + [VMEM] * len(plan),
        out_shape=[jax.ShapeDtypeStruct((rows, BAND, frame), jnp.bfloat16)]
        + [pltpu.SMEM(x.shape, x.dtype) for x in (*place, routes)]
        + blocks,
        scratch_shapes=[
            pltpu.VMEM((tiles, source, source), jnp.bfloat16),
            pltpu.SMEM((devices,), jnp.int32),
            pltpu.SMEM((slots,), jnp.int32),
            pltpu.SemaphoreType.DMA((4,)),
            pltpu.SemaphoreType.DMA((tiles,)),
        ],
        compiler_params=params(24),
        cost_estimate=cost(800_000_000, 4 << 20),
    )(*(pltpu.with_memory_space_constraint(x, pltpu.HBM) for x in (*place, routes, patches[0])))
    *place, routes = (
        pltpu.with_memory_space_constraint(x, pltpu.SMEM) for x in (zoom, frac, offset, routes)
    )

    base = pl.pallas_call(
        functools.partial(moment_kernel, sizes),
        name="moments",
        in_specs=[SMEM] * 3 + [VMEM],
        out_specs=VMEM,
        out_shape=jax.ShapeDtypeStruct((PAYLOAD_ROWS, width), jnp.float32),
        scratch_shapes=[pltpu.VMEM((3, 6 * tiles, frame), jnp.float32)],
        compiler_params=params(24),
        cost_estimate=cost(20_000_000, 1 << 20),
    )(*place, frames)

    codes = pl.pallas_call(
        functools.partial(scan_kernel, sizes),
        name="scan",
        in_specs=[SMEM],
        out_specs=SMEM,
        out_shape=pltpu.SMEM((slots + 1,), jnp.int32),
        compiler_params=params(24),
        cost_estimate=cost(20_000_000, 1 << 20),
    )(routes)

    cover_sum, col_cover, slot_lines, slot_bands = pl.pallas_call(
        functools.partial(slot_kernel, sizes),
        name="slots",
        in_specs=[SMEM] * 4,
        out_specs=[VMEM] * 3 + [SMEM],
        out_shape=[
            jax.ShapeDtypeStruct((bands + 1, BAND, frame), jnp.float32),
            jax.ShapeDtypeStruct((all_tiles + ROWS, frame), jnp.float32),
            jax.ShapeDtypeStruct((3, slots, LANES), jnp.float32),
            pltpu.SMEM((3, slots), jnp.int32),
        ],
        compiler_params=params(24),
        cost_estimate=cost(20_000_000, 1 << 20),
    )(*place, pltpu.with_memory_space_constraint(codes, pltpu.SMEM))

    def swapped(block, distance):
        return lax.ppermute(block, "tile", [(i, i ^ distance) for i in range(devices)])

    incoming = [outgoing[0]]
    for block, group in zip(outgoing[1:], plan[1:]):
        incoming.append(swapped(block, group[0]))
        if len(group) == 2:
            passed_on = incoming[-1][incoming[-1].shape[0] // 2 :]
    if devices == 8:
        incoming.append(swapped(passed_on, 1))

    slot_bands = pltpu.with_memory_space_constraint(slot_bands, pltpu.SMEM)
    total = jax.ShapeDtypeStruct((bands + 1, BAND, frame), jnp.float32)

    def blend(kernel, name, chosen, results, scratch, *operands):
        distances = [(block, arriving[block][1]) for block in chosen]
        arrays = [arriving[block][0] for block in chosen]
        packed = [
            array
            for array, (_, distance) in zip(arrays, distances)
            if is_packed(capacity, devices, distance)
        ]
        whole = jax.ShapeDtypeStruct((capacity, BAND, frame), jnp.bfloat16)
        found = pl.pallas_call(
            functools.partial(kernel, sizes, distances),
            name=name,
            in_specs=[SMEM] + [VMEM] * (len(operands) + len(chosen)),
            out_specs=[VMEM] * (len(results) + len(packed)),
            out_shape=results + [whole] * len(packed),
            scratch_shapes=scratch,
            compiler_params=params(24),
            cost_estimate=cost(1_000_000, 2 << 20),
        )(slot_bands, *operands, *(incoming[array] for array in arrays))
        for array, block in zip(packed, found[len(results) :]):
            incoming[array] = block
        return found[: len(results)]

    last = [5] if devices == 8 else range(devices - devices // 4, devices)
    middle = [4, 7] if devices == 8 else []
    early = [block for block in range(devices) if block not in [*middle, *last]]
    (before,) = blend(first_blend_kernel, "first_blend", early, [total], [], col_cover)
    if middle:
        (before,) = blend(
            middle_blend_kernel, "middle_blend", middle, [total], [], col_cover, before
        )
    half = jax.ShapeDtypeStruct((bands, BAND, frame // 2), jnp.bfloat16)
    grids = blend(
        last_blend_kernel,
        "last_blend",
        last,
        [half, half],
        [pltpu.VMEM(total.shape, total.dtype)],
        col_cover,
        cover_sum,
        before,
    )

    ring = [(i, (i - 1) % sections) for i in range(sections)]
    from_next = [lax.ppermute(grid, "sec", ring) for grid in grids]

    sums = jax.ShapeDtypeStruct((4, (all_tiles + 1) * ROWS, LANES), jnp.float32)
    weights, *zeros = pl.pallas_call(
        functools.partial(weight_kernel, sizes),
        name="weights",
        in_specs=[VMEM],
        out_specs=[VMEM] * 3,
        out_shape=[jax.ShapeDtypeStruct((2, slots, BAND, LANES), jnp.float32), sums, sums],
        compiler_params=params(24),
        cost_estimate=cost(1_000_000, 1 << 20),
    )(slot_lines)

    top_bands = top_grid.reshape(bands, BAND, frame)
    above = pltpu.VMEM((bands + 1, BAND, LANES), jnp.float32)
    left_sums = pl.pallas_call(
        functools.partial(left_gradient_kernel, sizes),
        name="left_gradient",
        in_specs=[SMEM] + [VMEM] * (4 + len(incoming)),
        out_specs=VMEM,
        out_shape=sums,
        scratch_shapes=[above],
        input_output_aliases={4: 0},
        compiler_params=params(24),
        cost_estimate=cost(8_000_000, 2 << 20),
    )(slot_bands, from_next[0], top_bands, weights, zeros[0], *incoming)

    payload, grid_out, _ = pl.pallas_call(
        functools.partial(gradient_kernel, sizes),
        name="gradient",
        in_specs=[SMEM] + [VMEM] * (9 + len(incoming)),
        out_specs=[VMEM, HBM, VMEM],
        out_shape=[
            jax.ShapeDtypeStruct((sections * devices, PAYLOAD_ROWS, width), jnp.float32),
            jax.ShapeDtypeStruct((bands, BAND, frame), jnp.bfloat16),
            sums,
        ],
        scratch_shapes=[above, pltpu.SemaphoreType.DMA((2,))],
        input_output_aliases={4: 2},
        compiler_params=params(24),
        cost_estimate=cost(8_000_000, 2 << 20),
    )(
        slot_bands,
        from_next[1],
        top_bands,
        weights,
        zeros[1],
        left_sums,
        col_cover,
        base,
        *grids,
        *incoming,
    )

    received = lax.all_to_all(
        payload, ("sec", "tile"), split_axis=0, concat_axis=0, tiled=True
    )

    corrections = pl.pallas_call(
        functools.partial(solve_kernel, sizes),
        name="solve",
        in_specs=[VMEM],
        out_specs=VMEM,
        out_shape=jax.ShapeDtypeStruct((tiles, 6), jnp.float32),
        compiler_params=params(24),
        cost_estimate=cost(100_000, 1 << 18),
    )(received)
    return (
        grid_out.reshape(1, 1, frame, frame),
        jnp.transpose(corrections[None], (2, 0, 1)),
    )


def solution(mesh):
    placed = (
        P("sec", "tile", None, None),
        P("sec", None, None),
        P("sec", None, None),
        P("sec", None, None),
        P("sec", None, None, None),
        P("tile", None, None),
    )
    return jax.shard_map(
        shards,
        mesh=mesh,
        in_specs=placed,
        out_specs=(P("sec", "tile", None, None), P(None, "sec", "tile")),
        check_vma=False,
    )
```

```python
import functools
import math

import jax
import jax.numpy as jnp
from jax import lax
from jax.experimental import pallas as pl
from jax.experimental.pallas import tpu as pltpu
from jax.sharding import PartitionSpec as P

BAND = 16
ITERS = 2
COUPLING = 0.25
LANES = 128
ROWS = 8
SPARE = 24
PACKED = 29
HBM = pl.BlockSpec(memory_space=pltpu.HBM)
SMEM = pl.BlockSpec(memory_space=pltpu.SMEM)
VMEM = pl.BlockSpec(memory_space=pltpu.VMEM)


def params(mebibytes):
    return pltpu.CompilerParams(vmem_limit_bytes=mebibytes * 1024 * 1024)


def cost(flops, size):
    return pl.CostEstimate(flops=flops, bytes_accessed=size, transcendentals=0)


def points_of(spots, zoom, frac, offset, axis, tile, ratio):
    scale = zoom[axis, tile] * ratio
    return (spots - offset[axis, tile].astype(jnp.float32) - frac[axis, tile]) / scale


def cover_of(points, source):
    return jnp.clip(jnp.minimum(points + 1.0, source - points), 0.0, 1.0)


def hat_weight(distance):
    return jnp.maximum(0.0, 1.0 - jnp.abs(distance))


def spots_along(shape, dim, start=0):
    return (lax.broadcasted_iota(jnp.int32, shape, dim) + start).astype(jnp.float32)


def coords(spots, frame):
    return (spots - (frame - 1) / 2.0) / (frame / 2.0)


def exchange_plan(devices):
    if devices == 8:
        outgoing = [[0], [2, 3], [4], [5], [6], [7], [1]]
        return outgoing, [(0, 0), (1, 2), (2, 4), (3, 5), (4, 6), (5, 7), (6, 1), (7, 3)]
    return [[d] for d in range(devices)], [(d, d) for d in range(devices)]


def is_packed(capacity, devices, distance):
    return devices == 8 and capacity == 16 and distance > 0


def spare_pieces():
    kept = LANES - SPARE
    pieces = [(4 * i + c, kept, 13 + i, SPARE * c, SPARE) for i in range(3) for c in range(4)]
    return pieces + [(12, kept + 8 * i, 13 + i, 4 * SPARE, 8) for i in range(3)]


def moved(value, start, goal):
    shift = (goal - start) % LANES
    return pltpu.roll(value, shift, 1) if shift else value


def lane_window(start, count):
    lane = lax.broadcasted_iota(jnp.int32, (BAND, LANES), 1)
    return (lane >= start) & (lane < start + count)


def pack_block(there, start, firsts, seconds):
    for k in range(16):
        there[start + k] = firsts(k)
    values = [seconds(k).astype(jnp.float32) for k in range(16)]
    for slot, lane, donor, goal, count in spare_pieces():
        values[slot] = jnp.where(
            lane_window(lane, count), moved(values[donor], goal, lane), values[slot]
        )
    for k in range(13):
        there[start + 16 + k] = values[k].astype(jnp.bfloat16)


def unpack_block(block):
    firsts = [block[k].astype(jnp.float32) for k in range(16)]
    seconds = [block[16 + k].astype(jnp.float32) for k in range(13)]
    seconds += [jnp.zeros((BAND, LANES), jnp.float32)] * 3
    for slot, lane, donor, start, count in spare_pieces():
        seconds[donor] = jnp.where(
            lane_window(start, count), moved(seconds[slot], lane, start), seconds[donor]
        )
    kept = lane_window(0, LANES - SPARE)
    seconds = [
        jnp.where(kept, second, moved(first, 0, LANES - SPARE))
        for first, second in zip(firsts, seconds)
    ]
    return list(zip(firsts, seconds))


def render_kernel(
    sizes,
    zoom_in,
    frac_in,
    offset_in,
    owner_in,
    patches_in,
    frames,
    zoom,
    frac,
    offset,
    owner,
    *outgoing_and_scratch,
):
    tiles, bands, frame, source, capacity, devices = sizes
    plan, _ = exchange_plan(devices)
    outgoing = outgoing_and_scratch[: len(plan)]
    patches, named, rows, small_sems, patch_sems = outgoing_and_scratch[len(plan) :]
    me = lax.axis_index("tile")
    first_tile = me * tiles
    ratio = frame / source
    fetched = [
        pltpu.make_async_copy(patches_in.at[j], patches.at[j], patch_sems.at[j])
        for j in range(tiles)
    ]
    small = [
        pltpu.make_async_copy(there, here, small_sems.at[k])
        for k, (there, here) in enumerate(
            ((zoom_in, zoom), (frac_in, frac), (offset_in, offset), (owner_in, owner))
        )
    ]
    for copy in small + fetched:
        copy.start()
    for g in range(devices):
        named[g] = 0
    for slot in range(devices * capacity):
        rows[slot] = 0
    for copy in small:
        copy.wait()
    halves = []
    for j in range(tiles):
        tile = first_tile + j
        row_points = points_of(spots_along((frame, LANES), 0), zoom, frac, offset, 0, tile, ratio)
        row_weights = jnp.concatenate(
            [
                hat_weight(row_points - spots_along((frame, LANES), 1, p)).astype(jnp.bfloat16)
                for p in range(0, source, LANES)
            ],
            axis=1,
        )
        fetched[j].wait()
        half, quarter = source // 2, frame // 4
        upper = jnp.dot(
            row_weights[: 3 * quarter, :half],
            patches[j, :half],
            preferred_element_type=jnp.float32,
        )
        lower = jnp.dot(
            row_weights[quarter:, half:],
            patches[j, half:],
            preferred_element_type=jnp.float32,
        )
        halfway = jnp.concatenate(
            [upper[:quarter], upper[quarter:] + lower[: 2 * quarter], lower[2 * quarter :]]
        ).astype(jnp.bfloat16)
        for band in range(bands):
            target = owner[band, 0, tile]
            slot = named[target]
            named[target] = slot + 1
            rows[target * capacity + slot] = j * bands + band
        halves.append(halfway)
    for j in range(tiles):
        tile = first_tile + j
        col_points = points_of(spots_along((ROWS, frame), 1), zoom, frac, offset, 1, tile, ratio)
        over = moved(col_points[:, frame - LANES :], LANES - SPARE, 0)
        lane = lax.broadcasted_iota(jnp.int32, over.shape, 1)
        folded = (lane < SPARE) & (cover_of(over, source) > 0.0)
        col_points = jnp.concatenate(
            [jnp.where(folded, over, col_points[:, :LANES]), col_points[:, LANES:]], axis=1
        )
        col_points = jnp.broadcast_to(col_points[:1], (source, frame))
        col_weights = hat_weight(col_points - spots_along((source, frame), 0)).astype(jnp.bfloat16)
        halfway = halves[j]
        rendered = jnp.dot(
            halfway, col_weights, preferred_element_type=jnp.float32
        ).astype(jnp.bfloat16)
        frames[j * bands : (j + 1) * bands] = rendered.reshape(bands, BAND, frame)
    for there, group in zip(outgoing, plan):
        for position, distance in enumerate(group):
            target = me ^ distance
            if is_packed(capacity, devices, distance):
                taken = [rows[target * capacity + slot] for slot in range(capacity)]
                pack_block(
                    there,
                    PACKED * position,
                    lambda k: frames[taken[k], :, :LANES],
                    lambda k: frames[taken[k], :, LANES:],
                )
                continue
            for slot in range(capacity):
                there[position * capacity + slot] = frames[rows[target * capacity + slot]]


MOMENT_ROWS = ((0, 0, {0: 0, 1: 1}), (0, 1, {2: 0}), (1, 0, {0: 2}), (1, 1, {1: 1}), (1, 2, {2: 0}))
PAYLOAD_ROWS = 4


def scan_kernel(sizes, owner, _, codes):
    tiles, bands, frame, source, capacity, devices = sizes
    me = lax.axis_index("tile")

    def scan(block, distance):
        count = 0
        for j in range(tiles):
            tile = (me ^ distance) * tiles + j
            named = [owner[band, 0, tile] for band in range(bands)]
            for band in range(bands):
                codes[block * capacity + count] = tile * bands + band
                count += (named[band] == me).astype(jnp.int32)

        def blank(position, carry):
            codes[block * capacity + position] = -1
            return carry

        lax.fori_loop(count, capacity, blank, 0)

    arriving = exchange_plan(devices)[1]
    if devices == 8:
        for block, (_, distance) in enumerate(arriving):
            scan(block, distance)
    else:
        pl.loop(0, devices)(lambda block: scan(block, block))


def slot_kernel(
    sizes, zoom, frac, offset, codes, cover_sum, col_cover, slot_lines, slot_bands
):
    tiles, bands, frame, source, capacity, devices = sizes
    slots = devices * capacity
    all_tiles = tiles * devices
    ratio = frame / source

    @pl.loop(0, all_tiles // ROWS)
    def _(group):
        for k in range(ROWS):
            tile = group * ROWS + k
            points = points_of(spots_along((1, frame), 1), zoom, frac, offset, 1, tile, ratio)
            col_cover[pl.ds(tile, 1), :] = cover_of(points, source)

    col_cover[all_tiles:] = jnp.zeros((ROWS, frame), jnp.float32)
    cover_sum[...] = jnp.zeros_like(cover_sum)
    unroll = math.gcd(slots, ROWS)

    @pl.loop(0, slots // unroll)
    def _(group):
        for k in range(unroll):
            slot = group * unroll + k
            used = codes[slot] >= 0
            code = jnp.maximum(codes[slot], 0)
            tile, band = code // bands, code % bands
            before = jnp.maximum(codes[jnp.maximum(slot - 1, 0)], 0) // bands
            place = jnp.where(used, band, bands)
            slot_bands[0, slot] = place
            slot_bands[1, slot] = jnp.where(used, tile, all_tiles)
            slot_bands[2, slot] = (used & (before == tile)).astype(jnp.int32)
            here = pl.ds(slot, 1)
            row = jnp.zeros((1, LANES), jnp.float32)
            start = row + (band * BAND).astype(jnp.float32)
            shift = row + (offset[0, tile].astype(jnp.float32) + frac[0, tile])
            inverse = 1.0 / (row + zoom[0, tile] * ratio)
            slope = jnp.broadcast_to(inverse, (BAND, LANES))
            first = (start - shift) * inverse
            slot_lines[0, here, :] = inverse
            slot_lines[1, here, :] = first
            slot_lines[2, here, :] = coords(start, frame)
            cover = cover_of(spots_along((BAND, LANES), 0) * slope + first, source)
            columns = col_cover[pl.ds(tile, 1), :]
            for half in range(frame // LANES):
                part = slice(half * LANES, (half + 1) * LANES)
                cover_sum[place, :, part] += cover * columns[:, part]


def payload_lanes(tiles, devices):
    return pl.cdiv(2 * tiles * devices + 6 * tiles, LANES) * LANES


def moment_kernel(sizes, zoom, frac, offset, frames, base, parts):
    tiles, bands, frame, source, capacity, devices = sizes
    me = lax.axis_index("tile")
    all_tiles = tiles * devices
    ratio = frame / source
    x = coords(spots_along((1, frame), 1), frame)
    x_powers = (jnp.ones_like(x), x, x * x)
    for j in range(tiles):
        tile = me * tiles + j
        spots = spots_along((frame, frame), 0)
        y = coords(spots, frame)
        cover = cover_of(points_of(spots, zoom, frac, offset, 0, tile, ratio), source)
        level = frames[j * bands : (j + 1) * bands].reshape(frame, frame).astype(jnp.float32)
        columns = points_of(spots_along((1, frame), 1), zoom, frac, offset, 1, tile, ratio)
        columns = cover_of(columns, source)
        weighted = (cover, cover * y, cover * y * y)
        for power, image in enumerate((None, level, level * level)):
            sums = [
                columns * jnp.sum(rows if image is None else rows * image, axis=0, keepdims=True)
                for rows in weighted
            ]
            for half, a, wanted in MOMENT_ROWS:
                group = tiles * (2 * power + half) + j
                for r, degree in wanted.items():
                    parts[r, group : group + 1, :] = sums[a] * x_powers[degree]
    values = [jnp.sum(parts[r], axis=1, keepdims=True) for r in range(3)]
    count = parts.shape[1]
    place = lax.broadcasted_iota(jnp.int32, (count, LANES), 0) + 2 * all_tiles
    total = []
    for start in range(0, base.shape[1], LANES):
        here = lax.broadcasted_iota(jnp.int32, (count, LANES), 1) + start == place
        rows = [
            jnp.sum(jnp.where(here, value, 0.0), axis=0, keepdims=True) for value in values
        ]
        total.append(jnp.concatenate(rows + [jnp.zeros_like(rows[0])], axis=0))
    base[...] = jnp.concatenate(total, axis=1)


def add_blocks(sizes, chosen, slot_bands, col_cover, blocks, whole, total):
    tiles, bands, frame, source, capacity, devices = sizes
    whole = iter(whole)
    for (block, distance), values in zip(chosen, blocks):
        packed = is_packed(capacity, devices, distance)
        if packed:
            unpacked, levels = next(whole), unpack_block(values)
        for k in range(capacity):
            slot = block * capacity + k
            columns = col_cover[pl.ds(slot_bands[1, slot], 1), :]
            for half in range(frame // LANES):
                part = slice(half * LANES, (half + 1) * LANES)
                level = levels[k][half] if packed else values[k, :, part].astype(jnp.float32)
                if packed or half == 0:
                    level = jnp.where(columns[:, part] > 0.0, level, 0.0)
                total[slot_bands[0, slot], :, part] += level
                if packed:
                    unpacked[k, :, part] = level.astype(jnp.bfloat16)


def first_blend_kernel(sizes, chosen, slot_bands, col_cover, *refs):
    blocks, (total, *whole) = refs[: len(chosen)], refs[len(chosen) :]
    total[...] = jnp.zeros_like(total)
    add_blocks(sizes, chosen, slot_bands, col_cover, blocks, whole, total)


def middle_blend_kernel(sizes, chosen, slot_bands, col_cover, before, *refs):
    blocks, (total, *whole) = refs[: len(chosen)], refs[len(chosen) :]
    total[...] = before[...]
    add_blocks(sizes, chosen, slot_bands, col_cover, blocks, whole, total)


def last_blend_kernel(sizes, chosen, slot_bands, col_cover, cover_sum, before, *refs):
    bands, frame = sizes[1], sizes[2]
    blocks, (left, right, *whole, total) = refs[: len(chosen)], refs[len(chosen) :]
    total[...] = before[...]
    add_blocks(sizes, chosen, slot_bands, col_cover, blocks, whole, total)
    grid = (total[:bands] / (1.0 + cover_sum[:bands])).astype(jnp.bfloat16)
    left[...] = grid[:, :, : frame // 2]
    right[...] = grid[:, :, frame // 2 :]


def weight_kernel(sizes, slot_lines, weights, *sums):
    tiles, bands, frame, source, capacity, devices = sizes
    for ref in sums:
        ref[...] = jnp.zeros_like(ref)
    spots = spots_along((BAND, LANES), 0)
    raised = spots * (2.0 / frame)

    @pl.loop(0, devices * capacity // ROWS)
    def _(group):
        for k in range(ROWS):
            slot = group * ROWS + k
            here = pl.ds(slot, 1)
            cover = cover_of(spots * slot_lines[0, here, :] + slot_lines[1, here, :], source)
            weights[0, slot] = cover
            weights[1, slot] = cover * (raised + slot_lines[2, here, :])


GRADIENT_ROWS = ({0: 0, 1: 1}, {2: 0}, {3: 0, 4: 1}, {5: 0})


def add_gradients(sizes, half, slot_bands, from_next, top_grid, weights, blocks, sums, above):
    tiles, bands, frame, source, capacity, devices = sizes
    part = slice(half * LANES, (half + 1) * LANES)
    at_top = lax.axis_index("sec") == lax.axis_size("sec") - 1

    @pl.when(at_top)
    def _():
        above[:bands] = top_grid[:, :, part].astype(jnp.float32)

    @pl.when(jnp.logical_not(at_top))
    def _():
        above[:bands] = from_next[...].astype(jnp.float32)

    above[bands] = jnp.zeros((BAND, LANES), jnp.float32)

    for block, (array, _) in enumerate(exchange_plan(devices)[1]):
        running = None
        for k in range(capacity):
            slot = block * capacity + k
            cover, lifted = weights[0, slot], weights[1, slot]
            level = blocks[array][k, :, part].astype(jnp.float32)
            error = above[slot_bands[0, slot]] - level
            product = error * level
            terms = [cover * error, lifted * error, cover * product, lifted * product]
            terms = [term[:ROWS] + term[ROWS:] for term in terms]
            if running is not None:
                same = slot_bands[2, slot] == 1
                terms = [
                    term + jnp.where(same, before, 0.0) for term, before in zip(terms, running)
                ]
            running = terms
            rows = pl.ds(pl.multiple_of(slot_bands[1, slot] * ROWS, ROWS), ROWS)
            for kind, term in enumerate(terms):
                sums[kind, rows, :] = term


def left_gradient_kernel(sizes, slot_bands, from_next, top_grid, weights, _, *refs):
    *blocks, sums, above = refs
    add_gradients(sizes, 0, slot_bands, from_next, top_grid, weights, blocks, sums, above)


def gradient_kernel(
    sizes,
    slot_bands,
    from_next,
    top_grid,
    weights,
    _,
    left_sums,
    col_cover,
    base,
    left_grid,
    right_grid,
    *refs,
):
    tiles, bands, frame, source, capacity, devices = sizes
    *blocks, payload, grid_out, sums, above, grid_sems = refs
    halves = range(frame // LANES)
    written = [
        pltpu.make_async_copy(
            grid, grid_out.at[:, :, pl.ds(half * LANES, LANES)], grid_sems.at[half]
        )
        for half, grid in enumerate((left_grid, right_grid))
    ]
    for copy in written:
        copy.start()
    all_tiles = tiles * devices
    add_gradients(sizes, 1, slot_bands, from_next, top_grid, weights, blocks, sums, above)

    values = [jnp.zeros((all_tiles, 1), jnp.float32)] * 6
    for half in halves:
        columns = col_cover[:all_tiles, half * LANES : (half + 1) * LANES]
        x = coords(spots_along((all_tiles, LANES), 1, half * LANES), frame)
        for kind, wanted in enumerate(GRADIENT_ROWS):
            ref = (left_sums, sums)[half]
            value = ref[kind, pl.ds(0, all_tiles, stride=ROWS), :]
            for r in range(1, ROWS):
                value += ref[kind, pl.ds(r, all_tiles, stride=ROWS), :]
            value = value * columns
            for row, power in wanted.items():
                term = value * x if power else value
                values[row] += jnp.sum(term, axis=1, keepdims=True)
    total = []
    tile = lax.broadcasted_iota(jnp.int32, (all_tiles, LANES), 0)
    for start in range(0, base.shape[1], LANES):
        lane = lax.broadcasted_iota(jnp.int32, (all_tiles, LANES), 1) + start
        placed = [
            sum(jnp.where(lane == tile + k * all_tiles, values[3 * k + r], 0.0) for k in range(2))
            for r in range(3)
        ]
        rows = [jnp.sum(value, axis=0, keepdims=True) for value in placed]
        total.append(jnp.concatenate(rows + [jnp.zeros_like(rows[0])], axis=0))
    total = base[...] + jnp.concatenate(total, axis=1)
    payload[...] = jnp.broadcast_to(total[None], payload.shape)
    for copy in written:
        copy.wait()


def solve_kernel(sizes, received, corrections):
    tiles, bands, frame, source, capacity, devices = sizes
    sec, me = lax.axis_index("sec"), lax.axis_index("tile")
    sections = lax.axis_size("sec")
    all_tiles = tiles * devices
    lanes = sections * all_tiles
    lane = lax.broadcasted_iota(jnp.int32, (ROWS, lanes), 1)
    within = lane % all_tiles
    area = frame * frame

    width = max(lanes, received.shape[2])

    def rolled(value, shift):
        return pltpu.roll(value, shift % width, 1)

    def fetched(source):
        value = received[source]
        if value.shape[1] < width:
            value = jnp.pad(value, ((0, 0), (0, width - value.shape[1])))
        return jnp.concatenate([value, rolled(value, width - tiles)], axis=0)

    wide = lax.broadcasted_iota(jnp.int32, (ROWS, width), 1)
    gradients = [jnp.zeros((ROWS, width), jnp.float32)] * 2
    moments = [jnp.zeros((ROWS, width), jnp.float32)] * 3
    for s in range(sections):

        def gather(t, carry):
            own, *moments = carry
            value = fetched(s * devices + t)
            place = s * all_tiles + t * tiles
            here = (wide >= place) & (wide < place + tiles)
            for power in range(3):
                start = 2 * all_tiles + 2 * power * tiles
                moment = rolled(value, place - start + 2 * width)
                moments[power] = jnp.where(here, moment, moments[power])
            return (own + value, *moments)

        carry = (jnp.zeros((ROWS, width), jnp.float32), *moments)
        if devices <= 8:
            for t in range(devices):
                carry = gather(t, carry)
        else:
            carry = lax.fori_loop(0, devices, gather, carry)
        own, *moments = carry
        here = wide // all_tiles == s
        for k in range(2):
            part = rolled(own, (s - k) * all_tiles)
            gradients[k] = jnp.where(here, part, gradients[k])
    gradients = [value[:, :lanes] * (1.0 / area) for value in gradients]
    moments = [value[:, :lanes] * (1.0 / area) for value in moments]

    where = ((0, 1, 2), (1, 4, 5), (2, 5, 6))
    row = lax.broadcasted_iota(jnp.int32, (ROWS, lanes), 0)

    def entry(f, g):
        kind = moments[(f >= 3) + (g >= 3)]
        index = where[f % 3][g % 3]
        return kind[index : index + 1]

    def stacked(rows):
        result = jnp.zeros((ROWS, lanes), jnp.float32)
        for f, value in enumerate(rows):
            result = jnp.where(row == f, value, result)
        return result

    normal = [stacked([entry(f, g) for f in range(6)]) for g in range(6)]
    diagonal = stacked([entry(f, f) for f in range(6)])
    gradients = stacked([gradients[f // 3][f % 3 : f % 3 + 1] for f in range(6)])
    precond = 1.0 / (diagonal + 4.0 * COUPLING)

    def total(values):
        return jnp.sum(jnp.sum(values, axis=1, keepdims=True), axis=0, keepdims=True)

    def operator(vector):
        beside = jnp.where(within < all_tiles - 1, pltpu.roll(vector, lanes - 1, 1), 0.0)
        beside += jnp.where(within > 0, pltpu.roll(vector, 1, 1), 0.0)
        upward = pltpu.roll(vector, lanes - all_tiles, 1)
        beside += jnp.where(lane < lanes - all_tiles, upward, 0.0)
        beside += jnp.where(lane >= all_tiles, pltpu.roll(vector, all_tiles, 1), 0.0)
        image = COUPLING * (4.0 * vector - beside)
        for g in range(6):
            image += normal[g] * vector[g : g + 1]
        return image

    answer = jnp.zeros((ROWS, lanes), jnp.float32)
    residual = gradients
    scaled = precond * residual
    direction = scaled
    current = total(residual * scaled)
    for step in range(ITERS):
        image = operator(direction)
        alpha = current / total(direction * image)
        answer = answer + alpha * direction
        if step + 1 < ITERS:
            residual = residual - alpha * image
            scaled = precond * residual
            following = total(residual * scaled)
            direction = scaled + following / current * direction
            current = following

    first = sec * all_tiles + me * tiles
    chosen = (row + first == lane).astype(jnp.float32)
    place = lax.broadcasted_iota(jnp.int32, (ROWS, LANES), 1)
    own = jnp.zeros((ROWS, LANES), jnp.float32)
    for f in range(6):
        value = jnp.sum(chosen * answer[f : f + 1], axis=1, keepdims=True)
        own = jnp.where(place == f, value, own)
    corrections[...] = own[:tiles, :6]


def shards(patches, zoom, frac, offset, owner, top_grid):
    _, tiles, source, _ = patches.shape
    frame = top_grid.shape[1]
    devices, sections = lax.axis_size("tile"), lax.axis_size("sec")
    bands = frame // BAND
    capacity = max(2, 2 * tiles * bands // devices)
    slots = devices * capacity
    all_tiles = tiles * devices
    width = payload_lanes(tiles, devices)
    sizes = (tiles, bands, frame, source, capacity, devices)
    place = (zoom[0], frac[0], offset[0])
    routes = jnp.transpose(owner, (0, 2, 3, 1))[0]

    rows = tiles * bands
    plan, arriving = exchange_plan(devices)
    blocks = [
        jax.ShapeDtypeStruct(
            (len(group) * PACKED, BAND, LANES)
            if is_packed(capacity, devices, group[0])
            else (len(group) * capacity, BAND, frame),
            jnp.bfloat16,
        )
        for group in plan
    ]
    frames, zoom, frac, offset, routes, *outgoing = pl.pallas_call(
        functools.partial(render_kernel, sizes),
        name="render",
        in_specs=[HBM] * 5,
        out_specs=[VMEM] + [SMEM] * 4 + [VMEM] * len(plan),
        out_shape=[jax.ShapeDtypeStruct((rows, BAND, frame), jnp.bfloat16)]
        + [pltpu.SMEM(x.shape, x.dtype) for x in (*place, routes)]
        + blocks,
        scratch_shapes=[
            pltpu.VMEM((tiles, source, source), jnp.bfloat16),
            pltpu.SMEM((devices,), jnp.int32),
            pltpu.SMEM((slots,), jnp.int32),
            pltpu.SemaphoreType.DMA((4,)),
            pltpu.SemaphoreType.DMA((tiles,)),
        ],
        compiler_params=params(24),
        cost_estimate=cost(800_000_000, 4 << 20),
    )(*(pltpu.with_memory_space_constraint(x, pltpu.HBM) for x in (*place, routes, patches[0])))
    *place, routes = (
        pltpu.with_memory_space_constraint(x, pltpu.SMEM) for x in (zoom, frac, offset, routes)
    )

    base = pl.pallas_call(
        functools.partial(moment_kernel, sizes),
        name="moments",
        in_specs=[SMEM] * 3 + [VMEM],
        out_specs=VMEM,
        out_shape=jax.ShapeDtypeStruct((PAYLOAD_ROWS, width), jnp.float32),
        scratch_shapes=[pltpu.VMEM((3, 6 * tiles, frame), jnp.float32)],
        compiler_params=params(24),
        cost_estimate=cost(20_000_000, 1 << 20),
    )(*place, frames)

    codes = pl.pallas_call(
        functools.partial(scan_kernel, sizes),
        name="scan",
        in_specs=[SMEM, VMEM],
        out_specs=SMEM,
        out_shape=pltpu.SMEM((slots + 1,), jnp.int32),
        compiler_params=params(24),
        cost_estimate=cost(20_000_000, 1 << 20),
    )(routes, base)

    cover_sum, col_cover, slot_lines, slot_bands = pl.pallas_call(
        functools.partial(slot_kernel, sizes),
        name="slots",
        in_specs=[SMEM] * 4,
        out_specs=[VMEM] * 3 + [SMEM],
        out_shape=[
            jax.ShapeDtypeStruct((bands + 1, BAND, frame), jnp.float32),
            jax.ShapeDtypeStruct((all_tiles + ROWS, frame), jnp.float32),
            jax.ShapeDtypeStruct((3, slots, LANES), jnp.float32),
            pltpu.SMEM((3, slots), jnp.int32),
        ],
        compiler_params=params(24),
        cost_estimate=cost(20_000_000, 1 << 20),
    )(*place, pltpu.with_memory_space_constraint(codes, pltpu.SMEM))

    def swapped(block, distance):
        return lax.ppermute(block, "tile", [(i, i ^ distance) for i in range(devices)])

    incoming = [outgoing[0]]
    for block, group in zip(outgoing[1:], plan[1:]):
        incoming.append(swapped(block, group[0]))
        if len(group) == 2:
            passed_on = incoming[-1][incoming[-1].shape[0] // 2 :]
    if devices == 8:
        incoming.append(swapped(passed_on, 1))

    slot_bands = pltpu.with_memory_space_constraint(slot_bands, pltpu.SMEM)
    total = jax.ShapeDtypeStruct((bands + 1, BAND, frame), jnp.float32)

    def blend(kernel, name, chosen, results, scratch, *operands):
        distances = [(block, arriving[block][1]) for block in chosen]
        arrays = [arriving[block][0] for block in chosen]
        packed = [
            array
            for array, (_, distance) in zip(arrays, distances)
            if is_packed(capacity, devices, distance)
        ]
        whole = jax.ShapeDtypeStruct((capacity, BAND, frame), jnp.bfloat16)
        found = pl.pallas_call(
            functools.partial(kernel, sizes, distances),
            name=name,
            in_specs=[SMEM] + [VMEM] * (len(operands) + len(chosen)),
            out_specs=[VMEM] * (len(results) + len(packed)),
            out_shape=results + [whole] * len(packed),
            scratch_shapes=scratch,
            compiler_params=params(24),
            cost_estimate=cost(1_000_000, 2 << 20),
        )(slot_bands, *operands, *(incoming[array] for array in arrays))
        for array, block in zip(packed, found[len(results) :]):
            incoming[array] = block
        return found[: len(results)]

    last = [5] if devices == 8 else range(devices - devices // 4, devices)
    middle = [4, 7] if devices == 8 else []
    early = [block for block in range(devices) if block not in [*middle, *last]]
    (before,) = blend(first_blend_kernel, "first_blend", early, [total], [], col_cover)
    if middle:
        (before,) = blend(
            middle_blend_kernel, "middle_blend", middle, [total], [], col_cover, before
        )
    half = jax.ShapeDtypeStruct((bands, BAND, frame // 2), jnp.bfloat16)
    grids = blend(
        last_blend_kernel,
        "last_blend",
        last,
        [half, half],
        [pltpu.VMEM(total.shape, total.dtype)],
        col_cover,
        cover_sum,
        before,
    )

    ring = [(i, (i - 1) % sections) for i in range(sections)]
    from_next = [lax.ppermute(grid, "sec", ring) for grid in grids]

    sums = jax.ShapeDtypeStruct((4, (all_tiles + 1) * ROWS, LANES), jnp.float32)
    weights, *zeros = pl.pallas_call(
        functools.partial(weight_kernel, sizes),
        name="weights",
        in_specs=[VMEM],
        out_specs=[VMEM] * 3,
        out_shape=[jax.ShapeDtypeStruct((2, slots, BAND, LANES), jnp.float32), sums, sums],
        compiler_params=params(24),
        cost_estimate=cost(1_000_000, 1 << 20),
    )(slot_lines)

    top_bands = top_grid.reshape(bands, BAND, frame)
    above = pltpu.VMEM((bands + 1, BAND, LANES), jnp.float32)
    left_sums = pl.pallas_call(
        functools.partial(left_gradient_kernel, sizes),
        name="left_gradient",
        in_specs=[SMEM] + [VMEM] * (4 + len(incoming)),
        out_specs=VMEM,
        out_shape=sums,
        scratch_shapes=[above],
        input_output_aliases={4: 0},
        compiler_params=params(24),
        cost_estimate=cost(8_000_000, 2 << 20),
    )(slot_bands, from_next[0], top_bands, weights, zeros[0], *incoming)

    payload, grid_out, _ = pl.pallas_call(
        functools.partial(gradient_kernel, sizes),
        name="gradient",
        in_specs=[SMEM] + [VMEM] * (9 + len(incoming)),
        out_specs=[VMEM, HBM, VMEM],
        out_shape=[
            jax.ShapeDtypeStruct((sections * devices, PAYLOAD_ROWS, width), jnp.float32),
            jax.ShapeDtypeStruct((bands, BAND, frame), jnp.bfloat16),
            sums,
        ],
        scratch_shapes=[above, pltpu.SemaphoreType.DMA((2,))],
        input_output_aliases={4: 2},
        compiler_params=params(24),
        cost_estimate=cost(8_000_000, 2 << 20),
    )(
        slot_bands,
        from_next[1],
        top_bands,
        weights,
        zeros[1],
        left_sums,
        col_cover,
        base,
        *grids,
        *incoming,
    )

    received = lax.all_to_all(
        payload, ("sec", "tile"), split_axis=0, concat_axis=0, tiled=True
    )

    corrections = pl.pallas_call(
        functools.partial(solve_kernel, sizes),
        name="solve",
        in_specs=[VMEM],
        out_specs=VMEM,
        out_shape=jax.ShapeDtypeStruct((tiles, 6), jnp.float32),
        compiler_params=params(24),
        cost_estimate=cost(100_000, 1 << 18),
    )(received)
    return (
        grid_out.reshape(1, 1, frame, frame),
        jnp.transpose(corrections[None], (2, 0, 1)),
    )


def solution(mesh):
    placed = (
        P("sec", "tile", None, None),
        P("sec", None, None),
        P("sec", None, None),
        P("sec", None, None),
        P("sec", None, None, None),
        P("tile", None, None),
    )
    return jax.shard_map(
        shards,
        mesh=mesh,
        in_specs=placed,
        out_specs=(P("sec", "tile", None, None), P(None, "sec", "tile")),
        check_vma=False,
    )
```
